32 devices in a mesh: dp: 16 (over z, y, x), rep: 2 (over core).
Axes of the slice: x: 2, y: 2, z: 4, core: 2. Of those that a mesh axis runs over, the one named last changes fastest.
Arguments:
- tokens_in: bfloat16 [8192, 576], P(('dp', 'rep')), may hold values from -12 to 12
- positions: int32 [8192], P(('dp', 'rep')), may hold values from 0 to 127, as said below
- params: bfloat16 [3540096], P('dp'), may hold values from -0.5 to 1.5, as said below
- cotangent: bfloat16 [8192, 576], P(('dp', 'rep')), may hold values from -6 to 6
Outputs:
- output: bfloat16 [8192, 576], P(('dp', 'rep'))
- grad_input: float32 [8192, 576], P(('dp', 'rep'))
- grad_params: float32 [3540096], P('dp')
- grad_gain_mid: float32 [576], replicated
The draws below stay inside these ranges and needn't reach their ends.
Inputs may be any that keep to these rules, and one draw needn't show every extreme that they name: `positions`: positions count up by one from 0 and restart at 0 where a document begins, several times in most sequences; in sequence 0 they run 0 to 127. `params`: the norm gains lie in 0.5 to 1.5.
All inputs are finite; a program needn't handle non-finite values.
Results may differ from the reference program's by a relative error of at most 0.012.
Values may be sent and summed in bfloat16 or wider, within the bound.
No kernel may reach another device: no remote copies, remote signals or barrier semaphores. Data moves between devices by JAX's collectives and lax.ppermute only.
A program may use at most 128 MiB of HBM per device.

```python
import math
import jax
import jax.numpy as jnp
from jax import lax

D = 576
HEADS = 9
KV_HEADS = 3
HEAD = 64
FF = 1536
SEQ_LEN = 128
PARAMS = 3540096
TOKENS = 8192


def draw_tokens_in(key, part):
    key = jax.random.fold_in(key, 11)
    row_key, value_key = jax.random.split(key, 2)
    scale = jnp.exp(jax.random.uniform(row_key, (TOKENS, 1), minval=math.log(0.3), maxval=math.log(3.0)))
    base = jax.random.normal(value_key, (TOKENS, D))
    return jnp.clip(base * scale, -12.0, 12.0).astype(jnp.bfloat16)


def draw_positions(key, part):
    key = jax.random.fold_in(key, 23)
    seqs = TOKENS // SEQ_LEN
    ticks = jax.random.randint(key, (seqs, SEQ_LEN), 0, max(4, SEQ_LEN // 4))
    order = jnp.arange(SEQ_LEN, dtype=jnp.int32)[None, :]
    breaks = (ticks == 0) | (order == 0)
    breaks = breaks & ((jnp.arange(seqs, dtype=jnp.int32)[:, None] > 0) | (order == 0))
    starts = lax.cummax(jnp.where(breaks, order, 0), axis=1)
    return (order - starts).reshape(-1).astype(jnp.int32)


def draw_params(key, part):
    key = jax.random.fold_in(key, 37)
    gain_key, weight_key = jax.random.split(key)
    kv_width = KV_HEADS * HEAD
    spans = [(D * D, D), (D * kv_width, D), (D * kv_width, D), (D * D, max(1, D // 16)), (D * FF, D), (D * FF, D), (FF * D, max(1, FF // 4))]
    scales = jnp.concatenate([jnp.full((count,), fan ** (-0.5), jnp.float32) for count, fan in spans])
    weights = jnp.clip(jax.random.normal(weight_key, (PARAMS - 2 * D,)) * scales, -0.5, 0.5)
    gains = jax.random.uniform(gain_key, (2 * D,), minval=0.5, maxval=1.5)
    return jnp.concatenate([gains, weights]).astype(jnp.bfloat16)


def level_of(stream_key, shape, cuts, smallest, top_value):
    loudness, own = 1.0, jax.random.fold_in(stream_key, 6)
    for position, blocks in cuts:
        steps = jnp.exp(jax.random.uniform(jax.random.fold_in(own, position), (blocks,), jnp.float32, smallest / len(cuts), top_value / len(cuts)))
        loudness = loudness * jnp.repeat(steps, shape[position] // blocks).reshape([-1 if axis == position else 1 for axis in range(len(shape))])
    return loudness


def noise(stream_key, extent, width, reach, cuts=(), kind=jnp.bfloat16):
    array = jax.random.normal(stream_key, extent, jnp.float32) * width
    if len(cuts) > 0:
        array = level_of(stream_key, extent, cuts, -0.22, 0.18) * array
    return jnp.clip(array, min=-reach, max=reach).astype(kind)


def setup_inputs(seed: int = 0) -> dict:
    seeds = jax.random.split(jax.random.key(seed), 5)
    tokens_in = draw_tokens_in(jax.random.fold_in(seeds[4], 71), 0)
    positions = draw_positions(jax.random.fold_in(seeds[4], 71), 0)
    params = draw_params(jax.random.fold_in(seeds[4], 71), 0)
    cotangent = noise(seeds[3], (TOKENS, D), 1.0, 6.0, ((0, 32),))
    return {"tokens_in": tokens_in, "positions": positions, "params": params, "cotangent": cotangent}


EPS = 1e-05
ROPE_BASE = 100000.0

@jax.custom_vjp
def low(v):
    return lax.optimization_barrier(v.astype(jnp.bfloat16)).astype(jnp.float32)

@jax.custom_vjp
def low_back(v):
    return v

def low_keep(v):
    return (low(v), None)

def low_pass(kept, grad):
    return (grad,)

def back_keep(v):
    return (v, None)

def back_low(kept, grad):
    return (low(grad),)
low.defvjp(low_keep, low_pass)
low_back.defvjp(back_keep, back_low)

def matmul_high(left, right):
    return jnp.matmul(left, right, precision=lax.Precision.HIGHEST)

def split_params(flat):
    kv_width = KV_HEADS * HEAD
    shapes = [(D,), (D,), (D, D), (D, kv_width), (D, kv_width), (D, D), (D, FF), (D, FF), (FF, D)]
    pieces = []
    offset = 0
    for shape in shapes:
        count = math.prod(shape)
        pieces.append(flat[offset:offset + count].reshape(shape))
        offset = offset + count
    return pieces

def rope_tables(places):
    expon = jnp.arange(HEAD // 2).astype(jnp.float32) * (2.0 / HEAD)
    inverse = jnp.power(ROPE_BASE, -expon)
    angle = places.astype(jnp.float32)[..., None] * inverse
    return (jnp.cos(angle), jnp.sin(angle))

def rotate(vector, cosine, sine):
    half = vector.shape[-1] // 2
    first, second = (vector[..., :half], vector[..., half:])
    cosine = cosine[..., None, :]
    sine = sine[..., None, :]
    return jnp.concatenate([first * cosine - second * sine, second * cosine + first * sine], -1)

def rms_norm(stream):
    return stream * lax.rsqrt(lax.optimization_barrier(jnp.mean(stream * stream, -1, keepdims=True)) + EPS)

def layer(stream, cosine, sine, pieces):
    gain_in, gain_mid, w_query, w_key, w_value, w_out, w_gate, w_up, w_down = pieces
    batch, length = (stream.shape[0], stream.shape[1])
    repeat = HEADS // KV_HEADS
    norm_in = low(rms_norm(stream) * gain_in)
    query = low_back(matmul_high(norm_in, w_query)).reshape(batch, length, HEADS, HEAD)
    query = low(rotate(query, cosine, sine)).reshape(batch, length, KV_HEADS, repeat, HEAD)
    keys = low_back(matmul_high(norm_in, w_key)).reshape(batch, length, KV_HEADS, HEAD)
    keys = low(rotate(keys, cosine, sine))
    values = low(low_back(matmul_high(norm_in, w_value))).reshape(batch, length, KV_HEADS, HEAD)
    raw = jnp.einsum('bqgrd,bkgd->bgrqk', query, keys, precision=lax.Precision.HIGHEST)
    raw = low_back(raw * HEAD ** (-0.5))
    causal = jnp.arange(length)[:, None] >= jnp.arange(length)[None, :]
    masked = jnp.where(causal, raw, -1e+30)
    top = lax.optimization_barrier(jnp.max(masked, -1, keepdims=True))
    expon = jnp.exp(masked - top)
    probs = expon / lax.optimization_barrier(jnp.sum(expon, -1, keepdims=True))
    attended = jnp.einsum('bgrqk,bkgd->bqgrd', low(probs), values, precision=lax.Precision.HIGHEST)
    attended = low(low_back(attended.reshape(batch, length, D)))
    mixed = stream + low_back(matmul_high(attended, w_out))
    norm_mid = low(rms_norm(mixed) * gain_mid)
    gate = low_back(matmul_high(norm_mid, w_gate))
    upper = low_back(matmul_high(norm_mid, w_up))
    hidden = low(gate * jax.nn.sigmoid(gate) * upper)
    return mixed + low_back(matmul_high(hidden, w_down))

def reference(tokens_in, positions, params, cotangent):
    length = SEQ_LEN
    seqs = tokens_in.shape[0] // length
    per_block = math.gcd(seqs, max(1, 4096 // length))
    blocks = seqs // per_block
    cosine, sine = rope_tables(positions.reshape(blocks, per_block, length))

    def forward(stream, flat):
        pieces = split_params(flat)

        def run(item):
            return layer(item[0], item[1], item[2], pieces)
        shaped = stream.reshape(blocks, per_block, length, D)
        result = lax.map(jax.checkpoint(run), (shaped, cosine, sine))
        return result.reshape(-1, D)
    output, pullback = jax.vjp(forward, tokens_in.astype(jnp.float32), params.astype(jnp.float32))
    grad_input, grad_params = pullback(cotangent.astype(jnp.float32))
    return (output.astype(jnp.bfloat16), grad_input, grad_params, grad_params[D:2 * D])
```

```python
import jax
import jax.numpy as jnp
from jax import lax
from jax.sharding import PartitionSpec as P

HEADS = 9
KV_HEADS = 3
HEAD = 64
FF = 1536
SEQ_LEN = 128
PLANES = 4
CANON = 16

EPS = 1e-05
ROPE_BASE = 100000.0


class Layout:
    def __init__(self, count, total, width):
        self.count = count
        self.width = width
        self.gains = 2 * width
        self.shard = total // count
        self.chunk = (total - self.gains) // count
        self.step = self.gains // count
        self.rows = self.chunk // 128
        half = -(-(self.rows + 10) // 2)
        self.half = -(-half // 16) * 16
        self.first = -(-(self.half // 2) // 16) * 16
        self.extra = 2 * self.half - self.rows
        self.bits = count.bit_length() - 1
        rest = self.bits - 2
        self.x_bits = -(-rest // 2)
        self.y_bits = rest - self.x_bits
        self.in_plane = 1 << rest


def pack_wide(flat, width):
    panels = width // 128
    return flat.reshape(-1, panels, 128).transpose(1, 0, 2).reshape(-1, 128)


def unpack_wide(rows, width):
    panels = width // 128
    return rows.reshape(panels, -1, 128).transpose(1, 0, 2).reshape(-1)


def pack_narrow(flat):
    rows = flat.reshape(-1, 576)
    count = rows.shape[0]
    panels = rows[:, :512].reshape(count, 4, 128).transpose(1, 0, 2).reshape(-1, 128)
    tail = rows[:, 512:]
    return jnp.concatenate([panels, jnp.concatenate([tail[: count // 2], tail[count // 2 :]], 1)], 0)


def unpack_narrow(packed):
    count = packed.shape[0] * 2 // 9
    panels = packed[: 4 * count].reshape(4, count, 128).transpose(1, 0, 2).reshape(count, 512)
    half = packed[4 * count :]
    tail = jnp.concatenate([half[:, :64], half[:, 64:]], 0)
    return jnp.concatenate([panels, tail], 1).reshape(-1)


def head_narrow(flat):
    rows = flat.reshape(2, 576)
    tail = jnp.pad(rows[:, 512:], ((0, 0), (64, 0)))
    return jnp.concatenate([rows[:, :512].reshape(8, 128), tail], 0)


def unhead_narrow(rows):
    return jnp.concatenate([rows[:8].reshape(2, 512), rows[8:10, 64:]], 1).reshape(-1)


def head_wide(flat):
    return jnp.pad(flat.reshape(9, 128), ((0, 1), (0, 0)))


def unhead_wide(rows):
    return rows[:9].reshape(-1)


def is_wide(index, count):
    return (index >= count // 4) & (index < 3 * count // 4)


def pack_payload(window, index, lay):
    head, chunk = window[: lay.gains], window[lay.gains :]
    body = jnp.where(is_wide(index, lay.count), pack_wide(chunk, FF), pack_narrow(chunk))
    top = jnp.where(is_wide(index - 1, lay.count), head_wide(head), head_narrow(head))
    return jnp.concatenate([body, jnp.pad(top, ((0, lay.extra - 10), (0, 0)))], 0)


def unpack_payload(rows, index, lay):
    body, top = rows[: lay.rows], rows[lay.rows : lay.rows + 10]
    chunk = jnp.where(is_wide(index, lay.count), unpack_wide(body, FF), unpack_narrow(body))
    head = jnp.where(is_wide(index - 1, lay.count), unhead_wide(top), unhead_narrow(top))
    return jnp.concatenate([head, chunk])


def swap(value, mask, count):
    return lax.ppermute(value, "dp", [(i, i ^ mask) for i in range(count)])


def swap_rep(value):
    return lax.ppermute(value, "rep", [(0, 1), (1, 0)])


def gather_axis(value, shift, size, count):
    return jnp.stack([value] + [swap(value, d << shift, count) for d in range(1, size)], 0)


def gather(half, lay):
    n = lay.count
    x_size, y_size = 1 << lay.x_bits, 1 << lay.y_bits
    planes = [half] + [swap(half, s << (lay.bits - 2), n) for s in range(1, PLANES)]
    own, twin = [], []
    for plane in planes:
        first, second = plane[: lay.first], plane[lay.first :]
        first = gather_axis(gather_axis(first, 0, x_size, n), lay.x_bits, y_size, n)
        second = gather_axis(gather_axis(second, lay.x_bits, y_size, n), 0, x_size, n)
        second = second.transpose(1, 0, 2, 3)
        whole = jnp.concatenate([first, second], 2).reshape(lay.in_plane, lay.half, 128)
        own.append(whole)
        twin.append(swap_rep(whole))
    return own, twin


def add_axis(value, shift, size, count):
    total = value[0].astype(jnp.float32)
    for d in range(1, size):
        total = total + swap(value[d], d << shift, count).astype(jnp.float32)
    return total.astype(value.dtype)


def reduce_plane(value, lay):
    n = lay.count
    x_size, y_size = 1 << lay.x_bits, 1 << lay.y_bits
    grid = value.reshape(y_size, x_size, lay.half, 128)
    first, second = grid[:, :, : lay.first], grid[:, :, lay.first :]
    first = add_axis(add_axis(first, lay.x_bits, y_size, n), 0, x_size, n)
    second = add_axis(add_axis(second.transpose(1, 0, 2, 3), 0, x_size, n), lay.x_bits, y_size, n)
    return jnp.concatenate([first, second], 0)


def sum_everywhere(value, lay):
    value = value + swap_rep(value)
    for bit in range(lay.bits):
        value = value + swap(value, 1 << bit, lay.count)
    return value


def rope_tables(places):
    expon = jnp.arange(HEAD // 2).astype(jnp.float32) * (2.0 / HEAD)
    inverse = jnp.power(ROPE_BASE, -expon)
    angle = places.astype(jnp.float32)[..., None] * inverse
    return (jnp.cos(angle), jnp.sin(angle))


def rotate(vector, cosine, sine):
    half = vector.shape[-1] // 2
    first, second = (vector[..., :half], vector[..., half:])
    cosine = cosine[..., None, :]
    sine = sine[..., None, :]
    return jnp.concatenate([first * cosine - second * sine, second * cosine + first * sine], -1)


def layer(tokens, cosine, sine, cotangent, pieces):
    gain_in, gain_mid, w_query, w_key, w_value, w_out, w_gate, w_up, w_down = pieces
    f32, bf16 = jnp.float32, jnp.bfloat16
    stream = tokens.astype(f32)
    length = stream.shape[0]
    batch = length // SEQ_LEN
    repeat = HEADS // KV_HEADS
    scale = HEAD ** (-0.5)

    def mm(spec, left, right):
        return jnp.einsum(spec, left, right, preferred_element_type=f32)

    inverse_in = lax.rsqrt(jnp.mean(stream * stream, -1, keepdims=True) + EPS)
    normed_in = stream * inverse_in
    norm_in = (normed_in * gain_in).astype(bf16)
    query = rotate(mm("td,de->te", norm_in, w_query).reshape(length, HEADS, HEAD), cosine, sine)
    query = query.astype(bf16).reshape(batch, SEQ_LEN, KV_HEADS, repeat, HEAD)
    keys = rotate(mm("td,de->te", norm_in, w_key).reshape(length, KV_HEADS, HEAD), cosine, sine)
    keys = keys.astype(bf16).reshape(batch, SEQ_LEN, KV_HEADS, HEAD)
    values = mm("td,de->te", norm_in, w_value).astype(bf16).reshape(batch, SEQ_LEN, KV_HEADS, HEAD)
    raw = mm("bqgrd,bkgd->bgrqk", query, keys) * scale
    causal = jnp.arange(SEQ_LEN)[:, None] >= jnp.arange(SEQ_LEN)[None, :]
    raw = jnp.where(causal, raw, -1e30)
    expon = jnp.exp(raw - jnp.max(raw, -1, keepdims=True))
    full = expon / jnp.sum(expon, -1, keepdims=True)
    probs = full.astype(bf16)
    attended = mm("bgrqk,bkgd->bqgrd", probs, values).reshape(length, -1).astype(bf16)
    mixed = stream + mm("td,de->te", attended, w_out)
    inverse_mid = lax.rsqrt(jnp.mean(mixed * mixed, -1, keepdims=True) + EPS)
    normed_mid = mixed * inverse_mid
    norm_mid = (normed_mid * gain_mid).astype(bf16)
    gate = mm("td,df->tf", norm_mid, w_gate)
    upper = mm("td,df->tf", norm_mid, w_up)
    sigma = jax.nn.sigmoid(gate)
    hidden = (gate * sigma * upper).astype(bf16)
    output = (mixed + mm("tf,fd->td", hidden, w_down)).astype(bf16)

    grad_out = cotangent.astype(f32)
    d_down = mm("tf,td->fd", hidden, cotangent)
    d_hidden = mm("td,fd->tf", cotangent, w_down)
    d_gate = (d_hidden * upper * sigma * (1.0 + gate * (1.0 - sigma))).astype(bf16)
    d_up = (d_hidden * gate * sigma).astype(bf16)
    dw_gate = mm("td,tf->df", norm_mid, d_gate)
    dw_up = mm("td,tf->df", norm_mid, d_up)
    d_norm = mm("tf,df->td", d_gate, w_gate) + mm("tf,df->td", d_up, w_up)
    d_gain_mid = jnp.sum(d_norm * normed_mid, 0)
    scaled = d_norm * gain_mid
    d_mixed = grad_out + inverse_mid * (
        scaled - normed_mid * jnp.mean(scaled * normed_mid, -1, keepdims=True)
    )
    branch = d_mixed.astype(bf16)
    dw_out = mm("td,te->de", attended, branch)
    d_att = mm("te,de->td", branch, w_out).astype(bf16)
    d_att = d_att.reshape(batch, SEQ_LEN, KV_HEADS, repeat, HEAD)
    d_probs = mm("bqgrd,bkgd->bgrqk", d_att, values)
    d_value = mm("bgrqk,bqgrd->bkgd", probs, d_att).reshape(length, -1).astype(bf16)
    inner = jnp.sum(d_probs * full, -1, keepdims=True)
    d_raw = (full * (d_probs - inner)).astype(bf16)
    d_query = mm("bgrqk,bkgd->bqgrd", d_raw, keys).reshape(length, HEADS, HEAD) * scale
    d_query = rotate(d_query, cosine, -sine).reshape(length, -1).astype(bf16)
    d_keys = mm("bgrqk,bqgrd->bkgd", d_raw, query).reshape(length, KV_HEADS, HEAD) * scale
    d_keys = rotate(d_keys, cosine, -sine).reshape(length, -1).astype(bf16)
    dw_query = mm("td,te->de", norm_in, d_query)
    dw_key = mm("td,te->de", norm_in, d_keys)
    dw_value = mm("td,te->de", norm_in, d_value)
    d_norm = (
        mm("te,de->td", d_query, w_query)
        + mm("te,de->td", d_keys, w_key)
        + mm("te,de->td", d_value, w_value)
    )
    d_gain_in = jnp.sum(d_norm * normed_in, 0)
    scaled = d_norm * gain_in
    d_input = d_mixed + inverse_in * (
        scaled - normed_in * jnp.mean(scaled * normed_in, -1, keepdims=True)
    )
    grads = (d_gain_in, d_gain_mid, dw_query, dw_key, dw_value, dw_out, dw_gate, dw_up, d_down)
    return output, d_input, grads


def weights_of(payloads, lay):
    n, width = lay.count, lay.width
    kv_width = KV_HEADS * HEAD
    heads = payloads[:, lay.rows : lay.rows + 10]
    gains = unhead_narrow(heads[0]).reshape(2, width).astype(jnp.float32)
    flats = []
    for i in range(n):
        wide = n // 4 <= i < 3 * n // 4
        body = payloads[i, : lay.rows]
        flat = unpack_wide(body, FF) if wide else unpack_narrow(body)
        if i + 1 < n:
            tail = unhead_wide(heads[i + 1]) if wide else unhead_narrow(heads[i + 1])
            flat = jnp.concatenate([flat[: -lay.gains], flat[-lay.gains :] + tail])
        flats.append(flat)
    flat = jnp.concatenate(flats)
    shapes = [(width, width), (width, kv_width), (width, kv_width), (width, width)]
    shapes += [(width, FF), (width, FF), (FF, width)]
    pieces, offset = [gains[0], gains[1]], 0
    for rows, columns in shapes:
        pieces.append(flat[offset : offset + rows * columns].reshape(rows, columns))
        offset = offset + rows * columns
    return pieces


def payloads_of(grads, lay):
    flat = jnp.concatenate([piece.astype(jnp.bfloat16).reshape(-1) for piece in grads])
    windows = [
        flat[i * lay.chunk : (i + 1) * lay.chunk + lay.gains] for i in range(lay.count)
    ]
    return jnp.stack([pack_payload(window, i, lay) for i, window in enumerate(windows)], 0)


def on_device(lay, tokens_in, positions, params, cotangent):
    index = lax.axis_index("dp")
    core = lax.axis_index("rep")
    n, half, in_plane = lay.count, lay.half, lay.in_plane
    window = jnp.zeros((lay.gains + lay.chunk,), params.dtype)
    window = lax.dynamic_update_slice(window, params, (index * lay.step,))
    payload = pack_payload(window, index, lay)
    mine = lax.dynamic_slice_in_dim(payload, core * half, half, 0)
    own, twin = gather(mine, lay)

    plane, place = index // in_plane, index % in_plane
    own, twin = jnp.stack(own, 0), jnp.stack(twin, 0)
    both = jnp.where(core == 0, jnp.stack([own, twin], 2), jnp.stack([twin, own], 2))
    both = both.reshape(n, 2 * half, 128)
    order = jnp.arange(n, dtype=jnp.int32) ^ index
    payloads = jnp.take(both, order, axis=0)

    cosine, sine = rope_tables(positions)
    output, d_input, grads = layer(tokens_in, cosine, sine, cotangent, weights_of(payloads, lay))

    rows = payloads_of(grads, lay).reshape(PLANES, in_plane, 2, half, 128)
    rows = jnp.take(rows, jnp.arange(in_plane, dtype=jnp.int32) ^ place, axis=1)
    keep = jnp.take(rows, core, axis=2)
    send = jnp.take(rows, 1 - core, axis=2)
    planes = []
    for p in range(PLANES):
        pair = keep[p].astype(jnp.float32) + swap_rep(send[p]).astype(jnp.float32)
        planes.append(reduce_plane(pair.astype(jnp.bfloat16), lay))
    planes = jnp.stack(planes, 0)
    total = jnp.take(planes, plane, axis=0).astype(jnp.float32)
    for s in range(1, PLANES):
        part = swap(jnp.take(planes, plane ^ s, axis=0), s << (lay.bits - 2), n)
        total = total + part.astype(jnp.float32)
    other = swap_rep(total)
    whole = jnp.where(core == 0, jnp.stack([total, other], 0), jnp.stack([other, total], 0))
    window = unpack_payload(whole.reshape(2 * half, 128), index, lay)
    grad_params = lax.dynamic_slice(window, (index * lay.step,), (lay.shard,))
    return output, d_input, grad_params, sum_everywhere(grads[1], lay)


def solution(mesh):
    def run(tokens_in, positions, params, cotangent):
        lay = Layout(mesh.shape["dp"], params.shape[0], tokens_in.shape[1])
        rows = P(("dp", "rep"), None)
        return jax.shard_map(
            lambda *args: on_device(lay, *args),
            mesh=mesh,
            in_specs=(rows, P(("dp", "rep")), P("dp"), rows),
            out_specs=(rows, rows, P("dp"), P()),
            check_vma=False,
        )(tokens_in, positions, params, cotangent)

    return run
```

```python
import jax
import jax.numpy as jnp
from jax import lax
from jax.experimental import pallas as pl
from jax.experimental.pallas import tpu as pltpu
from jax.sharding import PartitionSpec as P

HEADS = 9
KV_HEADS = 3
HEAD = 64
FF = 1536
SEQ_LEN = 128
PLANES = 4
CANON = 16

EPS = 1e-05
ROPE_BASE = 100000.0

F32, BF16 = jnp.float32, jnp.bfloat16
ROWS, HALF = 1728, 880
NARROW, WIDE = 384, 144
VMEM_LIMIT = 52 * 1024 * 1024


class Layout:
    def __init__(self, count, total, width):
        self.count = count
        self.width = width
        self.gains = 2 * width
        self.shard = total // count
        self.chunk = (total - self.gains) // count
        self.step = self.gains // count
        self.rows = self.chunk // 128
        half = -(-(self.rows + 10) // 2)
        self.half = -(-half // 16) * 16
        self.first = -(-(self.half // 2) // 16) * 16
        self.extra = 2 * self.half - self.rows
        self.bits = count.bit_length() - 1
        rest = self.bits - 2
        self.x_bits = -(-rest // 2)
        self.y_bits = rest - self.x_bits
        self.in_plane = 1 << rest


def pack_wide(flat, width):
    panels = width // 128
    return flat.reshape(-1, panels, 128).transpose(1, 0, 2).reshape(-1, 128)


def unpack_wide(rows, width):
    panels = width // 128
    return rows.reshape(panels, -1, 128).transpose(1, 0, 2).reshape(-1)


def pack_narrow(flat):
    rows = flat.reshape(-1, 576)
    count = rows.shape[0]
    panels = rows[:, :512].reshape(count, 4, 128).transpose(1, 0, 2).reshape(-1, 128)
    tail = rows[:, 512:]
    return jnp.concatenate([panels, jnp.concatenate([tail[: count // 2], tail[count // 2 :]], 1)], 0)


def unpack_narrow(packed):
    count = packed.shape[0] * 2 // 9
    panels = packed[: 4 * count].reshape(4, count, 128).transpose(1, 0, 2).reshape(count, 512)
    half = packed[4 * count :]
    tail = jnp.concatenate([half[:, :64], half[:, 64:]], 0)
    return jnp.concatenate([panels, tail], 1).reshape(-1)


def head_narrow(flat):
    rows = flat.reshape(2, 576)
    tail = jnp.pad(rows[:, 512:], ((0, 0), (64, 0)))
    return jnp.concatenate([rows[:, :512].reshape(8, 128), tail], 0)


def unhead_narrow(rows):
    return jnp.concatenate([rows[:8].reshape(2, 512), rows[8:10, 64:]], 1).reshape(-1)


def head_wide(flat):
    return jnp.pad(flat.reshape(9, 128), ((0, 1), (0, 0)))


def unhead_wide(rows):
    return rows[:9].reshape(-1)


def is_wide(index, count):
    return (index >= count // 4) & (index < 3 * count // 4)


def pack_payload(window, index, lay):
    head, chunk = window[: lay.gains], window[lay.gains :]
    body = jnp.where(is_wide(index, lay.count), pack_wide(chunk, FF), pack_narrow(chunk))
    top = jnp.where(is_wide(index - 1, lay.count), head_wide(head), head_narrow(head))
    return jnp.concatenate([body, jnp.pad(top, ((0, lay.extra - 10), (0, 0)))], 0)


def unpack_payload(rows, index, lay):
    body, top = rows[: lay.rows], rows[lay.rows : lay.rows + 10]
    chunk = jnp.where(is_wide(index, lay.count), unpack_wide(body, FF), unpack_narrow(body))
    head = jnp.where(is_wide(index - 1, lay.count), unhead_wide(top), unhead_narrow(top))
    return jnp.concatenate([head, chunk])


def swap(value, mask, count):
    return lax.ppermute(value, "dp", [(i, i ^ mask) for i in range(count)])


def swap_rep(value):
    return lax.ppermute(value, "rep", [(0, 1), (1, 0)])


def gather_axis(value, shift, size, count):
    return jnp.stack([value] + [swap(value, d << shift, count) for d in range(1, size)], 0)


def gather(half, lay):
    n = lay.count
    x_size, y_size = 1 << lay.x_bits, 1 << lay.y_bits
    planes = [half] + [swap(half, s << (lay.bits - 2), n) for s in range(1, PLANES)]
    own, twin = [], []
    for plane in planes:
        first, second = plane[: lay.first], plane[lay.first :]
        first = gather_axis(gather_axis(first, 0, x_size, n), lay.x_bits, y_size, n)
        second = gather_axis(gather_axis(second, lay.x_bits, y_size, n), 0, x_size, n)
        second = second.transpose(1, 0, 2, 3)
        whole = jnp.concatenate([first, second], 2).reshape(lay.in_plane, lay.half, 128)
        own.append(whole)
        twin.append(swap_rep(whole))
    return own, twin


def add_axis(value, shift, size, count):
    total = value[0].astype(jnp.float32)
    for d in range(1, size):
        total = total + swap(value[d], d << shift, count).astype(jnp.float32)
    return total.astype(value.dtype)


def reduce_plane(value, lay):
    n = lay.count
    x_size, y_size = 1 << lay.x_bits, 1 << lay.y_bits
    grid = value.reshape(y_size, x_size, lay.half, 128)
    first, second = grid[:, :, : lay.first], grid[:, :, lay.first :]
    first = add_axis(add_axis(first, lay.x_bits, y_size, n), 0, x_size, n)
    second = add_axis(add_axis(second.transpose(1, 0, 2, 3), 0, x_size, n), lay.x_bits, y_size, n)
    return jnp.concatenate([first, second], 0)


def sum_everywhere(value, lay):
    value = value + swap_rep(value)
    for bit in range(lay.bits):
        value = value + swap(value, 1 << bit, lay.count)
    return value


def rope_tables(places):
    expon = jnp.arange(HEAD // 2).astype(jnp.float32) * (2.0 / HEAD)
    inverse = jnp.power(ROPE_BASE, -expon)
    angle = places.astype(jnp.float32)[..., None] * inverse
    return (jnp.cos(angle), jnp.sin(angle))


def dot(left, right):
    return jnp.dot(left, right, preferred_element_type=F32)


def dot_nt(left, right):
    return lax.dot_general(left, right, (((1,), (1,)), ((), ())), preferred_element_type=F32)


def dot_tn(left, right):
    return dot(left.astype(F32).T.astype(BF16), right)


def row_of_head(head, which):
    parts = [head[4 * which + j : 4 * which + j + 1] for j in range(4)]
    return jnp.concatenate(parts + [head[8 + which : 9 + which, 64:]], 1)


def head_of_rows(rows):
    parts = [row[:, 128 * j : 128 * j + 128] for row in rows for j in range(4)]
    zeros = jnp.zeros((1, 64), F32)
    parts = parts + [jnp.concatenate([zeros, row[:, 512:]], 1) for row in rows]
    return jnp.concatenate(parts + [jnp.zeros((6, 128), F32)], 0)


def load_narrow(ref, index):
    parts = [ref[index, NARROW * j : NARROW * (j + 1), :] for j in range(4)]
    half = ref[index, 4 * NARROW : ROWS, :]
    tail = jnp.concatenate([half[:, :64], half[:, 64:]], 0)
    return jnp.concatenate(parts + [tail], 1)


def store_narrow(ref, index, value):
    for j in range(4):
        ref[index, NARROW * j : NARROW * (j + 1), :] = value[:, 128 * j : 128 * (j + 1)].astype(BF16)
    tail = value[:, 512:]
    tail = jnp.concatenate([tail[: NARROW // 2], tail[NARROW // 2 :]], 1)
    ref[index, 4 * NARROW : ROWS, :] = tail.astype(BF16)


def narrow_tiles():
    tiles = [(NARROW * (j + 1) - 16, j, 4 + j) for j in range(4)]
    return tiles + [(ROWS - 16, 8, 9)]


def add_tail(ref, index, wide):
    head = ref[index + 1, ROWS : ROWS + 16, :].astype(F32)
    row = lax.broadcasted_iota(jnp.int32, (16, 128), 0)
    if wide:
        for k in range(9):
            at = WIDE * (4 + k) - 16
            tile = ref[index, at : at + 16, :].astype(F32)
            tile = tile + jnp.where(row == 15, head[k : k + 1], 0.0)
            ref[index, at : at + 16, :] = tile.astype(BF16)
    else:
        for at, upper, lower in narrow_tiles():
            tile = ref[index, at : at + 16, :].astype(F32)
            tile = tile + jnp.where(row == 14, head[upper : upper + 1], 0.0)
            tile = tile + jnp.where(row == 15, head[lower : lower + 1], 0.0)
            ref[index, at : at + 16, :] = tile.astype(BF16)


def tail_of(ref, index, wide):
    if wide:
        parts = []
        for k in range(9):
            at = WIDE * (4 + k) - 16
            parts.append(ref[index, at : at + 16, :].astype(F32)[15:16])
        return jnp.concatenate(parts + [jnp.zeros((7, 128), F32)], 0)
    tiles = [ref[index, at : at + 16, :].astype(F32) for at, _, _ in narrow_tiles()]
    parts = [tile[14:15] for tile in tiles[:4]] + [tile[15:16] for tile in tiles[:4]]
    parts = parts + [tiles[4][14:15], tiles[4][15:16]]
    return jnp.concatenate(parts + [jnp.zeros((6, 128), F32)], 0)


def spread(value, first, second, out):
    for m in range(3):
        part = value[:, 192 * m : 192 * (m + 1)].astype(F32)
        first[pl.ds(m, 192, stride=3), :] = part[:, :128]
        second[pl.ds(m, 192, stride=3), :] = jnp.concatenate([part[:, 128:], part[:, 128:]], 1)
    out[:, :128] = first[...].astype(BF16)
    out[:, 128:] = second[:, :64].astype(BF16)


def unspread(value, first, second):
    first[...] = value[:, :128]
    second[...] = jnp.concatenate([value[:, 128:], value[:, 128:]], 1)
    parts = []
    for m in range(3):
        parts.append(first[pl.ds(m, 192, stride=3), :])
        parts.append(second[pl.ds(m, 192, stride=3), :][:, :64])
    return jnp.concatenate(parts, 1)


def turn(vector, cosine, sine):
    swapped = jnp.concatenate([vector[:, 32:], vector[:, :32]], 1)
    return vector * cosine + swapped * sine


def piece_copies(idx, refs, dst, plane_base, sems, outward):
    plane, place, core = idx[0], idx[1], idx[2]
    copies = []
    for s, (own, twin) in enumerate(refs):
        for d in range(4):
            chunk = jnp.bitwise_xor(place, d)
            if plane_base is None:
                chunk = chunk + 4 * jnp.bitwise_xor(plane, s)
            else:
                chunk = chunk + plane_base + 4 * s
            for which, ref in enumerate((own, twin)):
                at = jnp.bitwise_xor(core, which) * HALF
                inner = dst.at[chunk, pl.ds(pl.multiple_of(at, 16), HALF), :]
                outer = ref.at[d]
                pair = (inner, outer) if outward else (outer, inner)
                copies.append(pltpu.make_async_copy(pair[0], pair[1], sems.at[len(copies)]))
    return copies


def first_kernel(
    idx, own0, own1, own2, own3, twin0, twin1, twin2, twin3, tok, cot, cos, sin,
    y_out, dr_out, att_out, p_out, q_out, k_out, v_out, wq, wk, wv, wo, gain_out, dg_out,
    keep1, keep2, keep3, send1, send2, send3,
    w, g, att, n2_ref, n2t_ref, y_acc, dn_acc, first, second, sems, out_sems,
):
    loads = piece_copies(
        idx, [(own0, twin0), (own1, twin1), (own2, twin2), (own3, twin3)], w, None, sems, False
    )
    for copy in loads:
        copy.start()
    tokens = tok.shape[0]
    x = tok[...].astype(F32)
    normed = x * lax.rsqrt(jnp.mean(x * x, -1, keepdims=True) + EPS)
    for copy in loads:
        copy.wait()
    for c in (0, 1, 2, 3, 12, 13, 14):
        add_tail(w, c, False)

    def fix(i, carry):
        add_tail(w, i + 4, True)
        return carry

    lax.fori_loop(0, 8, fix, 0)
    gains = w[0, ROWS : ROWS + 16, :].astype(F32)
    gain_in, gain_mid = row_of_head(gains, 0), row_of_head(gains, 1)
    gain_out[...] = gain_in
    n1 = (normed * gain_in).astype(BF16)
    wq[:NARROW, :] = load_narrow(w, 0)
    mixed_chunk = load_narrow(w, 1)
    wq[NARROW:, :] = mixed_chunk[:192]
    spread(mixed_chunk[192:], first, second, wk)
    mixed_chunk = load_narrow(w, 2)
    spread(mixed_chunk[:192], first, second, wv)
    wo[:192, :] = mixed_chunk[192:]
    wo[192:, :] = load_narrow(w, 3)

    query, keys, values = dot(n1, wq[...]), dot(n1, wk[...]), dot(n1, wv[...])
    row = lax.broadcasted_iota(jnp.int32, (3 * SEQ_LEN, SEQ_LEN), 0)
    causal = jnp.bitwise_and(row, SEQ_LEN - 1) >= lax.broadcasted_iota(
        jnp.int32, (3 * SEQ_LEN, SEQ_LEN), 1
    )
    for b in range(tokens // SEQ_LEN):
        part = slice(SEQ_LEN * b, SEQ_LEN * (b + 1))
        cosine, sine = cos[part, :], sin[part, :]
        for kv in range(KV_HEADS):
            at = KV_HEADS * b + kv
            heads = [
                turn(query[part, HEAD * h : HEAD * (h + 1)], cosine, sine)
                for h in range(3 * kv, 3 * kv + 3)
            ]
            q3 = jnp.concatenate(heads, 0).astype(BF16)
            k1 = turn(keys[part, HEAD * kv : HEAD * (kv + 1)], cosine, sine).astype(BF16)
            v1 = values[part, HEAD * kv : HEAD * (kv + 1)].astype(BF16)
            q_out[at], k_out[at], v_out[at] = q3, k1, v1
            score = jnp.where(causal, dot_nt(q3, k1) * HEAD**-0.5, -1e30)
            expon = jnp.exp(score - jnp.max(score, -1, keepdims=True))
            probs = expon / jnp.sum(expon, -1, keepdims=True)
            p_out[at] = probs
            mix = dot(probs.astype(BF16), v1)
            for r in range(3):
                h = 3 * kv + r
                att[part, HEAD * h : HEAD * (h + 1)] = mix[SEQ_LEN * r : SEQ_LEN * (r + 1)]
    attended = att[...].astype(BF16)
    att_out[...] = attended
    mixed = x + dot(attended, wo[...])
    inverse = lax.rsqrt(jnp.mean(mixed * mixed, -1, keepdims=True) + EPS)
    normed_mid = mixed * inverse
    n2 = normed_mid * gain_mid
    n2_ref[...] = n2.astype(BF16)
    n2t_ref[...] = n2.astype(BF16).astype(F32).T.astype(BF16)
    y_acc[...] = mixed
    dn_acc[...] = jnp.zeros_like(dn_acc)

    def block(k, carry):
        def wide(base, p):
            at = pl.multiple_of((3 * k + p) * WIDE, 16)
            return jnp.concatenate([w[base + d, pl.ds(at, WIDE), :] for d in range(4)], 0)

        w_gate = jnp.concatenate([wide(4, p) for p in range(3)], 1)
        w_up = jnp.concatenate([wide(8, p) for p in range(3)], 1)
        w_down = load_narrow(w, 12 + k)
        c = cot[...]
        gate, up = dot(n2_ref[...], w_gate), dot(n2_ref[...], w_up)
        sigma = 1.0 / (1.0 + jnp.exp(-gate))
        silu = gate * sigma
        hidden = (silu * up).astype(BF16)
        y_acc[...] += dot(hidden, w_down)
        store_narrow(g, 8 + k, dot_tn(hidden, c))
        d_hidden = dot_nt(c, w_down)
        d_gate = (d_hidden * up * sigma * (1.0 + gate * (1.0 - sigma))).astype(BF16)
        d_up = (d_hidden * silu).astype(BF16)
        dn_acc[...] += dot_nt(d_gate, w_gate) + dot_nt(d_up, w_up)
        for base, d_out in ((0, d_gate), (4, d_up)):
            grad = dot(n2t_ref[...], d_out).astype(BF16)
            for p in range(3):
                at = pl.multiple_of((3 * k + p) * WIDE, 16)
                for d in range(4):
                    g[base + d, pl.ds(at, WIDE), :] = grad[
                        WIDE * d : WIDE * (d + 1), 128 * p : 128 * (p + 1)
                    ]
        return carry

    lax.fori_loop(0, 4, block, 0)
    zeros = jnp.zeros((HALF * 2 - ROWS, 128), BF16)
    g[0, ROWS:, :] = zeros
    for c in range(1, 12):
        g[c, ROWS:, :] = zeros
        g[c, ROWS : ROWS + 16, :] = tail_of(g, c - 1, c - 1 < 8).astype(BF16)
    stores = piece_copies(
        idx, [(keep1, send1), (keep2, send2), (keep3, send3)], g, 0, out_sems, True
    )
    for copy in stores:
        copy.start()
    y_out[...] = y_acc[...].astype(BF16)
    d_norm = dn_acc[...]
    d_gain = jnp.sum(d_norm * normed_mid, 0, keepdims=True)
    dg_out[...] = d_gain
    scaled = d_norm * gain_mid
    dr_out[...] = cot[...].astype(F32) + inverse * (
        scaled - normed_mid * jnp.mean(scaled * normed_mid, -1, keepdims=True)
    )
    for copy in stores:
        copy.wait()


def second_kernel(
    idx, tok, cos, sin, dr, att, p_in, q_in, k_in, v_in, wq, wk, wv, wo, gain, dg,
    dx_out, keep, send,
    g, dq_ref, dk_ref, dv_ref, first, second, out_sems,
):
    tokens = tok.shape[0]
    d_mixed = dr[...]
    branch = d_mixed.astype(BF16)
    dw_out = dot_tn(att[...], branch)
    d_att = dot_nt(branch, wo[...])
    for b in range(tokens // SEQ_LEN):
        part = slice(SEQ_LEN * b, SEQ_LEN * (b + 1))
        cosine, sine = cos[part, :], -sin[part, :]
        for kv in range(KV_HEADS):
            at = KV_HEADS * b + kv
            heads = [d_att[part, HEAD * h : HEAD * (h + 1)] for h in range(3 * kv, 3 * kv + 3)]
            d3 = jnp.concatenate(heads, 0).astype(BF16)
            probs, q3, k1, v1 = p_in[at], q_in[at], k_in[at], v_in[at]
            d_probs = dot_nt(d3, v1)
            dv_ref[part, HEAD * kv : HEAD * (kv + 1)] = dot_tn(probs.astype(BF16), d3)
            inner = jnp.sum(d_probs * probs, -1, keepdims=True)
            d_score = (probs * (d_probs - inner)).astype(BF16)
            dq3 = dot(d_score, k1) * HEAD**-0.5
            for r in range(3):
                h = 3 * kv + r
                dq_ref[part, HEAD * h : HEAD * (h + 1)] = turn(
                    dq3[SEQ_LEN * r : SEQ_LEN * (r + 1)], cosine, sine
                )
            dk_ref[part, HEAD * kv : HEAD * (kv + 1)] = turn(
                dot_tn(d_score, q3) * HEAD**-0.5, cosine, sine
            )
    dq, dk, dv = dq_ref[...].astype(BF16), dk_ref[...].astype(BF16), dv_ref[...].astype(BF16)
    x = tok[...].astype(F32)
    inverse = lax.rsqrt(jnp.mean(x * x, -1, keepdims=True) + EPS)
    normed = x * inverse
    n1t = (normed * gain[...]).astype(BF16).astype(F32).T.astype(BF16)
    dw_query = dot(n1t, dq)
    store_narrow(g, 0, dw_query[:NARROW])
    dw = unspread(dot(n1t, dk), first, second)
    store_narrow(g, 1, jnp.concatenate([dw_query[NARROW:], dw], 0))
    dw = unspread(dot(n1t, dv), first, second)
    store_narrow(g, 2, jnp.concatenate([dw, dw_out[:192]], 0))
    store_narrow(g, 3, dw_out[192:])
    d_norm = dot_nt(dq, wq[...]) + dot_nt(dk, wk[...]) + dot_nt(dv, wv[...])
    d_gain = jnp.sum(d_norm * normed, 0, keepdims=True)
    for c in range(4):
        g[c, ROWS:, :] = jnp.zeros((HALF * 2 - ROWS, 128), BF16)
        if c:
            g[c, ROWS : ROWS + 16, :] = tail_of(g, c - 1, False).astype(BF16)
    g[0, ROWS : ROWS + 16, :] = head_of_rows([d_gain, dg[...]]).astype(BF16)
    g[0, ROWS + 16 : ROWS + 32, :] = tail_of(g, 3, False).astype(BF16)
    stores = piece_copies(idx, [(keep, send)], g, 0, out_sems, True)
    for copy in stores:
        copy.start()
    scaled = d_norm * gain[...]
    dx_out[...] = d_mixed + inverse * (
        scaled - normed * jnp.mean(scaled * normed, -1, keepdims=True)
    )
    for copy in stores:
        copy.wait()


def run_layer(idx, own, twin, tokens, cotangent, positions):
    length, width = tokens.shape
    groups = length // SEQ_LEN * KV_HEADS
    cosine, sine = rope_tables(positions)
    cosine = jnp.concatenate([cosine, cosine], 1)
    sine = jnp.concatenate([-sine, sine], 1)
    kv_width = KV_HEADS * HEAD
    smem = pl.BlockSpec(memory_space=pltpu.SMEM)
    vmem = pl.BlockSpec(memory_space=pltpu.VMEM)
    anywhere = pl.BlockSpec(memory_space=pl.ANY)

    def sds(shape, dtype):
        return jax.ShapeDtypeStruct(shape, dtype)

    piece = sds((4, HALF, 128), BF16)
    weights = [sds((width, width), BF16), sds((width, kv_width), BF16)]
    weights = weights + [weights[1], weights[0]]
    saved = [
        sds((groups, 3 * SEQ_LEN, SEQ_LEN), F32),
        sds((groups, 3 * SEQ_LEN, HEAD), BF16),
        sds((groups, SEQ_LEN, HEAD), BF16),
        sds((groups, SEQ_LEN, HEAD), BF16),
    ]
    outs = [sds((length, width), BF16), sds((length, width), F32), sds((length, width), BF16)]
    outs = outs + saved + weights + [sds((1, width), F32)] * 2
    results = pl.pallas_call(
        first_kernel,
        name="forward_and_ff_backward",
        in_specs=[smem] + [anywhere] * 8 + [vmem] * 4,
        out_specs=[vmem] * len(outs) + [anywhere] * 6,
        out_shape=outs + [piece] * 6,
        scratch_shapes=[
            pltpu.VMEM((CANON, 2 * HALF, 128), BF16),
            pltpu.VMEM((12, 2 * HALF, 128), BF16),
            pltpu.VMEM((length, width), F32),
            pltpu.VMEM((length, width), BF16),
            pltpu.VMEM((width, length), BF16),
            pltpu.VMEM((length, width), F32),
            pltpu.VMEM((length, width), F32),
            pltpu.VMEM((width, 128), F32),
            pltpu.VMEM((width, 128), F32),
            pltpu.SemaphoreType.DMA((32,)),
            pltpu.SemaphoreType.DMA((24,)),
        ],
        compiler_params=pltpu.CompilerParams(vmem_limit_bytes=VMEM_LIMIT),
        cost_estimate=pl.CostEstimate(
            flops=20 * length * width * FF, bytes_accessed=16_000_000, transcendentals=600_000
        ),
    )(idx, *own, *twin, tokens, cotangent, cosine, sine)
    output, d_mixed, attended, probs, q3, k1, v1, wq, wk, wv, wo, gain, d_gain = results[:13]
    keeps, sends = list(results[13:16]), list(results[16:19])
    d_input, keep, send = pl.pallas_call(
        second_kernel,
        name="attention_backward",
        in_specs=[smem] + [vmem] * 15,
        out_specs=[vmem] + [anywhere] * 2,
        out_shape=[sds((length, width), F32), piece, piece],
        scratch_shapes=[
            pltpu.VMEM((4, 2 * HALF, 128), BF16),
            pltpu.VMEM((length, width), F32),
            pltpu.VMEM((length, kv_width), F32),
            pltpu.VMEM((length, kv_width), F32),
            pltpu.VMEM((width, 128), F32),
            pltpu.VMEM((width, 128), F32),
            pltpu.SemaphoreType.DMA((8,)),
        ],
        compiler_params=pltpu.CompilerParams(vmem_limit_bytes=VMEM_LIMIT),
        cost_estimate=pl.CostEstimate(
            flops=10 * length * width * width, bytes_accessed=10_000_000, transcendentals=0
        ),
    )(idx, tokens, cosine, sine, d_mixed, attended, probs, q3, k1, v1, wq, wk, wv, wo, gain, d_gain)
    return output, d_input, d_gain[0], [keep] + keeps, [send] + sends


def flat_of(payloads, lay):
    n = lay.count
    heads = payloads[:, lay.rows : lay.rows + 10]
    flats = [unhead_narrow(heads[0])]
    for i in range(n):
        wide = n // 4 <= i < 3 * n // 4
        body = payloads[i, : lay.rows]
        flat = unpack_wide(body, FF) if wide else unpack_narrow(body)
        if i + 1 < n:
            tail = unhead_wide(heads[i + 1]) if wide else unhead_narrow(heads[i + 1])
            flat = jnp.concatenate([flat[: -lay.gains], flat[-lay.gains :] + tail])
        flats.append(flat)
    return jnp.concatenate(flats)


def payloads_of(flat, lay):
    windows = [
        flat[i * lay.chunk : (i + 1) * lay.chunk + lay.gains] for i in range(lay.count)
    ]
    return jnp.stack([pack_payload(window, i, lay) for i, window in enumerate(windows)], 0)


def canonical(own, twin, lay, canon, index, core):
    own, twin = jnp.stack(own, 0), jnp.stack(twin, 0)
    both = jnp.where(core == 0, jnp.stack([own, twin], 2), jnp.stack([twin, own], 2))
    both = both.reshape(lay.count, 2 * lay.half, 128)
    both = jnp.take(both, jnp.arange(lay.count, dtype=jnp.int32) ^ index, axis=0)
    flat = flat_of(both, lay)
    zeros = jnp.zeros((canon.gains,), flat.dtype)
    rows = []
    for i in range(CANON):
        window = flat[i * canon.chunk : (i + 1) * canon.chunk + canon.gains]
        if i:
            window = jnp.concatenate([zeros, window[canon.gains :]])
        rows.append(pack_payload(window, i, canon))
    rows = jnp.stack(rows, 0).reshape(PLANES, 4, 2, canon.half, 128)
    return [list(rows[:, :, c]) for c in range(2)]


def from_canonical(keeps, sends, lay, canon, place, core):
    rows = jnp.stack([jnp.stack(keeps, 0), jnp.stack(sends, 0)], 2)
    rows = rows.reshape(CANON, 2 * canon.half, 128)
    flats = [unhead_narrow(rows[0, canon.rows : canon.rows + 10])]
    for i in range(CANON):
        body = rows[i, : canon.rows]
        flats.append(unpack_wide(body, FF) if 4 <= i < 12 else unpack_narrow(body))
    rows = payloads_of(jnp.concatenate(flats), lay)
    rows = rows.reshape(PLANES, lay.in_plane, 2, lay.half, 128)
    rows = jnp.take(rows, jnp.arange(lay.in_plane, dtype=jnp.int32) ^ place, axis=1)
    return list(jnp.take(rows, core, axis=2)), list(jnp.take(rows, 1 - core, axis=2))


def on_device(lay, canon, tokens_in, positions, params, cotangent):
    index = lax.axis_index("dp")
    core = lax.axis_index("rep")
    n, half, in_plane = lay.count, lay.half, lay.in_plane
    plane, place = index // in_plane, index % in_plane
    same = n == CANON
    window = jnp.zeros((lay.gains + lay.chunk,), params.dtype)
    window = lax.dynamic_update_slice(window, params, (index * lay.step,))
    payload = pack_payload(window, index, lay)
    mine = lax.dynamic_slice_in_dim(payload, core * half, half, 0)
    own, twin = gather(mine, lay)

    if same:
        idx = jnp.stack([plane, place, core]).astype(jnp.int32)
    else:
        own, twin = canonical(own, twin, lay, canon, index, core)
        idx = jnp.zeros((3,), jnp.int32)
    output, d_input, d_gain, keeps, sends = run_layer(
        idx, own, twin, tokens_in, cotangent, positions
    )
    if not same:
        keeps, sends = from_canonical(keeps, sends, lay, canon, place, core)
    planes = []
    for keep, send in zip(keeps, sends):
        pair = keep.astype(F32) + swap_rep(send).astype(F32)
        planes.append(reduce_plane(pair.astype(BF16), lay))
    if same:
        at = ROWS - HALF
        late = jnp.where(core == 1, planes[0][at + 16 : at + 32], jnp.zeros((16, 128), BF16))
        planes[1] = jnp.concatenate([planes[1][:at], planes[1][at : at + 16] + late, planes[1][at + 16 :]])
    planes = jnp.stack(planes, 0)
    total = jnp.take(planes, plane, axis=0).astype(F32)
    for s in range(1, PLANES):
        part = swap(jnp.take(planes, plane ^ s, axis=0), s << (lay.bits - 2), n)
        total = total + part.astype(F32)
    other = swap_rep(total)
    whole = jnp.where(core == 0, jnp.stack([total, other], 0), jnp.stack([other, total], 0))
    window = unpack_payload(whole.reshape(2 * half, 128), index, lay)
    grad_params = lax.dynamic_slice(window, (index * lay.step,), (lay.shard,))
    return output, d_input, grad_params, sum_everywhere(d_gain, lay)


def solution(mesh):
    def run(tokens_in, positions, params, cotangent):
        total, width = params.shape[0], tokens_in.shape[1]
        lay = Layout(mesh.shape["dp"], total, width)
        canon = Layout(CANON, total, width)
        rows = P(("dp", "rep"), None)
        return jax.shard_map(
            lambda *args: on_device(lay, canon, *args),
            mesh=mesh,
            in_specs=(rows, P(("dp", "rep")), P("dp"), rows),
            out_specs=(rows, rows, P("dp"), P()),
            check_vma=False,
        )(tokens_in, positions, params, cotangent)

    return run
```

```python
import jax
import jax.numpy as jnp
from jax import lax
from jax.experimental import pallas as pl
from jax.experimental.pallas import tpu as pltpu
from jax.sharding import PartitionSpec as P

HEADS = 9
KV_HEADS = 3
HEAD = 64
FF = 1536
SEQ_LEN = 128
PLANES = 4
CANON = 16

EPS = 1e-05
ROPE_BASE = 100000.0

F32, BF16 = jnp.float32, jnp.bfloat16
ROWS, HALF = 1728, 880
NARROW, WIDE = 384, 144
VMEM_LIMIT = 52 * 1024 * 1024


class Layout:
    def __init__(self, count, total, width):
        self.count = count
        self.width = width
        self.gains = 2 * width
        self.shard = total // count
        self.chunk = (total - self.gains) // count
        self.step = self.gains // count
        self.rows = self.chunk // 128
        half = -(-(self.rows + 10) // 2)
        self.half = -(-half // 16) * 16
        self.first = -(-(self.half // 2) // 16) * 16
        self.extra = 2 * self.half - self.rows
        self.bits = count.bit_length() - 1
        rest = self.bits - 2
        self.x_bits = -(-rest // 2)
        self.y_bits = rest - self.x_bits
        self.in_plane = 1 << rest
        self.flip = self.x_bits == self.y_bits


def pack_wide(flat, width):
    panels = width // 128
    return flat.reshape(-1, panels, 128).transpose(1, 0, 2).reshape(-1, 128)


def unpack_wide(rows, width):
    panels = width // 128
    return rows.reshape(panels, -1, 128).transpose(1, 0, 2).reshape(-1)


def pack_narrow(flat):
    rows = flat.reshape(-1, 576)
    count = rows.shape[0]
    panels = rows[:, :512].reshape(count, 4, 128).transpose(1, 0, 2).reshape(-1, 128)
    tail = rows[:, 512:]
    return jnp.concatenate([panels, jnp.concatenate([tail[: count // 2], tail[count // 2 :]], 1)], 0)


def unpack_narrow(packed):
    count = packed.shape[0] * 2 // 9
    panels = packed[: 4 * count].reshape(4, count, 128).transpose(1, 0, 2).reshape(count, 512)
    half = packed[4 * count :]
    tail = jnp.concatenate([half[:, :64], half[:, 64:]], 0)
    return jnp.concatenate([panels, tail], 1).reshape(-1)


def head_narrow(flat):
    rows = flat.reshape(2, 576)
    tail = jnp.pad(rows[:, 512:], ((0, 0), (64, 0)))
    return jnp.concatenate([rows[:, :512].reshape(8, 128), tail], 0)


def unhead_narrow(rows):
    return jnp.concatenate([rows[:8].reshape(2, 512), rows[8:10, 64:]], 1).reshape(-1)


def head_wide(flat):
    return jnp.pad(flat.reshape(9, 128), ((0, 1), (0, 0)))


def unhead_wide(rows):
    return rows[:9].reshape(-1)


def is_wide(index, count):
    return (index >= count // 4) & (index < 3 * count // 4)


def pack_payload(window, index, lay):
    head, chunk = window[: lay.gains], window[lay.gains :]
    body = jnp.where(is_wide(index, lay.count), pack_wide(chunk, FF), pack_narrow(chunk))
    top = jnp.where(is_wide(index - 1, lay.count), head_wide(head), head_narrow(head))
    return jnp.concatenate([body, jnp.pad(top, ((0, lay.extra - 10), (0, 0)))], 0)


def unpack_payload(rows, index, lay):
    body, top = rows[: lay.rows], rows[lay.rows : lay.rows + 10]
    chunk = jnp.where(is_wide(index, lay.count), unpack_wide(body, FF), unpack_narrow(body))
    head = jnp.where(is_wide(index - 1, lay.count), unhead_wide(top), unhead_narrow(top))
    return jnp.concatenate([head, chunk])


def swap(value, mask, count):
    return lax.ppermute(value, "dp", [(i, i ^ mask) for i in range(count)])


def swap_rep(value):
    return lax.ppermute(value, "rep", [(0, 1), (1, 0)])


def hop(value, masks, count):
    pairs = [(2 * i + c, 2 * (i ^ masks[c]) + c) for i in range(count) for c in range(2)]
    return lax.ppermute(value, ("dp", "rep"), pairs)


def hops(lay):
    xs = [d for d in range(1, 1 << lay.x_bits)]
    ys = [e << lay.x_bits for e in range(1, 1 << lay.y_bits)]
    if lay.flip:
        return list(zip(xs, ys)), list(zip(ys, xs))
    return list(zip(xs, xs)), list(zip(ys, ys))


def gather_hops(value, masks, count):
    return jnp.stack([value] + [hop(value, pair, count) for pair in masks], 0)


def gather(half, lay):
    n = lay.count
    first, second = hops(lay)
    planes = [half] + [swap(half, s << (lay.bits - 2), n) for s in range(1, PLANES)]
    own, twin = [], []
    for plane in planes:
        whole = gather_hops(gather_hops(plane, first, n), second, n)
        whole = whole.reshape(lay.in_plane, lay.half, 128)
        own.append(whole)
        twin.append(swap_rep(whole))
    return own, twin


def add_hops(value, masks, count):
    total = value[0].astype(F32)
    for d, pair in enumerate(masks):
        total = total + hop(value[d + 1], pair, count).astype(F32)
    return total.astype(value.dtype)


def reduce_plane(value, lay):
    first, second = hops(lay)
    grid = value.reshape(len(second) + 1, len(first) + 1, lay.half, 128)
    return add_hops(add_hops(grid, second, lay.count), first, lay.count)


def sum_everywhere(value, lay):
    value = value + swap_rep(value)
    for bit in range(lay.bits):
        value = value + swap(value, 1 << bit, lay.count)
    return value


def rope_tables(places):
    expon = jnp.arange(HEAD // 2).astype(jnp.float32) * (2.0 / HEAD)
    inverse = jnp.power(ROPE_BASE, -expon)
    angle = places.astype(jnp.float32)[..., None] * inverse
    return (jnp.cos(angle), jnp.sin(angle))


def dot(left, right):
    return jnp.dot(left, right, preferred_element_type=F32)


def dot_nt(left, right):
    return lax.dot_general(left, right, (((1,), (1,)), ((), ())), preferred_element_type=F32)


def dot_tn(left, right):
    return dot(left.astype(F32).T.astype(BF16), right)


def row_of_head(head, which):
    parts = [head[4 * which + j : 4 * which + j + 1] for j in range(4)]
    return jnp.concatenate(parts + [head[8 + which : 9 + which, 64:]], 1)


def head_of_rows(rows):
    parts = [row[:, 128 * j : 128 * j + 128] for row in rows for j in range(4)]
    zeros = jnp.zeros((1, 64), F32)
    parts = parts + [jnp.concatenate([zeros, row[:, 512:]], 1) for row in rows]
    return jnp.concatenate(parts + [jnp.zeros((6, 128), F32)], 0)


def gain_rows(gain, low):
    parts = [gain[:, 128 * j : 128 * j + 128] for j in range(4)]
    parts = parts + [jnp.concatenate([gain[:, 512:], gain[:, 512:]], 1)]
    return jnp.concatenate([low[:10]] + parts + [jnp.zeros((1, 128), F32)], 0)


def load_narrow(ref, index):
    parts = [ref[index, NARROW * j : NARROW * (j + 1), :] for j in range(4)]
    half = ref[index, 4 * NARROW : ROWS, :]
    tail = jnp.concatenate([half[:, :64], half[:, 64:]], 0)
    return jnp.concatenate(parts + [tail], 1)


def store_narrow(ref, index, value):
    for j in range(4):
        ref[index, NARROW * j : NARROW * (j + 1), :] = value[:, 128 * j : 128 * (j + 1)].astype(BF16)
    tail = value[:, 512:]
    tail = jnp.concatenate([tail[: NARROW // 2], tail[NARROW // 2 :]], 1)
    ref[index, 4 * NARROW : ROWS, :] = tail.astype(BF16)


def narrow_tiles():
    tiles = [(NARROW * (j + 1) - 16, j, 4 + j) for j in range(4)]
    return tiles + [(ROWS - 16, 8, 9)]


def add_tail(ref, index, wide):
    head = ref[index + 1, ROWS : ROWS + 16, :].astype(F32)
    row = lax.broadcasted_iota(jnp.int32, (16, 128), 0)
    if wide:
        for k in range(9):
            at = WIDE * (4 + k) - 16
            tile = ref[index, at : at + 16, :].astype(F32)
            tile = tile + jnp.where(row == 15, head[k : k + 1], 0.0)
            ref[index, at : at + 16, :] = tile.astype(BF16)
    else:
        for at, upper, lower in narrow_tiles():
            tile = ref[index, at : at + 16, :].astype(F32)
            tile = tile + jnp.where(row == 14, head[upper : upper + 1], 0.0)
            tile = tile + jnp.where(row == 15, head[lower : lower + 1], 0.0)
            ref[index, at : at + 16, :] = tile.astype(BF16)


def tail_of(ref, index, wide):
    if wide:
        parts = []
        for k in range(9):
            at = WIDE * (4 + k) - 16
            parts.append(ref[index, at : at + 16, :].astype(F32)[15:16])
        return jnp.concatenate(parts + [jnp.zeros((7, 128), F32)], 0)
    tiles = [ref[index, at : at + 16, :].astype(F32) for at, _, _ in narrow_tiles()]
    parts = [tile[14:15] for tile in tiles[:4]] + [tile[15:16] for tile in tiles[:4]]
    parts = parts + [tiles[4][14:15], tiles[4][15:16]]
    return jnp.concatenate(parts + [jnp.zeros((6, 128), F32)], 0)


def spread(value, first, second, out):
    for m in range(3):
        part = value[:, 192 * m : 192 * (m + 1)].astype(F32)
        first[pl.ds(m, 192, stride=3), :] = part[:, :128]
        second[pl.ds(m, 192, stride=3), :] = jnp.concatenate([part[:, 128:], part[:, 128:]], 1)
    out[:, :128] = first[...].astype(BF16)
    out[:, 128:] = second[:, :64].astype(BF16)


def unspread(value, first, second):
    first[...] = value[:, :128]
    second[...] = jnp.concatenate([value[:, 128:], value[:, 128:]], 1)
    parts = []
    for m in range(3):
        parts.append(first[pl.ds(m, 192, stride=3), :])
        parts.append(second[pl.ds(m, 192, stride=3), :][:, :64])
    return jnp.concatenate(parts, 1)


def turn(vector, cosine, sine):
    swapped = jnp.concatenate([vector[:, 32:], vector[:, :32]], 1)
    return vector * cosine + swapped * sine


def piece_copies(idx, refs, dst, relative, sems, outward):
    plane, place, core, flip = idx[0], idx[1], idx[2], idx[3]
    copies = []
    for s, (own, twin) in enumerate(refs):
        at_plane = jnp.bitwise_xor(plane, s) if relative else s
        for d in range(4):
            turned = ((d & 1) << 1) | (d >> 1)
            for which, ref in enumerate((own, twin)):
                side = jnp.bitwise_xor(core, which)
                offset = jnp.where(side * flip == 1, turned, d)
                chunk = 4 * at_plane + jnp.bitwise_xor(place, offset)
                rows = pl.ds(pl.multiple_of(side * HALF, 16), HALF)
                inner, outer = dst.at[chunk, rows, :], ref.at[d]
                pair = (inner, outer) if outward else (outer, inner)
                copies.append(
                    pltpu.make_async_copy(pair[0], pair[1], sems.at[at_plane, 2 * d + which])
                )
    return copies


def first_kernel(
    idx, own0, own1, own2, own3, twin0, twin1, twin2, twin3, tok_hbm, cot_hbm, cos_hbm, sin_hbm,
    y_out, dr_out, att_out, p_out, q_out, k_out, v_out, wq, wk, wv, wo, gain_out, dg_out,
    keep1, keep2, keep3, send1, send2, send3,
    w, g, tok, cot, cos, sin, att, n2_ref, n2t_ref, y_acc, dn_acc, first, second,
    in_sems, sems, out_sems,
):
    inputs = [
        pltpu.make_async_copy(src, dst, in_sems.at[i])
        for i, (src, dst) in enumerate(
            ((tok_hbm, tok), (cos_hbm, cos), (sin_hbm, sin), (cot_hbm, cot))
        )
    ]
    for copy in inputs:
        copy.start()
    loads = piece_copies(
        idx, [(own0, twin0), (own1, twin1), (own2, twin2), (own3, twin3)], w, True, sems, False
    )
    for copy in loads:
        copy.start()

    def arrived(plane):
        for j in range(8):
            pltpu.make_async_copy(
                own0.at[0], w.at[4 * plane, pl.ds(0, HALF), :], sems.at[plane, j]
            ).wait()

    tokens = tok.shape[0]
    for copy in inputs:
        copy.wait()
    x = tok[...].astype(F32)
    normed = x * lax.rsqrt(jnp.mean(x * x, -1, keepdims=True) + EPS)
    arrived(0)
    for c in range(3):
        add_tail(w, c, False)
    arrived(1)
    add_tail(w, 3, False)
    gains = w[0, ROWS : ROWS + 16, :].astype(F32)
    gain_in, gain_mid = row_of_head(gains, 0), row_of_head(gains, 1)
    gain_out[...] = gain_in
    n1 = (normed * gain_in).astype(BF16)
    wq[:NARROW, :] = load_narrow(w, 0)
    mixed_chunk = load_narrow(w, 1)
    wq[NARROW:, :] = mixed_chunk[:192]
    spread(mixed_chunk[192:], first, second, wk)
    mixed_chunk = load_narrow(w, 2)
    spread(mixed_chunk[:192], first, second, wv)
    wo[:192, :] = mixed_chunk[192:]
    wo[192:, :] = load_narrow(w, 3)

    query, keys, values = dot(n1, wq[...]), dot(n1, wk[...]), dot(n1, wv[...])
    row = lax.broadcasted_iota(jnp.int32, (3 * SEQ_LEN, SEQ_LEN), 0)
    causal = jnp.bitwise_and(row, SEQ_LEN - 1) >= lax.broadcasted_iota(
        jnp.int32, (3 * SEQ_LEN, SEQ_LEN), 1
    )
    for b in range(tokens // SEQ_LEN):
        part = slice(SEQ_LEN * b, SEQ_LEN * (b + 1))
        cosine, sine = cos[part, :], sin[part, :]
        for kv in range(KV_HEADS):
            at = KV_HEADS * b + kv
            heads = [
                turn(query[part, HEAD * h : HEAD * (h + 1)], cosine, sine)
                for h in range(3 * kv, 3 * kv + 3)
            ]
            q3 = jnp.concatenate(heads, 0).astype(BF16)
            k1 = turn(keys[part, HEAD * kv : HEAD * (kv + 1)], cosine, sine).astype(BF16)
            v1 = values[part, HEAD * kv : HEAD * (kv + 1)].astype(BF16)
            q_out[at], k_out[at], v_out[at] = q3, k1, v1
            score = jnp.where(causal, dot_nt(q3, k1) * HEAD**-0.5, -1e30)
            expon = jnp.exp(score - jnp.max(score, -1, keepdims=True))
            probs = expon / jnp.sum(expon, -1, keepdims=True)
            p_out[at] = probs
            mix = dot(probs.astype(BF16), v1)
            for r in range(3):
                h = 3 * kv + r
                att[part, HEAD * h : HEAD * (h + 1)] = mix[SEQ_LEN * r : SEQ_LEN * (r + 1)]
    attended = att[...].astype(BF16)
    att_out[...] = attended
    mixed = x + dot(attended, wo[...])
    inverse = lax.rsqrt(jnp.mean(mixed * mixed, -1, keepdims=True) + EPS)
    normed_mid = mixed * inverse
    n2 = normed_mid * gain_mid
    n2_ref[...] = n2.astype(BF16)
    n2t_ref[...] = n2.astype(BF16).astype(F32).T.astype(BF16)
    y_acc[...] = mixed
    dn_acc[...] = jnp.zeros_like(dn_acc)
    arrived(2)
    arrived(3)

    def fix(i, carry):
        add_tail(w, i + 4, True)
        return carry

    lax.fori_loop(0, 8, fix, 0)
    for c in (12, 13, 14):
        add_tail(w, c, False)

    def block(k, carry):
        def wide(base, p):
            at = pl.multiple_of((3 * k + p) * WIDE, 16)
            return jnp.concatenate([w[base + d, pl.ds(at, WIDE), :] for d in range(4)], 0)

        w_gate = jnp.concatenate([wide(4, p) for p in range(3)], 1)
        w_up = jnp.concatenate([wide(8, p) for p in range(3)], 1)
        w_down = load_narrow(w, 12 + k)
        c = cot[...]
        gate, up = dot(n2_ref[...], w_gate), dot(n2_ref[...], w_up)
        sigma = 1.0 / (1.0 + jnp.exp(-gate))
        silu = gate * sigma
        hidden = (silu * up).astype(BF16)
        y_acc[...] += dot(hidden, w_down)
        store_narrow(g, 8 + k, dot_tn(hidden, c))
        d_hidden = dot_nt(c, w_down)
        d_gate = (d_hidden * up * sigma * (1.0 + gate * (1.0 - sigma))).astype(BF16)
        d_up = (d_hidden * silu).astype(BF16)
        dn_acc[...] += dot_nt(d_gate, w_gate) + dot_nt(d_up, w_up)
        for base, d_out in ((0, d_gate), (4, d_up)):
            grad = dot(n2t_ref[...], d_out).astype(BF16)
            for p in range(3):
                at = pl.multiple_of((3 * k + p) * WIDE, 16)
                for d in range(4):
                    g[base + d, pl.ds(at, WIDE), :] = grad[
                        WIDE * d : WIDE * (d + 1), 128 * p : 128 * (p + 1)
                    ]
        return carry

    lax.fori_loop(0, 4, block, 0)
    d_norm = dn_acc[...]
    d_gain = jnp.sum(d_norm * normed_mid, 0, keepdims=True)
    dg_out[...] = d_gain
    for c in range(12):
        top = tail_of(g, c - 1, c - 1 < 8) if c else jnp.zeros((16, 128), F32)
        g[c, ROWS : ROWS + 16, :] = top.astype(BF16)
        g[c, ROWS + 16 :, :] = gain_rows(d_gain, jnp.zeros((16, 128), F32)).astype(BF16)
    stores = piece_copies(
        idx, [(keep1, send1), (keep2, send2), (keep3, send3)], g, False, out_sems, True
    )
    for copy in stores:
        copy.start()
    y_out[...] = y_acc[...].astype(BF16)
    scaled = d_norm * gain_mid
    dr_out[...] = cot[...].astype(F32) + inverse * (
        scaled - normed_mid * jnp.mean(scaled * normed_mid, -1, keepdims=True)
    )
    for copy in stores:
        copy.wait()


def second_kernel(
    idx, tok, cos, sin, dr, att, p_in, q_in, k_in, v_in, wq, wk, wv, wo, gain, dg,
    dx_out, keep, send,
    g, dq_ref, dk_ref, dv_ref, first, second, out_sems,
):
    tokens = tok.shape[0]
    d_mixed = dr[...]
    branch = d_mixed.astype(BF16)
    dw_out = dot_tn(att[...], branch)
    d_att = dot_nt(branch, wo[...])
    for b in range(tokens // SEQ_LEN):
        part = slice(SEQ_LEN * b, SEQ_LEN * (b + 1))
        cosine, sine = cos[part, :], -sin[part, :]
        for kv in range(KV_HEADS):
            at = KV_HEADS * b + kv
            heads = [d_att[part, HEAD * h : HEAD * (h + 1)] for h in range(3 * kv, 3 * kv + 3)]
            d3 = jnp.concatenate(heads, 0).astype(BF16)
            probs, q3, k1, v1 = p_in[at], q_in[at], k_in[at], v_in[at]
            d_probs = dot_nt(d3, v1)
            dv_ref[part, HEAD * kv : HEAD * (kv + 1)] = dot_tn(probs.astype(BF16), d3)
            inner = jnp.sum(d_probs * probs, -1, keepdims=True)
            d_score = (probs * (d_probs - inner)).astype(BF16)
            dq3 = dot(d_score, k1) * HEAD**-0.5
            for r in range(3):
                h = 3 * kv + r
                dq_ref[part, HEAD * h : HEAD * (h + 1)] = turn(
                    dq3[SEQ_LEN * r : SEQ_LEN * (r + 1)], cosine, sine
                )
            dk_ref[part, HEAD * kv : HEAD * (kv + 1)] = turn(
                dot_tn(d_score, q3) * HEAD**-0.5, cosine, sine
            )
    dq, dk, dv = dq_ref[...].astype(BF16), dk_ref[...].astype(BF16), dv_ref[...].astype(BF16)
    x = tok[...].astype(F32)
    inverse = lax.rsqrt(jnp.mean(x * x, -1, keepdims=True) + EPS)
    normed = x * inverse
    n1t = (normed * gain[...]).astype(BF16).astype(F32).T.astype(BF16)
    dw_query = dot(n1t, dq)
    store_narrow(g, 0, dw_query[:NARROW])
    dw = unspread(dot(n1t, dk), first, second)
    store_narrow(g, 1, jnp.concatenate([dw_query[NARROW:], dw], 0))
    dw = unspread(dot(n1t, dv), first, second)
    store_narrow(g, 2, jnp.concatenate([dw, dw_out[:192]], 0))
    store_narrow(g, 3, dw_out[192:])
    d_norm = dot_nt(dq, wq[...]) + dot_nt(dk, wk[...]) + dot_nt(dv, wv[...])
    d_gain = jnp.sum(d_norm * normed, 0, keepdims=True)
    for c in range(4):
        top = tail_of(g, c - 1, False) if c else head_of_rows([d_gain, dg[...]])
        low = jnp.zeros((16, 128), F32) if c else tail_of(g, 3, False)
        g[c, ROWS : ROWS + 16, :] = top.astype(BF16)
        g[c, ROWS + 16 :, :] = gain_rows(dg[...], low).astype(BF16)
    stores = piece_copies(idx, [(keep, send)], g, False, out_sems, True)
    for copy in stores:
        copy.start()
    scaled = d_norm * gain[...]
    dx_out[...] = d_mixed + inverse * (
        scaled - normed * jnp.mean(scaled * normed, -1, keepdims=True)
    )
    for copy in stores:
        copy.wait()


def halves_turned(low, high):
    lane = lax.broadcasted_iota(jnp.int32, low.shape, 1)
    return jnp.where(lane < 64, pltpu.roll(low, 64, 1), pltpu.roll(high, 64, 1))


def pack_kernel(idx, flat, out, rolled, window, packed, mixed):
    index, core, down, right = idx[0], idx[1], idx[2], idx[3]
    lane = lax.broadcasted_iota(jnp.int32, (1, 128), 1)
    rolled[0:16, :] = jnp.zeros((16, 128), F32)
    rolled[16:1752, :] = pltpu.roll(flat[...].astype(F32), right, 1)
    rolled[1752:1760, :] = jnp.zeros((8, 128), F32)
    window[...] = jnp.where(
        lane >= right, rolled[pl.ds(16 - down, 1744), :], rolled[pl.ds(15 - down, 1744), :]
    )
    head = [window[k : k + 1, :] for k in range(9)]
    wide = (index >= 4) & (index < 12)

    @pl.when(wide)
    def _():
        for j in range(12):
            packed[WIDE * j : WIDE * (j + 1), :] = window[pl.ds(9 + j, WIDE, stride=12), :]

    @pl.when(jnp.logical_not(wide))
    def _():
        parts = [window[pl.ds(9 + k, NARROW // 2, stride=9), :] for k in range(9)]
        for j in range(4):
            packed[pl.ds(NARROW * j, NARROW // 2, stride=2), :] = parts[j]
            packed[pl.ds(NARROW * j + 1, NARROW // 2, stride=2), :] = halves_turned(
                parts[4 + j], parts[5 + j]
            )
        mixed[pl.ds(0, NARROW // 2, stride=2), :] = parts[4]
        mixed[pl.ds(1, NARROW // 2, stride=2), :] = pltpu.roll(parts[8], 64, 1)
        packed[4 * NARROW : ROWS, :] = jnp.where(
            lane < 64, mixed[: NARROW // 2, :], pltpu.roll(mixed[NARROW // 2 :, :], 64, 1)
        )

    last = jnp.zeros((23, 128), F32)
    after_wide = (index >= 5) & (index < 13)

    @pl.when(after_wide)
    def _():
        packed[ROWS:, :] = jnp.concatenate(head + [last], 0)

    @pl.when(jnp.logical_not(after_wide))
    def _():
        rows = head[:4] + [halves_turned(head[4 + j], head[5 + j]) for j in range(4)]
        rows.append(jnp.where(lane < 64, 0.0, pltpu.roll(head[4], 64, 1)))
        rows.append(jnp.where(lane < 64, 0.0, head[8]))
        packed[ROWS:, :] = jnp.concatenate(rows + [last[:22]], 0)

    out[...] = packed[pl.ds(pl.multiple_of(core * HALF, 16), HALF), :].astype(BF16)


def unpack_kernel(idx, own, twin, out, packed, window, mixed):
    index, core, down, left = idx[0], idx[1], idx[2], idx[3]
    lane = lax.broadcasted_iota(jnp.int32, (1, 128), 1)
    packed[pl.ds(pl.multiple_of(core * HALF, 16), HALF), :] = own[...]
    packed[pl.ds(pl.multiple_of((1 - core) * HALF, 16), HALF), :] = twin[...]
    head = [packed[ROWS + k : ROWS + k + 1, :] for k in range(10)]
    window[1737:, :] = jnp.zeros((15, 128), F32)
    wide = (index >= 4) & (index < 12)

    @pl.when(wide)
    def _():
        for j in range(12):
            window[pl.ds(9 + j, WIDE, stride=12), :] = packed[WIDE * j : WIDE * (j + 1), :]

    @pl.when(jnp.logical_not(wide))
    def _():
        half = packed[4 * NARROW : ROWS, :]
        mixed[: NARROW // 2, :] = half
        mixed[NARROW // 2 :, :] = pltpu.roll(half, 64, 1)
        odd = []
        for j in range(4):
            window[pl.ds(9 + j, NARROW // 2, stride=9), :] = packed[
                pl.ds(NARROW * j, NARROW // 2, stride=2), :
            ]
            odd.append(pltpu.roll(packed[pl.ds(NARROW * j + 1, NARROW // 2, stride=2), :], 64, 1))
        odd.append(mixed[pl.ds(1, NARROW // 2, stride=2), :])
        before = mixed[pl.ds(0, NARROW // 2, stride=2), :]
        for j in range(4):
            window[pl.ds(13 + j, NARROW // 2, stride=9), :] = jnp.where(lane < 64, before, odd[j])
            before = odd[j]
        window[pl.ds(17, NARROW // 2, stride=9), :] = jnp.where(
            lane < 64, before, pltpu.roll(odd[4], 64, 1)
        )

    after_wide = (index >= 5) & (index < 13)

    @pl.when(after_wide)
    def _():
        window[0:9, :] = jnp.concatenate(head[:9], 0)

    @pl.when(jnp.logical_not(after_wide))
    def _():
        odd = [pltpu.roll(row, 64, 1) for row in head[4:8]]
        before, rows = pltpu.roll(head[8], 64, 1), head[:4]
        for j in range(4):
            rows.append(jnp.where(lane < 64, before, odd[j]))
            before = odd[j]
        rows.append(jnp.where(lane < 64, before, head[9]))
        window[0:9, :] = jnp.concatenate(rows, 0)

    lanes = pltpu.roll(window[...], jnp.bitwise_and(128 - left, 127), 1)
    window[...] = lanes
    out[...] = jnp.where(
        lane < 128 - left, window[pl.ds(down, 1736), :], window[pl.ds(down + 1, 1736), :]
    )


def chunk_index(index, core, lay):
    start = index * lay.step
    return jnp.stack([index, core, start // 128, start % 128]).astype(jnp.int32)


def pack_own(params, index, core, lay):
    if lay.count != CANON:
        window = jnp.zeros((lay.gains + lay.chunk,), params.dtype)
        window = lax.dynamic_update_slice(window, params, (index * lay.step,))
        payload = pack_payload(window, index, lay)
        return lax.dynamic_slice_in_dim(payload, core * lay.half, lay.half, 0)
    flat = jnp.pad(params, (0, 1736 * 128 - lay.shard)).reshape(1736, 128)
    vmem = pl.BlockSpec(memory_space=pltpu.VMEM)
    return pl.pallas_call(
        pack_kernel,
        name="pack_own_chunk",
        in_specs=[pl.BlockSpec(memory_space=pltpu.SMEM), vmem],
        out_specs=vmem,
        out_shape=jax.ShapeDtypeStruct((HALF, 128), BF16),
        scratch_shapes=[
            pltpu.VMEM((1760, 128), F32),
            pltpu.VMEM((1744, 128), F32),
            pltpu.VMEM((2 * HALF, 128), F32),
            pltpu.VMEM((NARROW, 128), F32),
        ],
        compiler_params=pltpu.CompilerParams(vmem_limit_bytes=VMEM_LIMIT),
    )(chunk_index(index, core, lay), flat)


def unpack_own(own, twin, index, core, lay):
    if lay.count != CANON:
        rows = jnp.where(core == 0, jnp.stack([own, twin], 0), jnp.stack([twin, own], 0))
        window = unpack_payload(rows.reshape(2 * lay.half, 128), index, lay)
        return lax.dynamic_slice(window, (index * lay.step,), (lay.shard,))
    vmem = pl.BlockSpec(memory_space=pltpu.VMEM)
    rows = pl.pallas_call(
        unpack_kernel,
        name="unpack_own_chunk",
        in_specs=[pl.BlockSpec(memory_space=pltpu.SMEM), vmem, vmem],
        out_specs=vmem,
        out_shape=jax.ShapeDtypeStruct((1736, 128), F32),
        scratch_shapes=[
            pltpu.VMEM((2 * HALF, 128), F32),
            pltpu.VMEM((1752, 128), F32),
            pltpu.VMEM((NARROW, 128), F32),
        ],
        compiler_params=pltpu.CompilerParams(vmem_limit_bytes=VMEM_LIMIT),
    )(chunk_index(index, core, lay), own, twin)
    return rows.reshape(-1)[: lay.shard]


def run_layer(idx, own, twin, tokens, cotangent, positions):
    length, width = tokens.shape
    groups = length // SEQ_LEN * KV_HEADS
    cosine, sine = rope_tables(positions)
    cosine = jnp.concatenate([cosine, cosine], 1)
    sine = jnp.concatenate([-sine, sine], 1)
    kv_width = KV_HEADS * HEAD
    smem = pl.BlockSpec(memory_space=pltpu.SMEM)
    vmem = pl.BlockSpec(memory_space=pltpu.VMEM)
    anywhere = pl.BlockSpec(memory_space=pl.ANY)

    def sds(shape, dtype):
        return jax.ShapeDtypeStruct(shape, dtype)

    piece = sds((4, HALF, 128), BF16)
    weights = [sds((width, width), BF16), sds((width, kv_width), BF16)]
    weights = weights + [weights[1], weights[0]]
    saved = [
        sds((groups, 3 * SEQ_LEN, SEQ_LEN), F32),
        sds((groups, 3 * SEQ_LEN, HEAD), BF16),
        sds((groups, SEQ_LEN, HEAD), BF16),
        sds((groups, SEQ_LEN, HEAD), BF16),
    ]
    outs = [sds((length, width), BF16), sds((length, width), F32), sds((length, width), BF16)]
    outs = outs + saved + weights + [sds((1, width), F32)] * 2
    results = pl.pallas_call(
        first_kernel,
        name="forward_and_ff_backward",
        in_specs=[smem] + [anywhere] * 12,
        out_specs=[vmem] * len(outs) + [anywhere] * 6,
        out_shape=outs + [piece] * 6,
        scratch_shapes=[
            pltpu.VMEM((CANON, 2 * HALF, 128), BF16),
            pltpu.VMEM((12, 2 * HALF, 128), BF16),
            pltpu.VMEM((length, width), BF16),
            pltpu.VMEM((length, width), BF16),
            pltpu.VMEM((length, HEAD), F32),
            pltpu.VMEM((length, HEAD), F32),
            pltpu.VMEM((length, width), F32),
            pltpu.VMEM((length, width), BF16),
            pltpu.VMEM((width, length), BF16),
            pltpu.VMEM((length, width), F32),
            pltpu.VMEM((length, width), F32),
            pltpu.VMEM((width, 128), F32),
            pltpu.VMEM((width, 128), F32),
            pltpu.SemaphoreType.DMA((4,)),
            pltpu.SemaphoreType.DMA((4, 8)),
            pltpu.SemaphoreType.DMA((3, 8)),
        ],
        compiler_params=pltpu.CompilerParams(vmem_limit_bytes=VMEM_LIMIT),
        cost_estimate=pl.CostEstimate(
            flops=20 * length * width * FF, bytes_accessed=16_000_000, transcendentals=600_000
        ),
    )(idx, *own, *twin, tokens, cotangent, cosine, sine)
    output, d_mixed, attended, probs, q3, k1, v1, wq, wk, wv, wo, gain, d_gain = results[:13]
    keeps, sends = list(results[13:16]), list(results[16:19])
    d_input, keep, send = pl.pallas_call(
        second_kernel,
        name="attention_backward",
        in_specs=[smem] + [vmem] * 15,
        out_specs=[vmem] + [anywhere] * 2,
        out_shape=[sds((length, width), F32), piece, piece],
        scratch_shapes=[
            pltpu.VMEM((4, 2 * HALF, 128), BF16),
            pltpu.VMEM((length, width), F32),
            pltpu.VMEM((length, kv_width), F32),
            pltpu.VMEM((length, kv_width), F32),
            pltpu.VMEM((width, 128), F32),
            pltpu.VMEM((width, 128), F32),
            pltpu.SemaphoreType.DMA((1, 8)),
        ],
        compiler_params=pltpu.CompilerParams(vmem_limit_bytes=VMEM_LIMIT),
        cost_estimate=pl.CostEstimate(
            flops=10 * length * width * width, bytes_accessed=10_000_000, transcendentals=0
        ),
    )(idx, tokens, cosine, sine, d_mixed, attended, probs, q3, k1, v1, wq, wk, wv, wo, gain, d_gain)
    return output, d_input, d_gain[0], [keep] + keeps, [send] + sends


def flat_of(payloads, lay):
    n = lay.count
    heads = payloads[:, lay.rows : lay.rows + 10]
    flats = [unhead_narrow(heads[0])]
    for i in range(n):
        wide = n // 4 <= i < 3 * n // 4
        body = payloads[i, : lay.rows]
        flat = unpack_wide(body, FF) if wide else unpack_narrow(body)
        if i + 1 < n:
            tail = unhead_wide(heads[i + 1]) if wide else unhead_narrow(heads[i + 1])
            flat = jnp.concatenate([flat[: -lay.gains], flat[-lay.gains :] + tail])
        flats.append(flat)
    return jnp.concatenate(flats)


def payloads_of(flat, lay):
    windows = [
        flat[i * lay.chunk : (i + 1) * lay.chunk + lay.gains] for i in range(lay.count)
    ]
    return jnp.stack([pack_payload(window, i, lay) for i, window in enumerate(windows)], 0)


def canonical(own, twin, lay, canon, index, core):
    own, twin = jnp.stack(own, 0), jnp.stack(twin, 0)
    both = jnp.where(core == 0, jnp.stack([own, twin], 2), jnp.stack([twin, own], 2))
    both = both.reshape(lay.count, 2 * lay.half, 128)
    both = jnp.take(both, jnp.arange(lay.count, dtype=jnp.int32) ^ index, axis=0)
    flat = flat_of(both, lay)
    zeros = jnp.zeros((canon.gains,), flat.dtype)
    rows = []
    for i in range(CANON):
        window = flat[i * canon.chunk : (i + 1) * canon.chunk + canon.gains]
        if i:
            window = jnp.concatenate([zeros, window[canon.gains :]])
        rows.append(pack_payload(window, i, canon))
    rows = jnp.stack(rows, 0).reshape(PLANES, 4, 2, canon.half, 128)
    return [list(rows[:, :, c]) for c in range(2)]


def from_canonical(keeps, sends, lay, canon, place, core):
    rows = jnp.stack([jnp.stack(keeps, 0), jnp.stack(sends, 0)], 2)
    rows = rows.reshape(CANON, 2 * canon.half, 128)
    flats = [unhead_narrow(rows[0, canon.rows : canon.rows + 10])]
    for i in range(CANON):
        body = rows[i, : canon.rows]
        flats.append(unpack_wide(body, FF) if 4 <= i < 12 else unpack_narrow(body))
    rows = payloads_of(jnp.concatenate(flats), lay)
    rows = rows.reshape(PLANES, lay.in_plane, 2, lay.half, 128)
    rows = jnp.take(rows, jnp.arange(lay.in_plane, dtype=jnp.int32) ^ place, axis=1)
    return list(jnp.take(rows, core, axis=2)), list(jnp.take(rows, 1 - core, axis=2))


def on_device(lay, canon, tokens_in, positions, params, cotangent):
    index = lax.axis_index("dp")
    core = lax.axis_index("rep")
    n, half, in_plane = lay.count, lay.half, lay.in_plane
    plane, place = index // in_plane, index % in_plane
    same = n == CANON
    own, twin = gather(pack_own(params, index, core, lay), lay)
    if same:
        idx = jnp.stack([plane, place, core, 1]).astype(jnp.int32)
    else:
        own, twin = canonical(own, twin, lay, canon, index, core)
        idx = jnp.zeros((4,), jnp.int32)
    output, d_input, d_gain, keeps, sends = run_layer(
        idx, own, twin, tokens_in, cotangent, positions
    )
    if not same:
        keeps, sends = from_canonical(keeps, sends, lay, canon, place, core)
    planes = []
    for keep, send in zip(keeps, sends):
        pair = keep.astype(F32) + swap_rep(send).astype(F32)
        planes.append(reduce_plane(pair.astype(BF16), lay))
    if same:
        at = ROWS - HALF
        row = jnp.arange(16)[:, None]
        late = jnp.where((core == 1) & (row < 10), planes[0][at + 16 : at + 32], jnp.zeros((16, 128), BF16))
        planes[1] = jnp.concatenate([planes[1][:at], planes[1][at : at + 16] + late, planes[1][at + 16 :]])
    planes = jnp.stack(planes, 0)
    parts = [jnp.take(planes, plane, axis=0).astype(F32)]
    for s in range(1, PLANES):
        part = swap(jnp.take(planes, plane ^ s, axis=0), s << (lay.bits - 2), n)
        parts.append(part.astype(F32))
    total = (parts[0] + parts[1]) + (parts[2] + parts[3])
    other = swap_rep(total)
    if same:
        at = ROWS + 26 - HALF
        d_gain = jnp.where(core == 1, total[at : at + 5], other[at : at + 5]).reshape(-1)[: lay.width]
    else:
        d_gain = sum_everywhere(d_gain, lay)
    return output, d_input, unpack_own(total, other, index, core, lay), d_gain


def solution(mesh):
    def run(tokens_in, positions, params, cotangent):
        total, width = params.shape[0], tokens_in.shape[1]
        lay = Layout(mesh.shape["dp"], total, width)
        canon = Layout(CANON, total, width)
        rows = P(("dp", "rep"), None)
        return jax.shard_map(
            lambda *args: on_device(lay, canon, *args),
            mesh=mesh,
            in_specs=(rows, P(("dp", "rep")), P("dp"), rows),
            out_specs=(rows, rows, P("dp"), P()),
            check_vma=False,
        )(tokens_in, positions, params, cotangent)

    return run
```

```python
import jax
import jax.numpy as jnp
from jax import lax
from jax.experimental import pallas as pl
from jax.experimental.pallas import tpu as pltpu
from jax.sharding import PartitionSpec as P

HEADS = 9
KV_HEADS = 3
HEAD = 64
FF = 1536
SEQ_LEN = 128
PLANES = 4
CANON = 16

EPS = 1e-05
ROPE_BASE = 100000.0

F32, BF16 = jnp.float32, jnp.bfloat16
ROWS, HALF = 1728, 880
NARROW, WIDE = 384, 144
VMEM_LIMIT = 52 * 1024 * 1024


class Layout:
    def __init__(self, count, total, width):
        self.count = count
        self.width = width
        self.gains = 2 * width
        self.shard = total // count
        self.chunk = (total - self.gains) // count
        self.step = self.gains // count
        self.rows = self.chunk // 128
        half = -(-(self.rows + 10) // 2)
        self.half = -(-half // 16) * 16
        self.first = -(-(self.half // 2) // 16) * 16
        self.extra = 2 * self.half - self.rows
        self.bits = count.bit_length() - 1
        rest = self.bits - 2
        self.x_bits = -(-rest // 2)
        self.y_bits = rest - self.x_bits
        self.in_plane = 1 << rest
        self.flip = self.x_bits == self.y_bits


def pack_wide(flat, width):
    panels = width // 128
    return flat.reshape(-1, panels, 128).transpose(1, 0, 2).reshape(-1, 128)


def unpack_wide(rows, width):
    panels = width // 128
    return rows.reshape(panels, -1, 128).transpose(1, 0, 2).reshape(-1)


def pack_narrow(flat):
    rows = flat.reshape(-1, 576)
    count = rows.shape[0]
    panels = rows[:, :512].reshape(count, 4, 128).transpose(1, 0, 2).reshape(-1, 128)
    tail = rows[:, 512:]
    return jnp.concatenate([panels, jnp.concatenate([tail[: count // 2], tail[count // 2 :]], 1)], 0)


def unpack_narrow(packed):
    count = packed.shape[0] * 2 // 9
    panels = packed[: 4 * count].reshape(4, count, 128).transpose(1, 0, 2).reshape(count, 512)
    half = packed[4 * count :]
    tail = jnp.concatenate([half[:, :64], half[:, 64:]], 0)
    return jnp.concatenate([panels, tail], 1).reshape(-1)


def head_narrow(flat):
    rows = flat.reshape(2, 576)
    tail = jnp.pad(rows[:, 512:], ((0, 0), (64, 0)))
    return jnp.concatenate([rows[:, :512].reshape(8, 128), tail], 0)


def unhead_narrow(rows):
    return jnp.concatenate([rows[:8].reshape(2, 512), rows[8:10, 64:]], 1).reshape(-1)


def head_wide(flat):
    return jnp.pad(flat.reshape(9, 128), ((0, 1), (0, 0)))


def unhead_wide(rows):
    return rows[:9].reshape(-1)


def is_wide(index, count):
    return (index >= count // 4) & (index < 3 * count // 4)


def pack_payload(window, index, lay):
    head, chunk = window[: lay.gains], window[lay.gains :]
    body = jnp.where(is_wide(index, lay.count), pack_wide(chunk, FF), pack_narrow(chunk))
    top = jnp.where(is_wide(index - 1, lay.count), head_wide(head), head_narrow(head))
    return jnp.concatenate([body, jnp.pad(top, ((0, lay.extra - 10), (0, 0)))], 0)


def unpack_payload(rows, index, lay):
    body, top = rows[: lay.rows], rows[lay.rows : lay.rows + 10]
    chunk = jnp.where(is_wide(index, lay.count), unpack_wide(body, FF), unpack_narrow(body))
    head = jnp.where(is_wide(index - 1, lay.count), unhead_wide(top), unhead_narrow(top))
    return jnp.concatenate([head, chunk])


def swap(value, mask, count):
    return lax.ppermute(value, "dp", [(i, i ^ mask) for i in range(count)])


def swap_rep(value):
    return lax.ppermute(value, "rep", [(0, 1), (1, 0)])


def hop(value, masks, count):
    pairs = [(2 * i + c, 2 * (i ^ masks[c]) + c) for i in range(count) for c in range(2)]
    return lax.ppermute(value, ("dp", "rep"), pairs)


def hops(lay):
    xs = [d for d in range(1, 1 << lay.x_bits)]
    ys = [e << lay.x_bits for e in range(1, 1 << lay.y_bits)]
    if lay.flip:
        return list(zip(xs, ys)), list(zip(ys, xs))
    return list(zip(xs, xs)), list(zip(ys, ys))


def gather_hops(value, masks, count):
    return jnp.stack([value] + [hop(value, pair, count) for pair in masks], 0)


def plane_of(plane, batch):
    other = jnp.bitwise_and(jnp.bitwise_xor(plane, 2), 2)
    return [plane, jnp.bitwise_xor(plane, 1), other, other + 1][batch]


def gather(half, plane, core, lay, beside):
    n = lay.count
    first, second = hops(lay)
    near, far = 1 << (lay.bits - 2), 2 << (lay.bits - 2)
    pair = swap(half, near, n)
    pair, beside = lax.optimization_barrier((pair, beside))
    even = plane % 2 == 0
    low, high = jnp.where(even, half, pair), jnp.where(even, pair, half)
    if n == CANON:
        at = ROWS - HALF
        extra = jnp.where(core == 1, high[at : at + 16], low[at + 16 : at + 32])
        low = jnp.concatenate([low[: at + 16], extra], 0)
    batches = [half, pair, swap(low, far, n), swap(high, far, n)]
    own, twin = [], []
    for batch in batches:
        whole = gather_hops(gather_hops(batch, first, n), second, n)
        whole = whole.reshape(lay.in_plane, lay.half, 128)
        own.append(whole)
        twin.append(swap_rep(whole))
    return own, twin, beside


def add_hops(value, masks, count):
    total = value[0].astype(F32)
    for d, pair in enumerate(masks):
        total = total + hop(value[d + 1], pair, count).astype(F32)
    return total.astype(value.dtype)


def reduce_plane(value, lay):
    first, second = hops(lay)
    grid = value.reshape(len(second) + 1, len(first) + 1, lay.half, 128)
    return add_hops(add_hops(grid, second, lay.count), first, lay.count)


def sum_everywhere(value, lay):
    value = value + swap_rep(value)
    for bit in range(lay.bits):
        value = value + swap(value, 1 << bit, lay.count)
    return value


def rope_tables(places):
    expon = jnp.arange(HEAD // 2).astype(jnp.float32) * (2.0 / HEAD)
    inverse = jnp.power(ROPE_BASE, -expon)
    angle = places.astype(jnp.float32)[..., None] * inverse
    return (jnp.cos(angle), jnp.sin(angle))


def dot(left, right):
    return jnp.dot(left, right, preferred_element_type=F32)


def dot_nt(left, right):
    return lax.dot_general(left, right, (((1,), (1,)), ((), ())), preferred_element_type=F32)


def dot_tn(left, right):
    return dot(left.astype(F32).T.astype(BF16), right)


def row_of_head(head, which):
    parts = [head[4 * which + j : 4 * which + j + 1] for j in range(4)]
    return jnp.concatenate(parts + [head[8 + which : 9 + which, 64:]], 1)


def head_of_rows(rows):
    parts = [row[:, 128 * j : 128 * j + 128] for row in rows for j in range(4)]
    zeros = jnp.zeros((1, 64), F32)
    parts = parts + [jnp.concatenate([zeros, row[:, 512:]], 1) for row in rows]
    return jnp.concatenate(parts + [jnp.zeros((6, 128), F32)], 0)


def gain_rows(gain, low):
    parts = [gain[:, 128 * j : 128 * j + 128] for j in range(4)]
    parts = parts + [jnp.concatenate([gain[:, 512:], gain[:, 512:]], 1)]
    return jnp.concatenate([low[:10]] + parts + [jnp.zeros((1, 128), F32)], 0)


def load_narrow(ref, index):
    parts = [ref[index, NARROW * j : NARROW * (j + 1), :] for j in range(4)]
    half = ref[index, 4 * NARROW : ROWS, :]
    tail = jnp.concatenate([half[:, :64], half[:, 64:]], 0)
    return jnp.concatenate(parts + [tail], 1)


def store_narrow(ref, index, value):
    for j in range(4):
        ref[index, NARROW * j : NARROW * (j + 1), :] = value[:, 128 * j : 128 * (j + 1)].astype(BF16)
    tail = value[:, 512:]
    tail = jnp.concatenate([tail[: NARROW // 2], tail[NARROW // 2 :]], 1)
    ref[index, 4 * NARROW : ROWS, :] = tail.astype(BF16)


def narrow_tiles():
    tiles = [(NARROW * (j + 1) - 16, j, 4 + j) for j in range(4)]
    return tiles + [(ROWS - 16, 8, 9)]


def add_tail(ref, index, wide):
    head = ref[index + 1, ROWS : ROWS + 16, :].astype(F32)
    row = lax.broadcasted_iota(jnp.int32, (16, 128), 0)
    if wide:
        for k in range(9):
            at = WIDE * (4 + k) - 16
            tile = ref[index, at : at + 16, :].astype(F32)
            tile = tile + jnp.where(row == 15, head[k : k + 1], 0.0)
            ref[index, at : at + 16, :] = tile.astype(BF16)
    else:
        for at, upper, lower in narrow_tiles():
            tile = ref[index, at : at + 16, :].astype(F32)
            tile = tile + jnp.where(row == 14, head[upper : upper + 1], 0.0)
            tile = tile + jnp.where(row == 15, head[lower : lower + 1], 0.0)
            ref[index, at : at + 16, :] = tile.astype(BF16)


def tail_of(ref, index, wide):
    if wide:
        parts = []
        for k in range(9):
            at = WIDE * (4 + k) - 16
            parts.append(ref[index, at : at + 16, :].astype(F32)[15:16])
        return jnp.concatenate(parts + [jnp.zeros((7, 128), F32)], 0)
    tiles = [ref[index, at : at + 16, :].astype(F32) for at, _, _ in narrow_tiles()]
    parts = [tile[14:15] for tile in tiles[:4]] + [tile[15:16] for tile in tiles[:4]]
    parts = parts + [tiles[4][14:15], tiles[4][15:16]]
    return jnp.concatenate(parts + [jnp.zeros((6, 128), F32)], 0)


def spread(value, first, second, out):
    for m in range(3):
        part = value[:, 192 * m : 192 * (m + 1)].astype(F32)
        first[pl.ds(m, 192, stride=3), :] = part[:, :128]
        second[pl.ds(m, 192, stride=3), :] = jnp.concatenate([part[:, 128:], part[:, 128:]], 1)
    out[:, :128] = first[...].astype(BF16)
    out[:, 128:] = second[:, :64].astype(BF16)


def unspread(value, first, second):
    first[...] = value[:, :128]
    second[...] = jnp.concatenate([value[:, 128:], value[:, 128:]], 1)
    parts = []
    for m in range(3):
        parts.append(first[pl.ds(m, 192, stride=3), :])
        parts.append(second[pl.ds(m, 192, stride=3), :][:, :64])
    return jnp.concatenate(parts, 1)


def turn(vector, cosine, sine):
    swapped = jnp.concatenate([vector[:, 32:], vector[:, :32]], 1)
    return vector * cosine + swapped * sine


def piece_copies(idx, refs, dst, relative, sems, outward):
    plane, place, core, flip = idx[0], idx[1], idx[2], idx[3]
    copies = []
    for s, (own, twin) in enumerate(refs):
        at_plane = plane_of(plane, s) if relative else s
        for d in range(4):
            turned = ((d & 1) << 1) | (d >> 1)
            for which, ref in enumerate((own, twin)):
                side = jnp.bitwise_xor(core, which)
                offset = jnp.where(side * flip == 1, turned, d)
                chunk = 4 * at_plane + jnp.bitwise_xor(place, offset)
                rows = pl.ds(pl.multiple_of(side * HALF, 16), HALF)
                inner, outer = dst.at[chunk, rows, :], ref.at[d]
                pair = (inner, outer) if outward else (outer, inner)
                copies.append(
                    pltpu.make_async_copy(pair[0], pair[1], sems.at[at_plane, 2 * d + which])
                )
    return copies


def fetch_plane(idx, refs, w, sems):
    plane, place, core, flip = idx[0], idx[1], idx[2], idx[3]
    for batch in range(3):
        copies = piece_copies(idx, [refs[batch]], w, False, sems, False)

        @pl.when(jnp.minimum(plane, 2) == batch)
        def _():
            for copy in copies:
                copy.start()

    turned = ((place & 1) << 1) | (place >> 1)
    spot = jnp.where(flip == 1, turned, place)
    target = w.at[4, pl.ds(ROWS, 16), :]
    for batch, (own, twin) in enumerate(refs):
        at = ROWS - HALF + (16 if batch == 2 else 0)
        for side, ref in ((1, own), (0, twin)):
            source = ref.at[spot, pl.ds(at, 16), :]
            right = (core == side) & (jnp.where(plane < 2, 1 - plane, 2) == batch)

            @pl.when(right)
            def _():
                pltpu.make_async_copy(source, target, sems.at[1, 0]).start()


def attention_kernel(
    idx, own0, own1, own2, twin0, twin1, twin2, tok_hbm, cos, sin,
    mixed_out, att_out, p_out, q_out, k_out, v_out, wq, wk, wv, wo, gain_out, gain_mid_out,
    w, tok, att, first, second, in_sem, sems,
):
    load = pltpu.make_async_copy(tok_hbm, tok, in_sem.at[0])
    load.start()
    fetch_plane(idx, [(own0, twin0), (own1, twin1), (own2, twin2)], w, sems)
    tokens = tok.shape[0]
    load.wait()
    x = tok[...].astype(F32)
    normed = x * lax.rsqrt(jnp.mean(x * x, -1, keepdims=True) + EPS)
    for j in range(8):
        pltpu.make_async_copy(own0.at[0], w.at[0, pl.ds(0, HALF), :], sems.at[0, j]).wait()
    pltpu.make_async_copy(
        own0.at[0, pl.ds(0, 16), :], w.at[4, pl.ds(ROWS, 16), :], sems.at[1, 0]
    ).wait()
    for c in range(4):
        add_tail(w, c, False)
    gains = w[0, ROWS : ROWS + 16, :].astype(F32)
    gain_in, gain_mid = row_of_head(gains, 0), row_of_head(gains, 1)
    gain_out[...], gain_mid_out[...] = gain_in, gain_mid
    n1 = (normed * gain_in).astype(BF16)
    wq[:NARROW, :] = load_narrow(w, 0)
    mixed_chunk = load_narrow(w, 1)
    wq[NARROW:, :] = mixed_chunk[:192]
    spread(mixed_chunk[192:], first, second, wk)
    mixed_chunk = load_narrow(w, 2)
    spread(mixed_chunk[:192], first, second, wv)
    wo[:192, :] = mixed_chunk[192:]
    wo[192:, :] = load_narrow(w, 3)

    query, keys, values = dot(n1, wq[...]), dot(n1, wk[...]), dot(n1, wv[...])
    row = lax.broadcasted_iota(jnp.int32, (3 * SEQ_LEN, SEQ_LEN), 0)
    causal = jnp.bitwise_and(row, SEQ_LEN - 1) >= lax.broadcasted_iota(
        jnp.int32, (3 * SEQ_LEN, SEQ_LEN), 1
    )
    for b in range(tokens // SEQ_LEN):
        part = slice(SEQ_LEN * b, SEQ_LEN * (b + 1))
        cosine, sine = cos[part, :], sin[part, :]
        for kv in range(KV_HEADS):
            at = KV_HEADS * b + kv
            heads = [
                turn(query[part, HEAD * h : HEAD * (h + 1)], cosine, sine)
                for h in range(3 * kv, 3 * kv + 3)
            ]
            q3 = jnp.concatenate(heads, 0).astype(BF16)
            k1 = turn(keys[part, HEAD * kv : HEAD * (kv + 1)], cosine, sine).astype(BF16)
            v1 = values[part, HEAD * kv : HEAD * (kv + 1)].astype(BF16)
            q_out[at], k_out[at], v_out[at] = q3, k1, v1
            score = jnp.where(causal, dot_nt(q3, k1) * HEAD**-0.5, -1e30)
            expon = jnp.exp(score - jnp.max(score, -1, keepdims=True))
            probs = expon / jnp.sum(expon, -1, keepdims=True)
            p_out[at] = probs
            mix = dot(probs.astype(BF16), v1)
            for r in range(3):
                h = 3 * kv + r
                att[part, HEAD * h : HEAD * (h + 1)] = mix[SEQ_LEN * r : SEQ_LEN * (r + 1)]
    attended = att[...].astype(BF16)
    att_out[...] = attended
    mixed_out[...] = x + dot(attended, wo[...])


def first_kernel(
    idx, own0, own1, own2, own3, twin0, twin1, twin2, twin3, mixed_in, gain_mid_in, cot_hbm,
    y_hbm, dr_out, dg_out, keep1, keep2, keep3, send1, send2, send3,
    w, g, cot, y_out, n2_ref, n2t_ref, y_acc, dn_acc, in_sem, sems, out_sems,
):
    load = pltpu.make_async_copy(cot_hbm, cot, in_sem.at[0])
    load.start()
    refs = [(own0, twin0), (own1, twin1), (own2, twin2), (own3, twin3)]
    loads = piece_copies(idx, refs, w, True, sems, False)
    for batch in range(4):

        @pl.when(plane_of(idx[0], batch) > 0)
        def _():
            for copy in loads[8 * batch : 8 * batch + 8]:
                copy.start()

    def arrived(plane):
        for j in range(8):
            pltpu.make_async_copy(
                own0.at[0], w.at[4 * plane, pl.ds(0, HALF), :], sems.at[plane, j]
            ).wait()

    mixed, gain_mid = mixed_in[...], gain_mid_in[...]
    inverse = lax.rsqrt(jnp.mean(mixed * mixed, -1, keepdims=True) + EPS)
    normed_mid = mixed * inverse
    n2 = normed_mid * gain_mid
    n2_ref[...] = n2.astype(BF16)
    n2t_ref[...] = n2.astype(BF16).astype(F32).T.astype(BF16)
    y_acc[...] = mixed
    dn_acc[...] = jnp.zeros_like(dn_acc)
    load.wait()
    arrived(1)
    arrived(2)
    arrived(3)

    def fix(i, carry):
        add_tail(w, i + 4, True)
        return carry

    lax.fori_loop(0, 8, fix, 0)
    for c in (12, 13, 14):
        add_tail(w, c, False)

    def block(k, carry):
        def wide(base, p):
            at = pl.multiple_of((3 * k + p) * WIDE, 16)
            return jnp.concatenate([w[base + d, pl.ds(at, WIDE), :] for d in range(4)], 0)

        w_gate = jnp.concatenate([wide(4, p) for p in range(3)], 1)
        w_up = jnp.concatenate([wide(8, p) for p in range(3)], 1)
        w_down = load_narrow(w, 12 + k)
        c = cot[...]
        gate, up = dot(n2_ref[...], w_gate), dot(n2_ref[...], w_up)
        sigma = 1.0 / (1.0 + jnp.exp(-gate))
        silu = gate * sigma
        hidden = (silu * up).astype(BF16)
        y_acc[...] += dot(hidden, w_down)
        store_narrow(g, 8 + k, dot_tn(hidden, c))
        d_hidden = dot_nt(c, w_down)
        d_gate = (d_hidden * up * sigma * (1.0 + gate * (1.0 - sigma))).astype(BF16)
        d_up = (d_hidden * silu).astype(BF16)
        dn_acc[...] += dot_nt(d_gate, w_gate) + dot_nt(d_up, w_up)
        for base, d_out in ((0, d_gate), (4, d_up)):
            grad = dot(n2t_ref[...], d_out).astype(BF16)
            for p in range(3):
                at = pl.multiple_of((3 * k + p) * WIDE, 16)
                for d in range(4):
                    g[base + d, pl.ds(at, WIDE), :] = grad[
                        WIDE * d : WIDE * (d + 1), 128 * p : 128 * (p + 1)
                    ]
        return carry

    lax.fori_loop(0, 4, block, 0)
    d_norm = dn_acc[...]
    d_gain = jnp.sum(d_norm * normed_mid, 0, keepdims=True)
    dg_out[...] = d_gain
    for c in range(12):
        top = tail_of(g, c - 1, c - 1 < 8) if c else jnp.zeros((16, 128), F32)
        g[c, ROWS : ROWS + 16, :] = top.astype(BF16)
        g[c, ROWS + 16 :, :] = gain_rows(d_gain, jnp.zeros((16, 128), F32)).astype(BF16)
    stores = piece_copies(
        idx, [(keep1, send1), (keep2, send2), (keep3, send3)], g, False, out_sems, True
    )
    for copy in stores:
        copy.start()
    y_out[...] = y_acc[...].astype(BF16)
    y_store = pltpu.make_async_copy(y_out, y_hbm, in_sem.at[0])
    y_store.start()
    scaled = d_norm * gain_mid
    dr_out[...] = cot[...].astype(F32) + inverse * (
        scaled - normed_mid * jnp.mean(scaled * normed_mid, -1, keepdims=True)
    )
    for copy in stores:
        copy.wait()
    y_store.wait()


def second_kernel(
    idx, tok, cos, sin, dr, att, p_in, q_in, k_in, v_in, wq, wk, wv, wo, gain, dg,
    dx_hbm, keep, send,
    g, dx_out, dq_ref, dk_ref, dv_ref, first, second, in_sem, out_sems,
):
    tokens = tok.shape[0]
    d_mixed = dr[...]
    branch = d_mixed.astype(BF16)
    dw_out = dot_tn(att[...], branch)
    d_att = dot_nt(branch, wo[...])
    for b in range(tokens // SEQ_LEN):
        part = slice(SEQ_LEN * b, SEQ_LEN * (b + 1))
        cosine, sine = cos[part, :], -sin[part, :]
        for kv in range(KV_HEADS):
            at = KV_HEADS * b + kv
            heads = [d_att[part, HEAD * h : HEAD * (h + 1)] for h in range(3 * kv, 3 * kv + 3)]
            d3 = jnp.concatenate(heads, 0).astype(BF16)
            probs, q3, k1, v1 = p_in[at], q_in[at], k_in[at], v_in[at]
            d_probs = dot_nt(d3, v1)
            dv_ref[part, HEAD * kv : HEAD * (kv + 1)] = dot_tn(probs.astype(BF16), d3)
            inner = jnp.sum(d_probs * probs, -1, keepdims=True)
            d_score = (probs * (d_probs - inner)).astype(BF16)
            dq3 = dot(d_score, k1) * HEAD**-0.5
            for r in range(3):
                h = 3 * kv + r
                dq_ref[part, HEAD * h : HEAD * (h + 1)] = turn(
                    dq3[SEQ_LEN * r : SEQ_LEN * (r + 1)], cosine, sine
                )
            dk_ref[part, HEAD * kv : HEAD * (kv + 1)] = turn(
                dot_tn(d_score, q3) * HEAD**-0.5, cosine, sine
            )
    dq, dk, dv = dq_ref[...].astype(BF16), dk_ref[...].astype(BF16), dv_ref[...].astype(BF16)
    x = tok[...].astype(F32)
    inverse = lax.rsqrt(jnp.mean(x * x, -1, keepdims=True) + EPS)
    normed = x * inverse
    n1t = (normed * gain[...]).astype(BF16).astype(F32).T.astype(BF16)
    dw_query = dot(n1t, dq)
    store_narrow(g, 0, dw_query[:NARROW])
    dw = unspread(dot(n1t, dk), first, second)
    store_narrow(g, 1, jnp.concatenate([dw_query[NARROW:], dw], 0))
    dw = unspread(dot(n1t, dv), first, second)
    store_narrow(g, 2, jnp.concatenate([dw, dw_out[:192]], 0))
    store_narrow(g, 3, dw_out[192:])
    d_norm = dot_nt(dq, wq[...]) + dot_nt(dk, wk[...]) + dot_nt(dv, wv[...])
    d_gain = jnp.sum(d_norm * normed, 0, keepdims=True)
    for c in range(4):
        top = tail_of(g, c - 1, False) if c else head_of_rows([d_gain, dg[...]])
        low = jnp.zeros((16, 128), F32) if c else tail_of(g, 3, False)
        g[c, ROWS : ROWS + 16, :] = top.astype(BF16)
        g[c, ROWS + 16 :, :] = gain_rows(dg[...], low).astype(BF16)
    stores = piece_copies(idx, [(keep, send)], g, False, out_sems, True)
    for copy in stores:
        copy.start()
    scaled = d_norm * gain[...]
    dx_out[...] = d_mixed + inverse * (
        scaled - normed * jnp.mean(scaled * normed, -1, keepdims=True)
    )
    dx_store = pltpu.make_async_copy(dx_out, dx_hbm, in_sem.at[0])
    dx_store.start()
    for copy in stores:
        copy.wait()
    dx_store.wait()


def halves_turned(low, high):
    lane = lax.broadcasted_iota(jnp.int32, low.shape, 1)
    return jnp.where(lane < 64, pltpu.roll(low, 64, 1), pltpu.roll(high, 64, 1))


def pack_kernel(idx, flat, out, rolled, window, packed, mixed):
    index, core, down, right = idx[0], idx[1], idx[2], idx[3]
    lane = lax.broadcasted_iota(jnp.int32, (1, 128), 1)
    rolled[0:16, :] = jnp.zeros((16, 128), F32)
    rolled[16:1752, :] = pltpu.roll(flat[...].astype(F32), right, 1)
    rolled[1752:1760, :] = jnp.zeros((8, 128), F32)
    window[...] = jnp.where(
        lane >= right, rolled[pl.ds(16 - down, 1744), :], rolled[pl.ds(15 - down, 1744), :]
    )
    head = [window[k : k + 1, :] for k in range(9)]
    wide = (index >= 4) & (index < 12)

    @pl.when(wide)
    def _():
        for j in range(12):
            packed[WIDE * j : WIDE * (j + 1), :] = window[pl.ds(9 + j, WIDE, stride=12), :]

    @pl.when(jnp.logical_not(wide))
    def _():
        parts = [window[pl.ds(9 + k, NARROW // 2, stride=9), :] for k in range(9)]
        for j in range(4):
            packed[pl.ds(NARROW * j, NARROW // 2, stride=2), :] = parts[j]
            packed[pl.ds(NARROW * j + 1, NARROW // 2, stride=2), :] = halves_turned(
                parts[4 + j], parts[5 + j]
            )
        mixed[pl.ds(0, NARROW // 2, stride=2), :] = parts[4]
        mixed[pl.ds(1, NARROW // 2, stride=2), :] = pltpu.roll(parts[8], 64, 1)
        packed[4 * NARROW : ROWS, :] = jnp.where(
            lane < 64, mixed[: NARROW // 2, :], pltpu.roll(mixed[NARROW // 2 :, :], 64, 1)
        )

    last = jnp.zeros((23, 128), F32)
    after_wide = (index >= 5) & (index < 13)

    @pl.when(after_wide)
    def _():
        packed[ROWS:, :] = jnp.concatenate(head + [last], 0)

    @pl.when(jnp.logical_not(after_wide))
    def _():
        rows = head[:4] + [halves_turned(head[4 + j], head[5 + j]) for j in range(4)]
        rows.append(jnp.where(lane < 64, 0.0, pltpu.roll(head[4], 64, 1)))
        rows.append(jnp.where(lane < 64, 0.0, head[8]))
        packed[ROWS:, :] = jnp.concatenate(rows + [last[:22]], 0)

    out[...] = packed[pl.ds(pl.multiple_of(core * HALF, 16), HALF), :].astype(BF16)


def unpack_kernel(idx, own, twin, out, packed, window, mixed):
    index, core, down, left = idx[0], idx[1], idx[2], idx[3]
    lane = lax.broadcasted_iota(jnp.int32, (1, 128), 1)
    packed[pl.ds(pl.multiple_of(core * HALF, 16), HALF), :] = own[...]
    packed[pl.ds(pl.multiple_of((1 - core) * HALF, 16), HALF), :] = twin[...]
    head = [packed[ROWS + k : ROWS + k + 1, :] for k in range(10)]
    window[1737:, :] = jnp.zeros((15, 128), F32)
    wide = (index >= 4) & (index < 12)

    @pl.when(wide)
    def _():
        for j in range(12):
            window[pl.ds(9 + j, WIDE, stride=12), :] = packed[WIDE * j : WIDE * (j + 1), :]

    @pl.when(jnp.logical_not(wide))
    def _():
        half = packed[4 * NARROW : ROWS, :]
        mixed[: NARROW // 2, :] = half
        mixed[NARROW // 2 :, :] = pltpu.roll(half, 64, 1)
        odd = []
        for j in range(4):
            window[pl.ds(9 + j, NARROW // 2, stride=9), :] = packed[
                pl.ds(NARROW * j, NARROW // 2, stride=2), :
            ]
            odd.append(pltpu.roll(packed[pl.ds(NARROW * j + 1, NARROW // 2, stride=2), :], 64, 1))
        odd.append(mixed[pl.ds(1, NARROW // 2, stride=2), :])
        before = mixed[pl.ds(0, NARROW // 2, stride=2), :]
        for j in range(4):
            window[pl.ds(13 + j, NARROW // 2, stride=9), :] = jnp.where(lane < 64, before, odd[j])
            before = odd[j]
        window[pl.ds(17, NARROW // 2, stride=9), :] = jnp.where(
            lane < 64, before, pltpu.roll(odd[4], 64, 1)
        )

    after_wide = (index >= 5) & (index < 13)

    @pl.when(after_wide)
    def _():
        window[0:9, :] = jnp.concatenate(head[:9], 0)

    @pl.when(jnp.logical_not(after_wide))
    def _():
        odd = [pltpu.roll(row, 64, 1) for row in head[4:8]]
        before, rows = pltpu.roll(head[8], 64, 1), head[:4]
        for j in range(4):
            rows.append(jnp.where(lane < 64, before, odd[j]))
            before = odd[j]
        rows.append(jnp.where(lane < 64, before, head[9]))
        window[0:9, :] = jnp.concatenate(rows, 0)

    lanes = pltpu.roll(window[...], jnp.bitwise_and(128 - left, 127), 1)
    window[...] = lanes
    out[...] = jnp.where(
        lane < 128 - left, window[pl.ds(down, 1736), :], window[pl.ds(down + 1, 1736), :]
    )


def chunk_index(index, core, lay):
    start = index * lay.step
    return jnp.stack([index, core, start // 128, start % 128]).astype(jnp.int32)


def pack_own(params, index, core, lay):
    if lay.count != CANON:
        window = jnp.zeros((lay.gains + lay.chunk,), params.dtype)
        window = lax.dynamic_update_slice(window, params, (index * lay.step,))
        payload = pack_payload(window, index, lay)
        return lax.dynamic_slice_in_dim(payload, core * lay.half, lay.half, 0)
    flat = jnp.pad(params, (0, 1736 * 128 - lay.shard)).reshape(1736, 128)
    vmem = pl.BlockSpec(memory_space=pltpu.VMEM)
    return pl.pallas_call(
        pack_kernel,
        name="pack_own_chunk",
        in_specs=[pl.BlockSpec(memory_space=pltpu.SMEM), vmem],
        out_specs=vmem,
        out_shape=jax.ShapeDtypeStruct((HALF, 128), BF16),
        scratch_shapes=[
            pltpu.VMEM((1760, 128), F32),
            pltpu.VMEM((1744, 128), F32),
            pltpu.VMEM((2 * HALF, 128), F32),
            pltpu.VMEM((NARROW, 128), F32),
        ],
        compiler_params=pltpu.CompilerParams(vmem_limit_bytes=VMEM_LIMIT),
    )(chunk_index(index, core, lay), flat)


def unpack_own(own, twin, index, core, lay):
    if lay.count != CANON:
        rows = jnp.where(core == 0, jnp.stack([own, twin], 0), jnp.stack([twin, own], 0))
        window = unpack_payload(rows.reshape(2 * lay.half, 128), index, lay)
        return lax.dynamic_slice(window, (index * lay.step,), (lay.shard,))
    vmem = pl.BlockSpec(memory_space=pltpu.VMEM)
    rows = pl.pallas_call(
        unpack_kernel,
        name="unpack_own_chunk",
        in_specs=[pl.BlockSpec(memory_space=pltpu.SMEM), vmem, vmem],
        out_specs=vmem,
        out_shape=jax.ShapeDtypeStruct((1736, 128), F32),
        scratch_shapes=[
            pltpu.VMEM((2 * HALF, 128), F32),
            pltpu.VMEM((1752, 128), F32),
            pltpu.VMEM((NARROW, 128), F32),
        ],
        compiler_params=pltpu.CompilerParams(vmem_limit_bytes=VMEM_LIMIT),
    )(chunk_index(index, core, lay), own, twin)
    return rows.reshape(-1)[: lay.shard]


def tables(positions):
    cosine, sine = rope_tables(positions)
    return jnp.concatenate([cosine, cosine], 1), jnp.concatenate([-sine, sine], 1)


def run_layer(idx, own, twin, tokens, cotangent, cosine, sine):
    length, width = tokens.shape
    groups = length // SEQ_LEN * KV_HEADS
    kv_width = KV_HEADS * HEAD
    smem = pl.BlockSpec(memory_space=pltpu.SMEM)
    vmem = pl.BlockSpec(memory_space=pltpu.VMEM)
    hbm = pl.BlockSpec(memory_space=pltpu.HBM)
    anywhere = pl.BlockSpec(memory_space=pl.ANY)
    params = pltpu.CompilerParams(vmem_limit_bytes=VMEM_LIMIT)

    def sds(shape, dtype):
        return jax.ShapeDtypeStruct(shape, dtype)

    def cost(flops):
        return pl.CostEstimate(flops=flops, bytes_accessed=8_000_000, transcendentals=600_000)

    piece = sds((4, HALF, 128), BF16)
    weights = [sds((width, width), BF16), sds((width, kv_width), BF16)]
    weights = weights + [weights[1], weights[0]]
    saved = [
        sds((groups, 3 * SEQ_LEN, SEQ_LEN), F32),
        sds((groups, 3 * SEQ_LEN, HEAD), BF16),
        sds((groups, SEQ_LEN, HEAD), BF16),
        sds((groups, SEQ_LEN, HEAD), BF16),
    ]
    rows = sds((length, width), F32)
    low_rows = sds((length, width), BF16)
    outs = [rows, low_rows] + saved + weights + [sds((1, width), F32)] * 2
    results = pl.pallas_call(
        attention_kernel,
        name="attention_forward",
        in_specs=[smem] + [anywhere] * 6 + [hbm] + [vmem] * 2,
        out_specs=[vmem] * len(outs),
        out_shape=outs,
        scratch_shapes=[
            pltpu.VMEM((5, 2 * HALF, 128), BF16),
            pltpu.VMEM((length, width), BF16),
            pltpu.VMEM((length, width), F32),
            pltpu.VMEM((width, 128), F32),
            pltpu.VMEM((width, 128), F32),
            pltpu.SemaphoreType.DMA((1,)),
            pltpu.SemaphoreType.DMA((2, 8)),
        ],
        compiler_params=params,
        cost_estimate=cost(10 * length * width * width),
    )(idx, *own[:3], *twin[:3], tokens, cosine, sine)
    mixed, attended, probs, q3, k1, v1, wq, wk, wv, wo, gain, gain_mid = results
    results = pl.pallas_call(
        first_kernel,
        name="feed_forward",
        in_specs=[smem] + [anywhere] * 8 + [vmem] * 2 + [hbm],
        out_specs=[hbm] + [vmem] * 2 + [anywhere] * 6,
        out_shape=[low_rows, rows, sds((1, width), F32)] + [piece] * 6,
        scratch_shapes=[
            pltpu.VMEM((CANON, 2 * HALF, 128), BF16),
            pltpu.VMEM((12, 2 * HALF, 128), BF16),
            pltpu.VMEM((length, width), BF16),
            pltpu.VMEM((length, width), BF16),
            pltpu.VMEM((length, width), BF16),
            pltpu.VMEM((width, length), BF16),
            pltpu.VMEM((length, width), F32),
            pltpu.VMEM((length, width), F32),
            pltpu.SemaphoreType.DMA((1,)),
            pltpu.SemaphoreType.DMA((4, 8)),
            pltpu.SemaphoreType.DMA((3, 8)),
        ],
        compiler_params=params,
        cost_estimate=cost(18 * length * width * FF),
    )(idx, *own, *twin, mixed, gain_mid, cotangent)
    output, d_mixed, d_gain = results[:3]
    keeps, sends = list(results[3:6]), list(results[6:9])
    d_input, keep, send = pl.pallas_call(
        second_kernel,
        name="attention_backward",
        in_specs=[smem] + [vmem] * 15,
        out_specs=[hbm] + [anywhere] * 2,
        out_shape=[rows, piece, piece],
        scratch_shapes=[
            pltpu.VMEM((4, 2 * HALF, 128), BF16),
            pltpu.VMEM((length, width), F32),
            pltpu.VMEM((length, width), F32),
            pltpu.VMEM((length, kv_width), F32),
            pltpu.VMEM((length, kv_width), F32),
            pltpu.VMEM((width, 128), F32),
            pltpu.VMEM((width, 128), F32),
            pltpu.SemaphoreType.DMA((1,)),
            pltpu.SemaphoreType.DMA((1, 8)),
        ],
        compiler_params=params,
        cost_estimate=cost(10 * length * width * width),
    )(idx, tokens, cosine, sine, d_mixed, attended, probs, q3, k1, v1, wq, wk, wv, wo, gain, d_gain)
    return output, d_input, d_gain[0], [keep] + keeps, [send] + sends


def flat_of(payloads, lay):
    n = lay.count
    heads = payloads[:, lay.rows : lay.rows + 10]
    flats = [unhead_narrow(heads[0])]
    for i in range(n):
        wide = n // 4 <= i < 3 * n // 4
        body = payloads[i, : lay.rows]
        flat = unpack_wide(body, FF) if wide else unpack_narrow(body)
        if i + 1 < n:
            tail = unhead_wide(heads[i + 1]) if wide else unhead_narrow(heads[i + 1])
            flat = jnp.concatenate([flat[: -lay.gains], flat[-lay.gains :] + tail])
        flats.append(flat)
    return jnp.concatenate(flats)


def payloads_of(flat, lay):
    windows = [
        flat[i * lay.chunk : (i + 1) * lay.chunk + lay.gains] for i in range(lay.count)
    ]
    return jnp.stack([pack_payload(window, i, lay) for i, window in enumerate(windows)], 0)


def batch_order(lay, index):
    plane, place = index // lay.in_plane, index % lay.in_plane
    planes = jnp.stack([plane_of(plane, batch) for batch in range(PLANES)])
    batch = jnp.argsort(planes).astype(jnp.int32)
    spots = jnp.arange(lay.in_plane, dtype=jnp.int32) ^ place
    return (batch[:, None] * lay.in_plane + spots[None, :]).reshape(-1)


def canonical(own, twin, lay, canon, index, core):
    own, twin = jnp.stack(own, 0), jnp.stack(twin, 0)
    both = jnp.where(core == 0, jnp.stack([own, twin], 2), jnp.stack([twin, own], 2))
    both = both.reshape(lay.count, 2 * lay.half, 128)
    both = jnp.take(both, batch_order(lay, index), axis=0)
    flat = flat_of(both, lay)
    zeros = jnp.zeros((canon.gains,), flat.dtype)
    rows = []
    for i in range(CANON):
        window = flat[i * canon.chunk : (i + 1) * canon.chunk + canon.gains]
        if i:
            window = jnp.concatenate([zeros, window[canon.gains :]])
        rows.append(pack_payload(window, i, canon))
    rows = jnp.stack(rows, 0).reshape(PLANES, 4, 2, canon.half, 128)
    return [list(rows[:, :, c]) for c in range(2)]


def from_canonical(keeps, sends, lay, canon, place, core):
    rows = jnp.stack([jnp.stack(keeps, 0), jnp.stack(sends, 0)], 2)
    rows = rows.reshape(CANON, 2 * canon.half, 128)
    flats = [unhead_narrow(rows[0, canon.rows : canon.rows + 10])]
    for i in range(CANON):
        body = rows[i, : canon.rows]
        flats.append(unpack_wide(body, FF) if 4 <= i < 12 else unpack_narrow(body))
    rows = payloads_of(jnp.concatenate(flats), lay)
    rows = rows.reshape(PLANES, lay.in_plane, 2, lay.half, 128)
    rows = jnp.take(rows, jnp.arange(lay.in_plane, dtype=jnp.int32) ^ place, axis=1)
    return list(jnp.take(rows, core, axis=2)), list(jnp.take(rows, 1 - core, axis=2))


def on_device(lay, canon, tokens_in, positions, params, cotangent):
    index = lax.axis_index("dp")
    core = lax.axis_index("rep")
    n, half, in_plane = lay.count, lay.half, lay.in_plane
    plane, place = index // in_plane, index % in_plane
    same = n == CANON
    mine = pack_own(params, index, core, lay)
    own, twin, beside = gather(mine, plane, core, lay, tables(positions))
    if same:
        idx = jnp.stack([plane, place, core, 1]).astype(jnp.int32)
    else:
        own, twin = canonical(own, twin, lay, canon, index, core)
        idx = jnp.zeros((4,), jnp.int32)
    output, d_input, d_gain, keeps, sends = run_layer(
        idx, own, twin, tokens_in, cotangent, *beside
    )
    if not same:
        keeps, sends = from_canonical(keeps, sends, lay, canon, place, core)
    planes = []
    for keep, send in zip(keeps, sends):
        pair = keep.astype(F32) + swap_rep(send).astype(F32)
        planes.append(reduce_plane(pair.astype(BF16), lay))
    if same:
        at = ROWS - HALF
        row = jnp.arange(16)[:, None]
        late = jnp.where((core == 1) & (row < 10), planes[0][at + 16 : at + 32], jnp.zeros((16, 128), BF16))
        planes[1] = jnp.concatenate([planes[1][:at], planes[1][at : at + 16] + late, planes[1][at + 16 :]])
    planes = jnp.stack(planes, 0)
    parts = [jnp.take(planes, plane, axis=0).astype(F32)]
    for s in range(1, PLANES):
        part = swap(jnp.take(planes, plane ^ s, axis=0), s << (lay.bits - 2), n)
        parts.append(part.astype(F32))
    total = (parts[0] + parts[1]) + (parts[2] + parts[3])
    other = swap_rep(total)
    if same:
        at = ROWS + 26 - HALF
        d_gain = jnp.where(core == 1, total[at : at + 5], other[at : at + 5]).reshape(-1)[: lay.width]
    else:
        d_gain = sum_everywhere(d_gain, lay)
    return output, d_input, unpack_own(total, other, index, core, lay), d_gain


def solution(mesh):
    def run(tokens_in, positions, params, cotangent):
        total, width = params.shape[0], tokens_in.shape[1]
        lay = Layout(mesh.shape["dp"], total, width)
        canon = Layout(CANON, total, width)
        rows = P(("dp", "rep"), None)
        return jax.shard_map(
            lambda *args: on_device(lay, canon, *args),
            mesh=mesh,
            in_specs=(rows, P(("dp", "rep")), P("dp"), rows),
            out_specs=(rows, rows, P("dp"), P()),
            check_vma=False,
        )(tokens_in, positions, params, cotangent)

    return run
```

```python
import jax
import jax.numpy as jnp
from jax import lax
from jax.experimental import pallas as pl
from jax.experimental.pallas import tpu as pltpu
from jax.sharding import PartitionSpec as P

HEADS = 9
KV_HEADS = 3
HEAD = 64
FF = 1536
SEQ_LEN = 128
PLANES = 4
CANON = 16

EPS = 1e-05
ROPE_BASE = 100000.0

F32, BF16 = jnp.float32, jnp.bfloat16
ROWS, HALF = 1728, 880
MAIN, REST = 768, 112
NARROW, WIDE = 384, 144
VMEM_LIMIT = 52 * 1024 * 1024


class Layout:
    def __init__(self, count, total, width):
        self.count = count
        self.width = width
        self.gains = 2 * width
        self.shard = total // count
        self.chunk = (total - self.gains) // count
        self.step = self.gains // count
        self.rows = self.chunk // 128
        half = -(-(self.rows + 10) // 2)
        self.half = -(-half // 16) * 16
        self.first = -(-(self.half // 2) // 16) * 16
        self.extra = 2 * self.half - self.rows
        self.bits = count.bit_length() - 1
        rest = self.bits - 2
        self.x_bits = -(-rest // 2)
        self.y_bits = rest - self.x_bits
        self.in_plane = 1 << rest
        self.flip = self.x_bits == self.y_bits


def pack_wide(flat, width):
    panels = width // 128
    return flat.reshape(-1, panels, 128).transpose(1, 0, 2).reshape(-1, 128)


def unpack_wide(rows, width):
    panels = width // 128
    return rows.reshape(panels, -1, 128).transpose(1, 0, 2).reshape(-1)


def pack_narrow(flat):
    rows = flat.reshape(-1, 576)
    count = rows.shape[0]
    panels = rows[:, :512].reshape(count, 4, 128).transpose(1, 0, 2).reshape(-1, 128)
    tail = rows[:, 512:]
    return jnp.concatenate([panels, jnp.concatenate([tail[: count // 2], tail[count // 2 :]], 1)], 0)


def unpack_narrow(packed):
    count = packed.shape[0] * 2 // 9
    panels = packed[: 4 * count].reshape(4, count, 128).transpose(1, 0, 2).reshape(count, 512)
    half = packed[4 * count :]
    tail = jnp.concatenate([half[:, :64], half[:, 64:]], 0)
    return jnp.concatenate([panels, tail], 1).reshape(-1)


def head_narrow(flat):
    rows = flat.reshape(2, 576)
    tail = jnp.pad(rows[:, 512:], ((0, 0), (64, 0)))
    return jnp.concatenate([rows[:, :512].reshape(8, 128), tail], 0)


def unhead_narrow(rows):
    return jnp.concatenate([rows[:8].reshape(2, 512), rows[8:10, 64:]], 1).reshape(-1)


def head_wide(flat):
    return jnp.pad(flat.reshape(9, 128), ((0, 1), (0, 0)))


def unhead_wide(rows):
    return rows[:9].reshape(-1)


def is_wide(index, count):
    return (index >= count // 4) & (index < 3 * count // 4)


def pack_payload(window, index, lay):
    head, chunk = window[: lay.gains], window[lay.gains :]
    body = jnp.where(is_wide(index, lay.count), pack_wide(chunk, FF), pack_narrow(chunk))
    top = jnp.where(is_wide(index - 1, lay.count), head_wide(head), head_narrow(head))
    return jnp.concatenate([body, jnp.pad(top, ((0, lay.extra - 10), (0, 0)))], 0)


def unpack_payload(rows, index, lay):
    body, top = rows[: lay.rows], rows[lay.rows : lay.rows + 10]
    chunk = jnp.where(is_wide(index, lay.count), unpack_wide(body, FF), unpack_narrow(body))
    head = jnp.where(is_wide(index - 1, lay.count), unhead_wide(top), unhead_narrow(top))
    return jnp.concatenate([head, chunk])


def swap(value, mask, count):
    return lax.ppermute(value, "dp", [(i, i ^ mask) for i in range(count)])


def swap_rep(value):
    return lax.ppermute(value, "rep", [(0, 1), (1, 0)])


def hop(value, masks, count):
    pairs = [(2 * i + c, 2 * (i ^ masks[c]) + c) for i in range(count) for c in range(2)]
    return lax.ppermute(value, ("dp", "rep"), pairs)


def hops(lay):
    xs = [d for d in range(1, 1 << lay.x_bits)]
    ys = [e << lay.x_bits for e in range(1, 1 << lay.y_bits)]
    if lay.flip:
        return list(zip(xs, ys)), list(zip(ys, xs))
    return list(zip(xs, xs)), list(zip(ys, ys))


def gather_hops(value, masks, count):
    return jnp.stack([value] + [hop(value, pair, count) for pair in masks], 0)


def gather(half, lay):
    n = lay.count
    first, second = hops(lay)
    planes = [half] + [swap(half, s << (lay.bits - 2), n) for s in range(1, PLANES)]
    blocks = []
    for plane in planes:
        block = gather_hops(plane, first, n)
        blocks.append([block] + [hop(block, masks, n) for masks in second])
    return blocks


def balanced_gather(half, lay, beside):
    n = lay.count
    (first,), (second,) = hops(lay)
    both = tuple(a ^ b for a, b in zip(first, second))
    across = [swap(half, s << (lay.bits - 2), n) for s in range(1, PLANES)]
    plane = [hop(half, masks, n) for masks in (first, second, both)]
    across, plane, beside = lax.optimization_barrier((across, plane, beside))
    own = jnp.stack([half] + plane, 0)
    near = [jnp.stack([value, hop(value, first, n)], 0) for value in across]
    far = [hop(value, second, n) for value in near]
    early = [own] + near
    far, twins = lax.optimization_barrier((far, [swap_rep(value) for value in early]))
    return early + far + twins + [swap_rep(value) for value in far], beside


def pair_sum(keep, send):
    return [
        (mine.astype(F32) + swap_rep(other).astype(F32)).astype(BF16)
        for mine, other in zip(keep, send)
    ]


def send_blocks(blocks, masks, count):
    return [hop(block, pair, count) for block, pair in zip(blocks[1:], masks)]


def add_blocks(block, arrived):
    total = block.astype(F32)
    for value in arrived:
        total = total + value.astype(F32)
    return total.astype(BF16)


def split_first(planes, lay):
    return [jnp.stack([value[j] for value in planes], 0) for j in range(len(hops(lay)[0]) + 1)]


def reduce_planes(planes, plane, lay):
    parts = [jnp.take(planes, plane, axis=0).astype(F32)]
    for s in range(1, PLANES):
        part = swap(jnp.take(planes, plane ^ s, axis=0), s << (lay.bits - 2), lay.count)
        parts.append(part.astype(F32))
    return (parts[0] + parts[1]) + (parts[2] + parts[3])


def sum_everywhere(value, lay):
    value = value + swap_rep(value)
    for bit in range(lay.bits):
        value = value + swap(value, 1 << bit, lay.count)
    return value


def rope_tables(places):
    expon = jnp.arange(HEAD // 2).astype(jnp.float32) * (2.0 / HEAD)
    inverse = jnp.power(ROPE_BASE, -expon)
    angle = places.astype(jnp.float32)[..., None] * inverse
    return (jnp.cos(angle), jnp.sin(angle))


def dot(left, right):
    return jnp.dot(left, right, preferred_element_type=F32)


def dot_nt(left, right):
    return lax.dot_general(left, right, (((1,), (1,)), ((), ())), preferred_element_type=F32)


def dot_tn(left, right):
    return dot(left.astype(F32).T.astype(BF16), right)


def row_of_head(head, which):
    parts = [head[4 * which + j : 4 * which + j + 1] for j in range(4)]
    return jnp.concatenate(parts + [head[8 + which : 9 + which, 64:]], 1)


def head_of_rows(rows):
    parts = [row[:, 128 * j : 128 * j + 128] for row in rows for j in range(4)]
    zeros = jnp.zeros((1, 64), F32)
    parts = parts + [jnp.concatenate([zeros, row[:, 512:]], 1) for row in rows]
    return jnp.concatenate(parts + [jnp.zeros((6, 128), F32)], 0)


def gain_rows(gain, low):
    parts = [gain[:, 128 * j : 128 * j + 128] for j in range(4)]
    parts = parts + [jnp.concatenate([gain[:, 512:], gain[:, 512:]], 1)]
    return jnp.concatenate([low[:10]] + parts + [jnp.zeros((1, 128), F32)], 0)


def load_narrow(ref, index):
    parts = [ref[index, NARROW * j : NARROW * (j + 1), :] for j in range(4)]
    half = ref[index, 4 * NARROW : ROWS, :]
    tail = jnp.concatenate([half[:, :64], half[:, 64:]], 0)
    return jnp.concatenate(parts + [tail], 1)


def store_narrow(ref, index, value):
    for j in range(4):
        ref[index, NARROW * j : NARROW * (j + 1), :] = value[:, 128 * j : 128 * (j + 1)].astype(BF16)
    tail = value[:, 512:]
    tail = jnp.concatenate([tail[: NARROW // 2], tail[NARROW // 2 :]], 1)
    ref[index, 4 * NARROW : ROWS, :] = tail.astype(BF16)


def narrow_tiles():
    tiles = [(NARROW * (j + 1) - 16, j, 4 + j) for j in range(4)]
    return tiles + [(ROWS - 16, 8, 9)]


def add_tail(ref, index, wide):
    head = ref[index + 1, ROWS : ROWS + 16, :].astype(F32)
    row = lax.broadcasted_iota(jnp.int32, (16, 128), 0)
    if wide:
        for k in range(9):
            at = WIDE * (4 + k) - 16
            tile = ref[index, at : at + 16, :].astype(F32)
            tile = tile + jnp.where(row == 15, head[k : k + 1], 0.0)
            ref[index, at : at + 16, :] = tile.astype(BF16)
    else:
        for at, upper, lower in narrow_tiles():
            tile = ref[index, at : at + 16, :].astype(F32)
            tile = tile + jnp.where(row == 14, head[upper : upper + 1], 0.0)
            tile = tile + jnp.where(row == 15, head[lower : lower + 1], 0.0)
            ref[index, at : at + 16, :] = tile.astype(BF16)


def tail_of(ref, index, wide):
    if wide:
        parts = []
        for k in range(9):
            at = WIDE * (4 + k) - 16
            parts.append(ref[index, at : at + 16, :].astype(F32)[15:16])
        return jnp.concatenate(parts + [jnp.zeros((7, 128), F32)], 0)
    tiles = [ref[index, at : at + 16, :].astype(F32) for at, _, _ in narrow_tiles()]
    parts = [tile[14:15] for tile in tiles[:4]] + [tile[15:16] for tile in tiles[:4]]
    parts = parts + [tiles[4][14:15], tiles[4][15:16]]
    return jnp.concatenate(parts + [jnp.zeros((6, 128), F32)], 0)


def spread(value, first, second, out):
    for m in range(3):
        part = value[:, 192 * m : 192 * (m + 1)].astype(F32)
        first[pl.ds(m, 192, stride=3), :] = part[:, :128]
        second[pl.ds(m, 192, stride=3), :] = jnp.concatenate([part[:, 128:], part[:, 128:]], 1)
    out[:, :128] = first[...].astype(BF16)
    out[:, 128:] = second[:, :64].astype(BF16)


def unspread(value, first, second):
    first[...] = value[:, :128]
    second[...] = jnp.concatenate([value[:, 128:], value[:, 128:]], 1)
    parts = []
    for m in range(3):
        parts.append(first[pl.ds(m, 192, stride=3), :])
        parts.append(second[pl.ds(m, 192, stride=3), :][:, :64])
    return jnp.concatenate(parts, 1)


def turn(vector, cosine, sine):
    swapped = jnp.concatenate([vector[:, 32:], vector[:, :32]], 1)
    return vector * cosine + swapped * sine


def piece_copies(idx, at_plane, sides, dst, sem, outward):
    place, core, flip = idx[1], idx[2], idx[3]
    copies = []
    for which, refs in enumerate(sides):
        side = jnp.bitwise_xor(core, which)
        for d in range(4):
            turned = ((d & 1) << 1) | (d >> 1)
            chunk = 4 * at_plane + jnp.bitwise_xor(place, jnp.where(side * flip == 1, turned, d))
            if len(refs) == 1:
                parts = [(refs[0].at[d, pl.ds(at, size), :], at, size) for at, size in ((0, MAIN), (MAIN, REST))]
            else:
                parts = [(refs[d // 2].at[d % 2], 0, HALF)]
            for outer, start, rows in parts:
                at = pl.multiple_of(side * HALF + start, 16)
                inner = dst.at[chunk, pl.ds(at, rows), :]
                pair = (inner, outer) if outward else (outer, inner)
                copies.append((start > 0, pltpu.make_async_copy(pair[0], pair[1], sem)))
    return copies


def wait_plane(ref, base, sem):
    whole = ref.at[pl.ds(base, 4)]
    pltpu.make_async_copy(whole, whole, sem).wait()


def slot_plane(plane, slot):
    own = jnp.where(plane == 0, 3, plane)
    low = jnp.where(own == 1, 2, 1)
    return [low, 6 - own - low, own][slot]


def first_kernel(idx, *refs):
    pieces = list(zip(refs[:7], refs[7:14]))
    tok_hbm, cos, sin, cot_hbm = refs[14:18]
    refs = refs[18:]
    results, outs = refs[:13], refs[13:19]
    y_acc, dr_out, dg_out, att_out, p_out, q_out, k_out, v_out, wq, wk, wv, wo, gain_out = refs[19:32]
    w, g, tok, cot_t, cot, att, n2_ref, n2t_ref, dn_acc, first, second = refs[32:43]
    in_sem, sems, out_sems, result_sems = refs[43:]
    saves = [
        pltpu.make_async_copy(src, dst, result_sems.at[i])
        for i, (src, dst) in enumerate(zip(refs[19:32], results))
    ]
    load = pltpu.make_async_copy(tok_hbm, tok, in_sem.at[0])
    load.start()
    load_cot = pltpu.make_async_copy(cot_hbm, cot_t, in_sem.at[1])
    load_cot.start()
    for s in range(PLANES):
        sides = [[ref] for ref in pieces[0]]
        if s:
            sides = list(zip(pieces[s], pieces[s + 3]))
        at_plane = jnp.bitwise_xor(idx[0], s)
        for _, copy in piece_copies(idx, at_plane, sides, w, sems.at[at_plane], False):
            copy.start()
    tokens = tok.shape[1]
    load.wait()
    x = tok[...].astype(F32).T
    normed = x * lax.rsqrt(jnp.mean(x * x, -1, keepdims=True) + EPS)
    load_cot.wait()
    cot[...] = cot_t[...].astype(F32).T.astype(BF16)
    wait_plane(w, 0, sems.at[0])
    for c in range(3):
        add_tail(w, c, False)
    wait_plane(w, 4, sems.at[1])
    add_tail(w, 3, False)
    gains = w[0, ROWS : ROWS + 16, :].astype(F32)
    gain_in, gain_mid = row_of_head(gains, 0), row_of_head(gains, 1)
    gain_out[...] = gain_in
    n1 = (normed * gain_in).astype(BF16)
    wq[:NARROW, :] = load_narrow(w, 0)
    mixed_chunk = load_narrow(w, 1)
    wq[NARROW:, :] = mixed_chunk[:192]
    spread(mixed_chunk[192:], first, second, wk)
    mixed_chunk = load_narrow(w, 2)
    spread(mixed_chunk[:192], first, second, wv)
    wo[:192, :] = mixed_chunk[192:]
    wo[192:, :] = load_narrow(w, 3)

    query, keys, values = dot(n1, wq[...]), dot(n1, wk[...]), dot(n1, wv[...])
    row = lax.broadcasted_iota(jnp.int32, (3 * SEQ_LEN, SEQ_LEN), 0)
    causal = jnp.bitwise_and(row, SEQ_LEN - 1) >= lax.broadcasted_iota(
        jnp.int32, (3 * SEQ_LEN, SEQ_LEN), 1
    )
    for b in range(tokens // SEQ_LEN):
        part = slice(SEQ_LEN * b, SEQ_LEN * (b + 1))
        cosine, sine = cos[part, :], sin[part, :]
        for kv in range(KV_HEADS):
            at = KV_HEADS * b + kv
            heads = [
                turn(query[part, HEAD * h : HEAD * (h + 1)], cosine, sine)
                for h in range(3 * kv, 3 * kv + 3)
            ]
            q3 = jnp.concatenate(heads, 0).astype(BF16)
            k1 = turn(keys[part, HEAD * kv : HEAD * (kv + 1)], cosine, sine).astype(BF16)
            v1 = values[part, HEAD * kv : HEAD * (kv + 1)].astype(BF16)
            q_out[at], k_out[at], v_out[at] = q3, k1, v1
            score = jnp.where(causal, dot_nt(q3, k1) * HEAD**-0.5, -1e30)
            expon = jnp.exp(score - jnp.max(score, -1, keepdims=True))
            probs = expon / jnp.sum(expon, -1, keepdims=True)
            p_out[at] = probs
            mix = dot(probs.astype(BF16), v1)
            for r in range(3):
                h = 3 * kv + r
                att[part, HEAD * h : HEAD * (h + 1)] = mix[SEQ_LEN * r : SEQ_LEN * (r + 1)]
    attended = att[...].astype(BF16)
    att_out[...] = attended
    for copy in saves[3:]:
        copy.start()
    mixed = x + dot(attended, wo[...])
    inverse = lax.rsqrt(jnp.mean(mixed * mixed, -1, keepdims=True) + EPS)
    normed_mid = mixed * inverse
    n2 = normed_mid * gain_mid
    n2_ref[...] = n2.astype(BF16)
    n2t_ref[...] = n2.astype(BF16).astype(F32).T.astype(BF16)
    y_acc[...] = mixed
    dn_acc[...] = jnp.zeros_like(dn_acc)
    wait_plane(w, 8, sems.at[2])
    wait_plane(w, 12, sems.at[3])

    def fix(i, carry):
        add_tail(w, i + 4, True)
        return carry

    lax.fori_loop(0, 8, fix, 0)
    for c in (12, 13, 14):
        add_tail(w, c, False)

    def block(k, carry):
        def wide(base, p):
            at = pl.multiple_of((6 * k + p) * WIDE, 16)
            return jnp.concatenate([w[base + d, pl.ds(at, WIDE), :] for d in range(4)], 0)

        w_gate = jnp.concatenate([wide(4, p) for p in range(6)], 1)
        w_up = jnp.concatenate([wide(8, p) for p in range(6)], 1)
        w_down = jnp.concatenate([load_narrow(w, 12 + 2 * k), load_narrow(w, 13 + 2 * k)], 0)
        c = cot[...]
        gate, up = dot(n2_ref[...], w_gate), dot(n2_ref[...], w_up)
        sigma = 1.0 / (1.0 + jnp.exp(-gate))
        silu = gate * sigma
        hidden = (silu * up).astype(BF16)
        y_acc[...] += dot(hidden, w_down)
        d_down = dot_tn(hidden, c)
        store_narrow(g, 8 + 2 * k, d_down[:NARROW])
        store_narrow(g, 9 + 2 * k, d_down[NARROW:])
        d_hidden = dot_nt(c, w_down)
        d_gate = (d_hidden * up * sigma * (1.0 + gate * (1.0 - sigma))).astype(BF16)
        d_up = (d_hidden * silu).astype(BF16)
        dn_acc[...] += dot_nt(d_gate, w_gate) + dot_nt(d_up, w_up)
        for base, d_out in ((0, d_gate), (4, d_up)):
            grad = dot(n2t_ref[...], d_out).astype(BF16)
            for p in range(6):
                at = pl.multiple_of((6 * k + p) * WIDE, 16)
                for d in range(4):
                    g[base + d, pl.ds(at, WIDE), :] = grad[
                        WIDE * d : WIDE * (d + 1), 128 * p : 128 * (p + 1)
                    ]
        return carry

    lax.fori_loop(0, 2, block, 0)
    stores = []
    for slot in range(3):
        sides = [[ref] for ref in outs[2 * slot : 2 * slot + 2]]
        at_plane = slot_plane(idx[0], slot) - 1
        stores = stores + piece_copies(idx, at_plane, sides, g, out_sems.at[slot], True)
    for last, copy in stores:
        if not last:
            copy.start()
    d_norm = dn_acc[...]
    d_gain = jnp.sum(d_norm * normed_mid, 0, keepdims=True)
    dg_out[...] = d_gain
    scaled = d_norm * gain_mid
    d_mixed = cot[...].astype(F32) + inverse * (
        scaled - normed_mid * jnp.mean(scaled * normed_mid, -1, keepdims=True)
    )
    last_rows = dot_tn(att_out[:, 512:], d_mixed.astype(BF16))
    for c in range(12):
        if c:
            top = tail_of(g, c - 1, c - 1 < 8)
        else:
            top = head_of_rows([last_rows[62:63], last_rows[63:64]])
        g[c, ROWS : ROWS + 16, :] = top.astype(BF16)
        g[c, ROWS + 16 :, :] = gain_rows(d_gain, jnp.zeros((16, 128), F32)).astype(BF16)
    for last, copy in stores:
        if last:
            copy.start()
    dr_out[...] = d_mixed
    for copy in saves[:3]:
        copy.start()
    for copy in saves:
        copy.wait()
    for slot in range(3):
        wait_plane(g, 4 * slot, out_sems.at[slot])


def second_kernel(idx, *refs):
    y_out, dx_out, keep, send = refs[16:20]
    tok, cos, sin, y_in, dr, dg, att, p_in, q_in, k_in, v_in, wq, wk, wv, wo, gain = refs[20:36]
    g, y_t, dx_t, dq_ref, dk_ref, dv_ref, first, second, in_sem, out_sems = refs[36:]
    loads = [
        pltpu.make_async_copy(src, dst, in_sem.at[i])
        for i, (src, dst) in enumerate(zip(refs[:16], refs[20:36]))
    ]
    for copy in loads:
        copy.start()
    tokens = tok.shape[1]
    for copy in loads:
        copy.wait()
    d_mixed = dr[...]
    branch = d_mixed.astype(BF16)
    dw_out = dot_tn(att[...], branch)
    d_att = dot_nt(branch, wo[...])
    for b in range(tokens // SEQ_LEN):
        part = slice(SEQ_LEN * b, SEQ_LEN * (b + 1))
        cosine, sine = cos[part, :], -sin[part, :]
        for kv in range(KV_HEADS):
            at = KV_HEADS * b + kv
            heads = [d_att[part, HEAD * h : HEAD * (h + 1)] for h in range(3 * kv, 3 * kv + 3)]
            d3 = jnp.concatenate(heads, 0).astype(BF16)
            probs, q3, k1, v1 = p_in[at], q_in[at], k_in[at], v_in[at]
            d_probs = dot_nt(d3, v1)
            dv_ref[part, HEAD * kv : HEAD * (kv + 1)] = dot_tn(probs.astype(BF16), d3)
            inner = jnp.sum(d_probs * probs, -1, keepdims=True)
            d_score = (probs * (d_probs - inner)).astype(BF16)
            dq3 = dot(d_score, k1) * HEAD**-0.5
            for r in range(3):
                h = 3 * kv + r
                dq_ref[part, HEAD * h : HEAD * (h + 1)] = turn(
                    dq3[SEQ_LEN * r : SEQ_LEN * (r + 1)], cosine, sine
                )
            dk_ref[part, HEAD * kv : HEAD * (kv + 1)] = turn(
                dot_tn(d_score, q3) * HEAD**-0.5, cosine, sine
            )
    dq, dk, dv = dq_ref[...].astype(BF16), dk_ref[...].astype(BF16), dv_ref[...].astype(BF16)
    x = tok[...].astype(F32)
    inverse = lax.rsqrt(jnp.mean(x * x, 0, keepdims=True) + EPS)
    normed = x * inverse
    gain_column = jnp.broadcast_to(gain[...], (8, gain.shape[1])).T[:, :1]
    n1t = (normed * gain_column).astype(BF16)
    dw_query = dot(n1t, dq)
    store_narrow(g, 0, dw_query[:NARROW])
    dw = unspread(dot(n1t, dk), first, second)
    store_narrow(g, 1, jnp.concatenate([dw_query[NARROW:], dw], 0))
    dw = unspread(dot(n1t, dv), first, second)
    store_narrow(g, 2, jnp.concatenate([dw, dw_out[:192]], 0))
    store_narrow(g, 3, dw_out[192:])
    d_norm = dot_nt(wq[...], dq) + dot_nt(wk[...], dk) + dot_nt(wv[...], dv)
    d_gain = jnp.sum(d_norm * normed, 1, keepdims=True)
    d_gain = jnp.broadcast_to(d_gain, (d_gain.shape[0], 128)).T[:1]
    for c in range(4):
        top = tail_of(g, c - 1, False) if c else head_of_rows([d_gain, dg[...]])
        g[c, ROWS : ROWS + 16, :] = top.astype(BF16)
        g[c, ROWS + 16 :, :] = gain_rows(dg[...], jnp.zeros((16, 128), F32)).astype(BF16)
    for _, copy in piece_copies(idx, 0, [[keep], [send]], g, out_sems.at[0], True):
        copy.start()
    scaled = d_norm * gain_column
    dx_t[...] = d_mixed.T + inverse * (
        scaled - normed * jnp.mean(scaled * normed, 0, keepdims=True)
    )
    y_t[...] = y_in[...].T.astype(BF16)
    stores = [
        pltpu.make_async_copy(src, dst, in_sem.at[i])
        for i, (src, dst) in enumerate(((dx_t, dx_out), (y_t, y_out)))
    ]
    for copy in stores:
        copy.start()
    for copy in stores:
        copy.wait()
    wait_plane(g, 0, out_sems.at[0])


def halves_turned(low, high):
    lane = lax.broadcasted_iota(jnp.int32, low.shape, 1)
    return jnp.where(lane < 64, pltpu.roll(low, 64, 1), pltpu.roll(high, 64, 1))


def pack_kernel(idx, flat, out, rolled, window, packed, mixed):
    index, core, down, right = idx[0], idx[1], idx[2], idx[3]
    lane = lax.broadcasted_iota(jnp.int32, (1, 128), 1)
    rolled[0:16, :] = jnp.zeros((16, 128), F32)
    rolled[16:1752, :] = pltpu.roll(flat[...].astype(F32), right, 1)
    rolled[1752:1760, :] = jnp.zeros((8, 128), F32)
    window[...] = jnp.where(
        lane >= right, rolled[pl.ds(16 - down, 1744), :], rolled[pl.ds(15 - down, 1744), :]
    )
    head = [window[k : k + 1, :] for k in range(9)]
    wide = (index >= 4) & (index < 12)

    @pl.when(wide)
    def _():
        for j in range(12):
            packed[WIDE * j : WIDE * (j + 1), :] = window[pl.ds(9 + j, WIDE, stride=12), :]

    @pl.when(jnp.logical_not(wide))
    def _():
        parts = [window[pl.ds(9 + k, NARROW // 2, stride=9), :] for k in range(9)]
        for j in range(4):
            packed[pl.ds(NARROW * j, NARROW // 2, stride=2), :] = parts[j]
            packed[pl.ds(NARROW * j + 1, NARROW // 2, stride=2), :] = halves_turned(
                parts[4 + j], parts[5 + j]
            )
        mixed[pl.ds(0, NARROW // 2, stride=2), :] = parts[4]
        mixed[pl.ds(1, NARROW // 2, stride=2), :] = pltpu.roll(parts[8], 64, 1)
        packed[4 * NARROW : ROWS, :] = jnp.where(
            lane < 64, mixed[: NARROW // 2, :], pltpu.roll(mixed[NARROW // 2 :, :], 64, 1)
        )

    last = jnp.zeros((23, 128), F32)
    after_wide = (index >= 5) & (index < 13)

    @pl.when(after_wide)
    def _():
        packed[ROWS:, :] = jnp.concatenate(head + [last], 0)

    @pl.when(jnp.logical_not(after_wide))
    def _():
        rows = head[:4] + [halves_turned(head[4 + j], head[5 + j]) for j in range(4)]
        rows.append(jnp.where(lane < 64, 0.0, pltpu.roll(head[4], 64, 1)))
        rows.append(jnp.where(lane < 64, 0.0, head[8]))
        packed[ROWS:, :] = jnp.concatenate(rows + [last[:22]], 0)

    out[...] = packed[pl.ds(pl.multiple_of(core * HALF, 16), HALF), :].astype(BF16)


def unpack_kernel(idx, own, twin, out, packed, window, mixed):
    index, core, down, left = idx[0], idx[1], idx[2], idx[3]
    lane = lax.broadcasted_iota(jnp.int32, (1, 128), 1)
    packed[pl.ds(pl.multiple_of(core * HALF, 16), HALF), :] = own[...]
    packed[pl.ds(pl.multiple_of((1 - core) * HALF, 16), HALF), :] = twin[...]
    head = [packed[ROWS + k : ROWS + k + 1, :] for k in range(10)]
    window[1737:, :] = jnp.zeros((15, 128), F32)
    wide = (index >= 4) & (index < 12)

    @pl.when(wide)
    def _():
        for j in range(12):
            window[pl.ds(9 + j, WIDE, stride=12), :] = packed[WIDE * j : WIDE * (j + 1), :]

    @pl.when(jnp.logical_not(wide))
    def _():
        half = packed[4 * NARROW : ROWS, :]
        mixed[: NARROW // 2, :] = half
        mixed[NARROW // 2 :, :] = pltpu.roll(half, 64, 1)
        odd = []
        for j in range(4):
            window[pl.ds(9 + j, NARROW // 2, stride=9), :] = packed[
                pl.ds(NARROW * j, NARROW // 2, stride=2), :
            ]
            odd.append(pltpu.roll(packed[pl.ds(NARROW * j + 1, NARROW // 2, stride=2), :], 64, 1))
        odd.append(mixed[pl.ds(1, NARROW // 2, stride=2), :])
        before = mixed[pl.ds(0, NARROW // 2, stride=2), :]
        for j in range(4):
            window[pl.ds(13 + j, NARROW // 2, stride=9), :] = jnp.where(lane < 64, before, odd[j])
            before = odd[j]
        window[pl.ds(17, NARROW // 2, stride=9), :] = jnp.where(
            lane < 64, before, pltpu.roll(odd[4], 64, 1)
        )

    after_wide = (index >= 5) & (index < 13)

    @pl.when(after_wide)
    def _():
        window[0:9, :] = jnp.concatenate(head[:9], 0)

    @pl.when(jnp.logical_not(after_wide))
    def _():
        odd = [pltpu.roll(row, 64, 1) for row in head[4:8]]
        before, rows = pltpu.roll(head[8], 64, 1), head[:4]
        for j in range(4):
            rows.append(jnp.where(lane < 64, before, odd[j]))
            before = odd[j]
        rows.append(jnp.where(lane < 64, before, head[9]))
        window[0:9, :] = jnp.concatenate(rows, 0)

    lanes = pltpu.roll(window[...], jnp.bitwise_and(128 - left, 127), 1)
    window[...] = lanes
    out[...] = jnp.where(
        lane < 128 - left, window[pl.ds(down, 1736), :], window[pl.ds(down + 1, 1736), :]
    )


def chunk_index(index, core, lay):
    start = index * lay.step
    return jnp.stack([index, core, start // 128, start % 128]).astype(jnp.int32)


def pack_own(params, index, core, lay):
    if lay.count != CANON:
        window = jnp.zeros((lay.gains + lay.chunk,), params.dtype)
        window = lax.dynamic_update_slice(window, params, (index * lay.step,))
        payload = pack_payload(window, index, lay)
        return lax.dynamic_slice_in_dim(payload, core * lay.half, lay.half, 0)
    flat = jnp.pad(params, (0, 1736 * 128 - lay.shard)).reshape(1736, 128)
    vmem = pl.BlockSpec(memory_space=pltpu.VMEM)
    return pl.pallas_call(
        pack_kernel,
        name="pack_own_chunk",
        in_specs=[pl.BlockSpec(memory_space=pltpu.SMEM), vmem],
        out_specs=vmem,
        out_shape=jax.ShapeDtypeStruct((HALF, 128), BF16),
        scratch_shapes=[
            pltpu.VMEM((1760, 128), F32),
            pltpu.VMEM((1744, 128), F32),
            pltpu.VMEM((2 * HALF, 128), F32),
            pltpu.VMEM((NARROW, 128), F32),
        ],
        compiler_params=pltpu.CompilerParams(vmem_limit_bytes=VMEM_LIMIT),
    )(chunk_index(index, core, lay), flat)


def unpack_own(own, twin, index, core, lay):
    if lay.count != CANON:
        rows = jnp.where(core == 0, jnp.stack([own, twin], 0), jnp.stack([twin, own], 0))
        window = unpack_payload(rows.reshape(2 * lay.half, 128), index, lay)
        return lax.dynamic_slice(window, (index * lay.step,), (lay.shard,))
    vmem = pl.BlockSpec(memory_space=pltpu.VMEM)
    rows = pl.pallas_call(
        unpack_kernel,
        name="unpack_own_chunk",
        in_specs=[pl.BlockSpec(memory_space=pltpu.SMEM), vmem, vmem],
        out_specs=vmem,
        out_shape=jax.ShapeDtypeStruct((1736, 128), F32),
        scratch_shapes=[
            pltpu.VMEM((2 * HALF, 128), F32),
            pltpu.VMEM((1752, 128), F32),
            pltpu.VMEM((NARROW, 128), F32),
        ],
        compiler_params=pltpu.CompilerParams(vmem_limit_bytes=VMEM_LIMIT),
    )(chunk_index(index, core, lay), own, twin)
    return rows.reshape(-1)[: lay.shard]


def tables(positions):
    cosine, sine = rope_tables(positions)
    return jnp.concatenate([cosine, cosine], 1), jnp.concatenate([-sine, sine], 1)


def layer_kernels(length, width):
    groups = length // SEQ_LEN * KV_HEADS
    kv_width = KV_HEADS * HEAD
    smem = pl.BlockSpec(memory_space=pltpu.SMEM)
    vmem = pl.BlockSpec(memory_space=pltpu.VMEM)
    hbm = pl.BlockSpec(memory_space=pltpu.HBM)
    anywhere = pl.BlockSpec(memory_space=pl.ANY)
    params = pltpu.CompilerParams(vmem_limit_bytes=VMEM_LIMIT)

    def sds(shape, dtype):
        return jax.ShapeDtypeStruct(shape, dtype)

    def cost(flops):
        return pl.CostEstimate(flops=flops, bytes_accessed=8_000_000, transcendentals=600_000)

    piece = [sds((4, HALF, 128), BF16)]
    weights = [sds((width, width), BF16), sds((width, kv_width), BF16)]
    weights = weights + [weights[1], weights[0]]
    saved = [
        sds((groups, 3 * SEQ_LEN, SEQ_LEN), F32),
        sds((groups, 3 * SEQ_LEN, HEAD), BF16),
        sds((groups, SEQ_LEN, HEAD), BF16),
        sds((groups, SEQ_LEN, HEAD), BF16),
    ]
    rows = sds((length, width), F32)
    low_rows = sds((length, width), BF16)
    gain = sds((1, width), F32)
    outs = [rows, rows, gain, low_rows] + saved + weights + [gain]
    forward = pl.pallas_call(
        first_kernel,
        name="forward_and_ff_backward",
        in_specs=[smem] + [anywhere] * 14 + [hbm, vmem, vmem, hbm],
        out_specs=[hbm] * len(outs) + [anywhere] * 6,
        out_shape=outs + piece * 6,
        scratch_shapes=[pltpu.VMEM(out.shape, out.dtype) for out in outs]
        + [
            pltpu.VMEM((CANON, 2 * HALF, 128), BF16),
            pltpu.VMEM((12, 2 * HALF, 128), BF16),
            pltpu.VMEM((width, length), BF16),
            pltpu.VMEM((width, length), BF16),
            pltpu.VMEM((length, width), BF16),
            pltpu.VMEM((length, width), F32),
            pltpu.VMEM((length, width), BF16),
            pltpu.VMEM((width, length), BF16),
            pltpu.VMEM((length, width), F32),
            pltpu.VMEM((width, 128), F32),
            pltpu.VMEM((width, 128), F32),
            pltpu.SemaphoreType.DMA((2,)),
            pltpu.SemaphoreType.DMA((4,)),
            pltpu.SemaphoreType.DMA((3,)),
            pltpu.SemaphoreType.DMA((len(outs),)),
        ],
        compiler_params=params,
        cost_estimate=cost(20 * length * width * FF),
    )
    attention_back = pl.pallas_call(
        second_kernel,
        name="attention_backward",
        in_specs=[smem] + [hbm] * 16,
        out_specs=[hbm] * 2 + [anywhere] * 2,
        out_shape=[sds((width, length), BF16), sds((width, length), F32)] + piece * 2,
        scratch_shapes=[
            pltpu.VMEM((width, length), BF16),
            pltpu.VMEM((length, HEAD), F32),
            pltpu.VMEM((length, HEAD), F32),
        ]
        + [pltpu.VMEM(out.shape, out.dtype) for out in outs]
        + [
            pltpu.VMEM((4, 2 * HALF, 128), BF16),
            pltpu.VMEM((width, length), BF16),
            pltpu.VMEM((width, length), F32),
            pltpu.VMEM((length, width), F32),
            pltpu.VMEM((length, kv_width), F32),
            pltpu.VMEM((length, kv_width), F32),
            pltpu.VMEM((width, 128), F32),
            pltpu.VMEM((width, 128), F32),
            pltpu.SemaphoreType.DMA((16,)),
            pltpu.SemaphoreType.DMA((1,)),
        ],
        compiler_params=params,
        cost_estimate=cost(10 * length * width * width),
    )
    return forward, attention_back


def flat_of(payloads, lay):
    n = lay.count
    heads = payloads[:, lay.rows : lay.rows + 10]
    flats = [unhead_narrow(heads[0])]
    for i in range(n):
        wide = n // 4 <= i < 3 * n // 4
        body = payloads[i, : lay.rows]
        flat = unpack_wide(body, FF) if wide else unpack_narrow(body)
        if i + 1 < n:
            tail = unhead_wide(heads[i + 1]) if wide else unhead_narrow(heads[i + 1])
            flat = jnp.concatenate([flat[: -lay.gains], flat[-lay.gains :] + tail])
        flats.append(flat)
    return jnp.concatenate(flats)


def payloads_of(flat, lay):
    windows = [
        flat[i * lay.chunk : (i + 1) * lay.chunk + lay.gains] for i in range(lay.count)
    ]
    return jnp.stack([pack_payload(window, i, lay) for i, window in enumerate(windows)], 0)


def canonical(blocks, twins, lay, canon, index, core):
    sides = []
    for side in (blocks, twins):
        side = jnp.stack([jnp.concatenate(value, 0) for value in side], 0)
        sides.append(side.reshape(lay.count, lay.half, 128))
    both = jnp.where(core == 0, jnp.stack(sides, 1), jnp.stack(sides[::-1], 1))
    both = both.reshape(lay.count, 2 * lay.half, 128)
    both = jnp.take(both, jnp.arange(lay.count, dtype=jnp.int32) ^ index, axis=0)
    flat = flat_of(both, lay)
    zeros = jnp.zeros((canon.gains,), flat.dtype)
    rows = []
    for i in range(CANON):
        window = flat[i * canon.chunk : (i + 1) * canon.chunk + canon.gains]
        if i:
            window = jnp.concatenate([zeros, window[canon.gains :]])
        rows.append(pack_payload(window, i, canon))
    rows = jnp.stack(rows, 0).reshape(PLANES, 4, 2, canon.half, 128)
    pieces = []
    for c in range(2):
        side = rows[:, :, c]
        pieces = pieces + [side[0]] + [side[p, :2] for p in range(1, PLANES)]
        pieces = pieces + [side[p, 2:] for p in range(1, PLANES)]
    return pieces


def from_canonical(slots, lay, canon, place, core):
    sides = []
    for which in range(2):
        sides.append(jnp.stack([slot[which] for slot in slots], 0))
    rows = jnp.stack(sides, 2).reshape(CANON, 2 * canon.half, 128)
    flats = [unhead_narrow(rows[0, canon.rows : canon.rows + 10])]
    for i in range(CANON):
        body = rows[i, : canon.rows]
        flats.append(unpack_wide(body, FF) if 4 <= i < 12 else unpack_narrow(body))
    rows = payloads_of(jnp.concatenate(flats), lay)
    rows = rows.reshape(PLANES, lay.in_plane, 2, lay.half, 128)
    rows = jnp.take(rows, jnp.arange(lay.in_plane, dtype=jnp.int32) ^ place, axis=1)
    rows = rows.reshape(PLANES, 1 << lay.y_bits, 1 << lay.x_bits, 2, lay.half, 128)
    sides = [jnp.take(rows, side, axis=3) for side in (core, 1 - core)]
    return [[list(side[p]) for p in range(PLANES)] for side in sides]


def add(left, right):
    return left.astype(F32) + right.astype(F32)


def on_device(lay, canon, tokens_in, positions, params, cotangent):
    index = lax.axis_index("dp")
    core = lax.axis_index("rep")
    n, half, in_plane = lay.count, lay.half, lay.in_plane
    plane, place = index // in_plane, index % in_plane
    same = n == CANON
    firsts, seconds = hops(lay)
    forward, attention_back = layer_kernels(*tokens_in.shape)
    mine = pack_own(params, index, core, lay)
    angles = tables(positions)
    if same:
        idx = jnp.stack([plane, place, core, 1]).astype(jnp.int32)
        pieces, angles = balanced_gather(mine, lay, angles)
    else:
        idx = jnp.zeros((4,), jnp.int32)
        blocks = gather(mine, lay)
        twins = [[swap_rep(block) for block in value] for value in blocks]
        pieces = canonical(blocks, twins, lay, canon, index, core)
    results = forward(idx, *pieces, tokens_in.T, *angles, cotangent.T)
    d_gain = results[2]
    slots = [results[13 + 2 * p : 15 + 2 * p] for p in range(3)]
    if same:
        (first,), (second,) = firsts, seconds
        keeps, twins = [slot[0] for slot in slots], [swap_rep(slot[1]) for slot in slots]
        moved = [
            hop(add(keep[2:], twin[2:]).astype(BF16), second, n)
            for keep, twin in zip(keeps[:2], twins[:2])
        ]
    output, d_input, *slot = attention_back(idx, tokens_in.T, *angles, *results[:13])
    output, d_input = output.T, d_input.T
    if same:
        moved, slot, twins[2] = lax.optimization_barrier((moved, slot, twins[2]))
        early = [
            (add(keeps[j][:2], twins[j][:2]) + moved[j].astype(F32)).astype(BF16) for j in range(2)
        ]
        early = [add(value[0], hop(value[1], first, n)).astype(BF16) for value in early]
        ground = plane == 0
        other = add(slot[0], swap_rep(slot[1])).astype(BF16)
        third = add(keeps[2], twins[2]).astype(BF16)
        third, mine = jnp.where(ground, third, other), jnp.where(ground, other, third)
        third = add(third[:2], hop(third[2:], second, n)).astype(BF16)
        crossed, moved = lax.optimization_barrier((hop(third[1], first, n), hop(mine[2:], second, n)))
        third = add(third[0], crossed).astype(BF16)
        mine = add(mine[:2], moved).astype(BF16)

        def pick(values, s):
            table = ((0, 1, 2), (2, 1, 0), (1, 2, 0), (1, 0, 2))
            result = values[table[3][s - 1]]
            for z in range(3):
                result = jnp.where(plane == z, values[table[z][s - 1]], result)
            return result

        planes = early + [third]
        parts = [swap(pick(planes, s), s << (lay.bits - 2), n) for s in range(1, PLANES)]
        parts, crossed = lax.optimization_barrier((parts, hop(mine[1], first, n)))
        total = add(mine[0], crossed) + parts[0].astype(F32) + add(parts[1], parts[2])
    else:
        keeps, sends = from_canonical([slot] + slots, lay, canon, place, core)
        moved = []
        for keep, send in zip(keeps, sends):
            pair = pair_sum(keep, send)
            moved.append(add_blocks(pair[0], send_blocks(pair, seconds, n)))
        blocks = split_first(moved, lay)
        planes = add_blocks(blocks[0], send_blocks(blocks, firsts, n))
        total = reduce_planes(planes, plane, lay)
    other = swap_rep(total)
    if same:
        at = ROWS + 26 - HALF
        d_gain = jnp.where(core == 1, total[at : at + 5], other[at : at + 5]).reshape(-1)[: lay.width]
    else:
        d_gain = sum_everywhere(d_gain[0], lay)
    return output, d_input, unpack_own(total, other, index, core, lay), d_gain


def solution(mesh):
    def run(tokens_in, positions, params, cotangent):
        total, width = params.shape[0], tokens_in.shape[1]
        lay = Layout(mesh.shape["dp"], total, width)
        canon = Layout(CANON, total, width)
        rows = P(("dp", "rep"), None)
        return jax.shard_map(
            lambda *args: on_device(lay, canon, *args),
            mesh=mesh,
            in_specs=(rows, P(("dp", "rep")), P("dp"), rows),
            out_specs=(rows, rows, P("dp"), P()),
            check_vma=False,
        )(tokens_in, positions, params, cotangent)

    return run
```

```python
import jax
import jax.numpy as jnp
from jax import lax
from jax.experimental import pallas as pl
from jax.experimental.pallas import tpu as pltpu
from jax.sharding import PartitionSpec as P

HEADS = 9
KV_HEADS = 3
HEAD = 64
FF = 1536
SEQ_LEN = 128
PLANES = 4
CANON = 16

EPS = 1e-05
ROPE_BASE = 100000.0

F32, BF16 = jnp.float32, jnp.bfloat16
ROWS, HALF = 1728, 880
MAIN, REST = 768, 112
NARROW, WIDE = 384, 144
VMEM_LIMIT = 52 * 1024 * 1024


class Layout:
    def __init__(self, count, total, width):
        self.count = count
        self.width = width
        self.gains = 2 * width
        self.shard = total // count
        self.chunk = (total - self.gains) // count
        self.step = self.gains // count
        self.rows = self.chunk // 128
        half = -(-(self.rows + 10) // 2)
        self.half = -(-half // 16) * 16
        self.first = -(-(self.half // 2) // 16) * 16
        self.extra = 2 * self.half - self.rows
        self.bits = count.bit_length() - 1
        rest = self.bits - 2
        self.x_bits = -(-rest // 2)
        self.y_bits = rest - self.x_bits
        self.in_plane = 1 << rest
        self.flip = self.x_bits == self.y_bits


def pack_wide(flat, width):
    panels = width // 128
    return flat.reshape(-1, panels, 128).transpose(1, 0, 2).reshape(-1, 128)


def unpack_wide(rows, width):
    panels = width // 128
    return rows.reshape(panels, -1, 128).transpose(1, 0, 2).reshape(-1)


def pack_narrow(flat):
    rows = flat.reshape(-1, 576)
    count = rows.shape[0]
    panels = rows[:, :512].reshape(count, 4, 128).transpose(1, 0, 2).reshape(-1, 128)
    tail = rows[:, 512:]
    return jnp.concatenate([panels, jnp.concatenate([tail[: count // 2], tail[count // 2 :]], 1)], 0)


def unpack_narrow(packed):
    count = packed.shape[0] * 2 // 9
    panels = packed[: 4 * count].reshape(4, count, 128).transpose(1, 0, 2).reshape(count, 512)
    half = packed[4 * count :]
    tail = jnp.concatenate([half[:, :64], half[:, 64:]], 0)
    return jnp.concatenate([panels, tail], 1).reshape(-1)


def head_narrow(flat):
    rows = flat.reshape(2, 576)
    tail = jnp.pad(rows[:, 512:], ((0, 0), (64, 0)))
    return jnp.concatenate([rows[:, :512].reshape(8, 128), tail], 0)


def unhead_narrow(rows):
    return jnp.concatenate([rows[:8].reshape(2, 512), rows[8:10, 64:]], 1).reshape(-1)


def head_wide(flat):
    return jnp.pad(flat.reshape(9, 128), ((0, 1), (0, 0)))


def unhead_wide(rows):
    return rows[:9].reshape(-1)


def is_wide(index, count):
    return (index >= count // 4) & (index < 3 * count // 4)


def pack_payload(window, index, lay):
    head, chunk = window[: lay.gains], window[lay.gains :]
    body = jnp.where(is_wide(index, lay.count), pack_wide(chunk, FF), pack_narrow(chunk))
    top = jnp.where(is_wide(index - 1, lay.count), head_wide(head), head_narrow(head))
    return jnp.concatenate([body, jnp.pad(top, ((0, lay.extra - 10), (0, 0)))], 0)


def unpack_payload(rows, index, lay):
    body, top = rows[: lay.rows], rows[lay.rows : lay.rows + 10]
    chunk = jnp.where(is_wide(index, lay.count), unpack_wide(body, FF), unpack_narrow(body))
    head = jnp.where(is_wide(index - 1, lay.count), unhead_wide(top), unhead_narrow(top))
    return jnp.concatenate([head, chunk])


def swap(value, mask, count):
    return lax.ppermute(value, "dp", [(i, i ^ mask) for i in range(count)])


def swap_rep(value):
    return lax.ppermute(value, "rep", [(0, 1), (1, 0)])


def hop(value, masks, count):
    pairs = [(2 * i + c, 2 * (i ^ masks[c]) + c) for i in range(count) for c in range(2)]
    return lax.ppermute(value, ("dp", "rep"), pairs)


def hops(lay):
    xs = [d for d in range(1, 1 << lay.x_bits)]
    ys = [e << lay.x_bits for e in range(1, 1 << lay.y_bits)]
    if lay.flip:
        return list(zip(xs, ys)), list(zip(ys, xs))
    return list(zip(xs, xs)), list(zip(ys, ys))


def gather_hops(value, masks, count):
    return jnp.stack([value] + [hop(value, pair, count) for pair in masks], 0)


def gather(half, lay):
    n = lay.count
    first, second = hops(lay)
    planes = [half] + [swap(half, s << (lay.bits - 2), n) for s in range(1, PLANES)]
    blocks = []
    for plane in planes:
        block = gather_hops(plane, first, n)
        blocks.append([block] + [hop(block, masks, n) for masks in second])
    return blocks


def balanced_gather(half, lay, beside):
    n = lay.count
    (first,), (second,) = hops(lay)
    both = tuple(a ^ b for a, b in zip(first, second))
    across = [swap(half, s << (lay.bits - 2), n) for s in range(1, PLANES)]
    plane = [hop(half, masks, n) for masks in (first, second, both)]
    across, plane, beside = lax.optimization_barrier((across, plane, beside))
    own = jnp.stack([half] + plane, 0)
    near = [jnp.stack([value, hop(value, first, n)], 0) for value in across]
    far = [hop(value, second, n) for value in near]
    early = [own] + near
    far[0], twins = lax.optimization_barrier(
        (far[0], [swap_rep(value) for value in early + far[1:]])
    )
    return early + far + twins[:4] + [swap_rep(far[0])] + twins[4:], beside


def pair_sum(keep, send):
    return [
        (mine.astype(F32) + swap_rep(other).astype(F32)).astype(BF16)
        for mine, other in zip(keep, send)
    ]


def send_blocks(blocks, masks, count):
    return [hop(block, pair, count) for block, pair in zip(blocks[1:], masks)]


def add_blocks(block, arrived):
    total = block.astype(F32)
    for value in arrived:
        total = total + value.astype(F32)
    return total.astype(BF16)


def split_first(planes, lay):
    return [jnp.stack([value[j] for value in planes], 0) for j in range(len(hops(lay)[0]) + 1)]


def reduce_planes(planes, plane, lay):
    parts = [jnp.take(planes, plane, axis=0).astype(F32)]
    for s in range(1, PLANES):
        part = swap(jnp.take(planes, plane ^ s, axis=0), s << (lay.bits - 2), lay.count)
        parts.append(part.astype(F32))
    return (parts[0] + parts[1]) + (parts[2] + parts[3])


def sum_everywhere(value, lay):
    value = value + swap_rep(value)
    for bit in range(lay.bits):
        value = value + swap(value, 1 << bit, lay.count)
    return value


def rope_tables(places):
    expon = jnp.arange(HEAD // 2).astype(jnp.float32) * (2.0 / HEAD)
    inverse = jnp.power(ROPE_BASE, -expon)
    angle = places.astype(jnp.float32)[..., None] * inverse
    return (jnp.cos(angle), jnp.sin(angle))


def dot(left, right):
    return jnp.dot(left, right, preferred_element_type=F32)


def dot_nt(left, right):
    return lax.dot_general(left, right, (((1,), (1,)), ((), ())), preferred_element_type=F32)


def dot_tn(left, right):
    return dot(left.astype(F32).T.astype(BF16), right)


def row_of_head(head, which):
    parts = [head[4 * which + j : 4 * which + j + 1] for j in range(4)]
    return jnp.concatenate(parts + [head[8 + which : 9 + which, 64:]], 1)


def head_of_rows(rows):
    parts = [row[:, 128 * j : 128 * j + 128] for row in rows for j in range(4)]
    zeros = jnp.zeros((1, 64), F32)
    parts = parts + [jnp.concatenate([zeros, row[:, 512:]], 1) for row in rows]
    return jnp.concatenate(parts + [jnp.zeros((6, 128), F32)], 0)


def gain_rows(gain, low):
    parts = [gain[:, 128 * j : 128 * j + 128] for j in range(4)]
    parts = parts + [jnp.concatenate([gain[:, 512:], gain[:, 512:]], 1)]
    return jnp.concatenate([low[:10]] + parts + [jnp.zeros((1, 128), F32)], 0)


def load_narrow(ref, index):
    parts = [ref[index, NARROW * j : NARROW * (j + 1), :] for j in range(4)]
    half = ref[index, 4 * NARROW : ROWS, :]
    tail = jnp.concatenate([half[:, :64], half[:, 64:]], 0)
    return jnp.concatenate(parts + [tail], 1)


def store_narrow(ref, index, value):
    for j in range(4):
        ref[index, NARROW * j : NARROW * (j + 1), :] = value[:, 128 * j : 128 * (j + 1)].astype(BF16)
    tail = value[:, 512:]
    tail = jnp.concatenate([tail[: NARROW // 2], tail[NARROW // 2 :]], 1)
    ref[index, 4 * NARROW : ROWS, :] = tail.astype(BF16)


def narrow_tiles():
    tiles = [(NARROW * (j + 1) - 16, j, 4 + j) for j in range(4)]
    return tiles + [(ROWS - 16, 8, 9)]


def add_tail(ref, index, wide):
    head = ref[index + 1, ROWS : ROWS + 16, :].astype(F32)
    row = lax.broadcasted_iota(jnp.int32, (16, 128), 0)
    if wide:
        for k in range(9):
            at = WIDE * (4 + k) - 16
            tile = ref[index, at : at + 16, :].astype(F32)
            tile = tile + jnp.where(row == 15, head[k : k + 1], 0.0)
            ref[index, at : at + 16, :] = tile.astype(BF16)
    else:
        for at, upper, lower in narrow_tiles():
            tile = ref[index, at : at + 16, :].astype(F32)
            tile = tile + jnp.where(row == 14, head[upper : upper + 1], 0.0)
            tile = tile + jnp.where(row == 15, head[lower : lower + 1], 0.0)
            ref[index, at : at + 16, :] = tile.astype(BF16)


def tail_of(ref, index, wide):
    if wide:
        parts = []
        for k in range(9):
            at = WIDE * (4 + k) - 16
            parts.append(ref[index, at : at + 16, :].astype(F32)[15:16])
        return jnp.concatenate(parts + [jnp.zeros((7, 128), F32)], 0)
    tiles = [ref[index, at : at + 16, :].astype(F32) for at, _, _ in narrow_tiles()]
    parts = [tile[14:15] for tile in tiles[:4]] + [tile[15:16] for tile in tiles[:4]]
    parts = parts + [tiles[4][14:15], tiles[4][15:16]]
    return jnp.concatenate(parts + [jnp.zeros((6, 128), F32)], 0)


def spread(value, first, second, out):
    for m in range(3):
        part = value[:, 192 * m : 192 * (m + 1)].astype(F32)
        first[pl.ds(m, 192, stride=3), :] = part[:, :128]
        second[pl.ds(m, 192, stride=3), :] = jnp.concatenate([part[:, 128:], part[:, 128:]], 1)
    out[:, :128] = first[...].astype(BF16)
    out[:, 128:] = second[:, :64].astype(BF16)


def unspread(value, first, second):
    first[...] = value[:, :128]
    second[...] = jnp.concatenate([value[:, 128:], value[:, 128:]], 1)
    parts = []
    for m in range(3):
        parts.append(first[pl.ds(m, 192, stride=3), :])
        parts.append(second[pl.ds(m, 192, stride=3), :][:, :64])
    return jnp.concatenate(parts, 1)


def turn(vector, cosine, sine):
    swapped = jnp.concatenate([vector[:, 32:], vector[:, :32]], 1)
    return vector * cosine + swapped * sine


def piece_copies(idx, at_plane, sides, dst, sem, outward):
    place, core, flip = idx[1], idx[2], idx[3]
    copies = []
    for which, refs in enumerate(sides):
        side = jnp.bitwise_xor(core, which)
        for d in range(4):
            turned = ((d & 1) << 1) | (d >> 1)
            chunk = 4 * at_plane + jnp.bitwise_xor(place, jnp.where(side * flip == 1, turned, d))
            ref = refs[0].at[d] if len(refs) == 1 else refs[d // 2].at[d % 2]
            for start, rows in ((0, MAIN), (MAIN, REST)) if outward else ((0, HALF),):
                outer = ref.at[pl.ds(start, rows), :]
                at = pl.multiple_of(side * HALF + start, 16)
                inner = dst.at[chunk, pl.ds(at, rows), :]
                pair = (inner, outer) if outward else (outer, inner)
                copies.append((start > 0, pltpu.make_async_copy(pair[0], pair[1], sem)))
    return copies


def wait_plane(ref, base, sem):
    whole = ref.at[pl.ds(base, 4)]
    pltpu.make_async_copy(whole, whole, sem).wait()


def slot_plane(plane, slot):
    own = jnp.where(plane == 0, 3, plane)
    low = jnp.where(own == 1, 2, 1)
    return [low, 6 - own - low, own][slot]


def first_kernel(idx, *refs):
    pieces = list(zip(refs[:7], refs[7:14]))
    tok_hbm, cos, sin, cot_hbm = refs[14:18]
    refs = refs[18:]
    results, outs = refs[:13], refs[13:23]
    refs = refs[23:]
    y_acc, dr_out, dg_out, att_out, p_out, q_out, k_out, v_out, wq, wk, wv, wo, gain_out = refs[:13]
    w, g, tok, cot_t, cot, att, n2_ref, n2t_ref, dn_acc, first, second = refs[13:24]
    in_sem, sems, out_sems, result_sems = refs[24:]
    saves = [
        pltpu.make_async_copy(src, dst, result_sems.at[i])
        for i, (src, dst) in enumerate(zip(refs[:13], results))
    ]
    load = pltpu.make_async_copy(tok_hbm, tok, in_sem.at[0])
    load.start()
    load_cot = pltpu.make_async_copy(cot_hbm, cot_t, in_sem.at[1])
    load_cot.start()
    for s in range(PLANES):
        sides = [[ref] for ref in pieces[0]]
        if s:
            sides = list(zip(pieces[s], pieces[s + 3]))
        at_plane = jnp.bitwise_xor(idx[0], s)
        for _, copy in piece_copies(idx, at_plane, sides, w, sems.at[at_plane], False):
            copy.start()
    tokens = tok.shape[1]
    load.wait()
    x = tok[...].astype(F32).T
    normed = x * lax.rsqrt(jnp.mean(x * x, -1, keepdims=True) + EPS)
    load_cot.wait()
    cot[...] = cot_t[...].astype(F32).T.astype(BF16)
    wait_plane(w, 0, sems.at[0])
    for c in range(3):
        add_tail(w, c, False)
    gains = w[0, ROWS : ROWS + 16, :].astype(F32)
    gain_in, gain_mid = row_of_head(gains, 0), row_of_head(gains, 1)
    gain_out[...] = gain_in
    n1 = (normed * gain_in).astype(BF16)
    wq[:NARROW, :] = load_narrow(w, 0)
    mixed_chunk = load_narrow(w, 1)
    wq[NARROW:, :] = mixed_chunk[:192]
    spread(mixed_chunk[192:], first, second, wk)
    mixed_chunk = load_narrow(w, 2)
    spread(mixed_chunk[:192], first, second, wv)
    wo[:192, :] = mixed_chunk[192:]

    query, keys, values = dot(n1, wq[...]), dot(n1, wk[...]), dot(n1, wv[...])
    row = lax.broadcasted_iota(jnp.int32, (3 * SEQ_LEN, SEQ_LEN), 0)
    causal = jnp.bitwise_and(row, SEQ_LEN - 1) >= lax.broadcasted_iota(
        jnp.int32, (3 * SEQ_LEN, SEQ_LEN), 1
    )
    for b in range(tokens // SEQ_LEN):
        part = slice(SEQ_LEN * b, SEQ_LEN * (b + 1))
        cosine, sine = cos[part, :], sin[part, :]
        for kv in range(KV_HEADS):
            at = KV_HEADS * b + kv
            heads = [
                turn(query[part, HEAD * h : HEAD * (h + 1)], cosine, sine)
                for h in range(3 * kv, 3 * kv + 3)
            ]
            q3 = jnp.concatenate(heads, 0).astype(BF16)
            k1 = turn(keys[part, HEAD * kv : HEAD * (kv + 1)], cosine, sine).astype(BF16)
            v1 = values[part, HEAD * kv : HEAD * (kv + 1)].astype(BF16)
            q_out[at], k_out[at], v_out[at] = q3, k1, v1
            score = jnp.where(causal, dot_nt(q3, k1) * HEAD**-0.5, -1e30)
            expon = jnp.exp(score - jnp.max(score, -1, keepdims=True))
            probs = expon / jnp.sum(expon, -1, keepdims=True)
            p_out[at] = probs
            mix = dot(probs.astype(BF16), v1)
            for r in range(3):
                h = 3 * kv + r
                att[part, HEAD * h : HEAD * (h + 1)] = mix[SEQ_LEN * r : SEQ_LEN * (r + 1)]
    attended = att[...].astype(BF16)
    att_out[...] = attended
    wait_plane(w, 4, sems.at[1])
    add_tail(w, 3, False)
    wo[192:, :] = load_narrow(w, 3)
    for copy in saves[3:]:
        copy.start()
    mixed = x + dot(attended, wo[...])
    inverse = lax.rsqrt(jnp.mean(mixed * mixed, -1, keepdims=True) + EPS)
    normed_mid = mixed * inverse
    n2 = normed_mid * gain_mid
    n2_ref[...] = n2.astype(BF16)
    n2t_ref[...] = n2.astype(BF16).astype(F32).T.astype(BF16)
    y_acc[...] = mixed
    dn_acc[...] = jnp.zeros_like(dn_acc)
    wait_plane(w, 8, sems.at[2])
    wait_plane(w, 12, sems.at[3])

    def fix(i, carry):
        add_tail(w, i + 4, True)
        return carry

    lax.fori_loop(0, 8, fix, 0)
    for c in (12, 13, 14):
        add_tail(w, c, False)

    def block(k, carry):
        def wide(base, p):
            at = pl.multiple_of((6 * k + p) * WIDE, 16)
            return jnp.concatenate([w[base + d, pl.ds(at, WIDE), :] for d in range(4)], 0)

        w_gate = jnp.concatenate([wide(4, p) for p in range(6)], 1)
        w_up = jnp.concatenate([wide(8, p) for p in range(6)], 1)
        w_down = jnp.concatenate([load_narrow(w, 12 + 2 * k), load_narrow(w, 13 + 2 * k)], 0)
        c = cot[...]
        gate, up = dot(n2_ref[...], w_gate), dot(n2_ref[...], w_up)
        sigma = 1.0 / (1.0 + jnp.exp(-gate))
        silu = gate * sigma
        hidden = (silu * up).astype(BF16)
        y_acc[...] += dot(hidden, w_down)
        d_down = dot_tn(hidden, c)
        store_narrow(g, 8 + 2 * k, d_down[:NARROW])
        store_narrow(g, 9 + 2 * k, d_down[NARROW:])
        d_hidden = dot_nt(c, w_down)
        d_gate = (d_hidden * up * sigma * (1.0 + gate * (1.0 - sigma))).astype(BF16)
        d_up = (d_hidden * silu).astype(BF16)
        dn_acc[...] += dot_nt(d_gate, w_gate) + dot_nt(d_up, w_up)
        for base, d_out in ((0, d_gate), (4, d_up)):
            grad = dot(n2t_ref[...], d_out).astype(BF16)
            for p in range(6):
                at = pl.multiple_of((6 * k + p) * WIDE, 16)
                for d in range(4):
                    g[base + d, pl.ds(at, WIDE), :] = grad[
                        WIDE * d : WIDE * (d + 1), 128 * p : 128 * (p + 1)
                    ]
        return carry

    lax.fori_loop(0, 2, block, 0)
    stores = []
    for slot in range(3):
        sides = [outs[4 * slot : 4 * slot + 2], outs[4 * slot + 2 : 4 * slot + 4]]
        if slot == 2:
            sides = [outs[8:9], outs[9:10]]
        at_plane = slot_plane(idx[0], slot) - 1
        stores = stores + piece_copies(idx, at_plane, sides, g, out_sems.at[slot], True)
    for last, copy in stores:
        if not last:
            copy.start()
    d_norm = dn_acc[...]
    d_gain = jnp.sum(d_norm * normed_mid, 0, keepdims=True)
    dg_out[...] = d_gain
    scaled = d_norm * gain_mid
    d_mixed = cot[...].astype(F32) + inverse * (
        scaled - normed_mid * jnp.mean(scaled * normed_mid, -1, keepdims=True)
    )
    last_rows = dot_tn(att_out[:, 512:], d_mixed.astype(BF16))
    for c in range(12):
        if c:
            top = tail_of(g, c - 1, c - 1 < 8)
        else:
            top = head_of_rows([last_rows[62:63], last_rows[63:64]])
        g[c, ROWS : ROWS + 16, :] = top.astype(BF16)
        g[c, ROWS + 16 :, :] = gain_rows(d_gain, jnp.zeros((16, 128), F32)).astype(BF16)
    for last, copy in stores:
        if last:
            copy.start()
    dr_out[...] = d_mixed
    for copy in saves[:3]:
        copy.start()
    for copy in saves:
        copy.wait()
    for slot in range(3):
        wait_plane(g, 4 * slot, out_sems.at[slot])


def second_kernel(idx, *refs):
    tok, cos, sin, y_in, dr, dg, att, p_in, q_in, k_in, v_in, wq, wk, wv, wo, gain = refs[:16]
    held, (y_out, dx_out), third, mine = refs[16:18], refs[18:20], refs[20:24], refs[24:26]
    g, bounce, y_t, dx_t, dq_ref, dk_ref, dv_ref, first, second, in_sem, out_sems, held_sem = refs[26:]
    tokens = tok.shape[1]
    ground = idx[0] == 0
    fetch = [
        pltpu.make_async_copy(held[side], bounce.at[side], held_sem.at[side]) for side in range(2)
    ]
    for copy in fetch:
        copy.start()
    d_mixed = dr[...]
    branch = d_mixed.astype(BF16)
    dw_out = dot_tn(att[...], branch)
    d_att = dot_nt(branch, wo[...])
    for b in range(tokens // SEQ_LEN):
        part = slice(SEQ_LEN * b, SEQ_LEN * (b + 1))
        cosine, sine = cos[part, :], -sin[part, :]
        for kv in range(KV_HEADS):
            at = KV_HEADS * b + kv
            heads = [d_att[part, HEAD * h : HEAD * (h + 1)] for h in range(3 * kv, 3 * kv + 3)]
            d3 = jnp.concatenate(heads, 0).astype(BF16)
            probs, q3, k1, v1 = p_in[at], q_in[at], k_in[at], v_in[at]
            d_probs = dot_nt(d3, v1)
            dv_ref[part, HEAD * kv : HEAD * (kv + 1)] = dot_tn(probs.astype(BF16), d3)
            inner = jnp.sum(d_probs * probs, -1, keepdims=True)
            d_score = (probs * (d_probs - inner)).astype(BF16)
            dq3 = dot(d_score, k1) * HEAD**-0.5
            for r in range(3):
                h = 3 * kv + r
                dq_ref[part, HEAD * h : HEAD * (h + 1)] = turn(
                    dq3[SEQ_LEN * r : SEQ_LEN * (r + 1)], cosine, sine
                )
            dk_ref[part, HEAD * kv : HEAD * (kv + 1)] = turn(
                dot_tn(d_score, q3) * HEAD**-0.5, cosine, sine
            )
    dq, dk, dv = dq_ref[...].astype(BF16), dk_ref[...].astype(BF16), dv_ref[...].astype(BF16)
    for copy in fetch:
        copy.wait()

    @pl.when(ground)
    def _():
        for side in range(2):
            for j in range(2):
                source = bounce.at[side, pl.ds(2 * j, 2)]
                pltpu.make_async_copy(source, third[2 * side + j], held_sem.at[2]).start()

    @pl.when(jnp.logical_not(ground))
    def _():
        for side in range(2):
            pltpu.make_async_copy(bounce.at[side], mine[side], held_sem.at[2]).start()

    x = tok[...].astype(F32)
    inverse = lax.rsqrt(jnp.mean(x * x, 0, keepdims=True) + EPS)
    normed = x * inverse
    gain_column = jnp.broadcast_to(gain[...], (8, gain.shape[1])).T[:, :1]
    n1t = (normed * gain_column).astype(BF16)
    dw_query = dot(n1t, dq)
    store_narrow(g, 0, dw_query[:NARROW])
    dw = unspread(dot(n1t, dk), first, second)
    store_narrow(g, 1, jnp.concatenate([dw_query[NARROW:], dw], 0))
    dw = unspread(dot(n1t, dv), first, second)
    store_narrow(g, 2, jnp.concatenate([dw, dw_out[:192]], 0))
    store_narrow(g, 3, dw_out[192:])
    d_norm = dot_nt(wq[...], dq) + dot_nt(wk[...], dk) + dot_nt(wv[...], dv)
    d_gain = jnp.sum(d_norm * normed, 1, keepdims=True)
    d_gain = jnp.broadcast_to(d_gain, (d_gain.shape[0], 128)).T[:1]
    for c in range(4):
        top = tail_of(g, c - 1, False) if c else head_of_rows([d_gain, dg[...]])
        g[c, ROWS : ROWS + 16, :] = top.astype(BF16)
        g[c, ROWS + 16 :, :] = gain_rows(dg[...], jnp.zeros((16, 128), F32)).astype(BF16)

    @pl.when(ground)
    def _():
        for _, copy in piece_copies(idx, 0, [mine[:1], mine[1:]], g, out_sems.at[0], True):
            copy.start()

    @pl.when(jnp.logical_not(ground))
    def _():
        for _, copy in piece_copies(idx, 0, [third[:2], third[2:]], g, out_sems.at[0], True):
            copy.start()

    scaled = d_norm * gain_column
    dx_t[...] = d_mixed.T + inverse * (
        scaled - normed * jnp.mean(scaled * normed, 0, keepdims=True)
    )
    y_t[...] = y_in[...].T.astype(BF16)
    stores = [
        pltpu.make_async_copy(src, dst, in_sem.at[i])
        for i, (src, dst) in enumerate(((dx_t, dx_out), (y_t, y_out)))
    ]
    for copy in stores:
        copy.start()
    for copy in stores:
        copy.wait()
    wait_plane(g, 0, out_sems.at[0])
    wait_plane(g, 0, held_sem.at[2])


def halves_turned(low, high):
    lane = lax.broadcasted_iota(jnp.int32, low.shape, 1)
    return jnp.where(lane < 64, pltpu.roll(low, 64, 1), pltpu.roll(high, 64, 1))


def pack_kernel(idx, flat, out, rolled, window, packed, mixed):
    index, core, down, right = idx[0], idx[1], idx[2], idx[3]
    lane = lax.broadcasted_iota(jnp.int32, (1, 128), 1)
    rolled[0:16, :] = jnp.zeros((16, 128), F32)
    rolled[16:1752, :] = pltpu.roll(flat[...].astype(F32), right, 1)
    rolled[1752:1760, :] = jnp.zeros((8, 128), F32)
    window[...] = jnp.where(
        lane >= right, rolled[pl.ds(16 - down, 1744), :], rolled[pl.ds(15 - down, 1744), :]
    )
    head = [window[k : k + 1, :] for k in range(9)]
    wide = (index >= 4) & (index < 12)

    @pl.when(wide)
    def _():
        for j in range(12):
            packed[WIDE * j : WIDE * (j + 1), :] = window[pl.ds(9 + j, WIDE, stride=12), :]

    @pl.when(jnp.logical_not(wide))
    def _():
        parts = [window[pl.ds(9 + k, NARROW // 2, stride=9), :] for k in range(9)]
        for j in range(4):
            packed[pl.ds(NARROW * j, NARROW // 2, stride=2), :] = parts[j]
            packed[pl.ds(NARROW * j + 1, NARROW // 2, stride=2), :] = halves_turned(
                parts[4 + j], parts[5 + j]
            )
        mixed[pl.ds(0, NARROW // 2, stride=2), :] = parts[4]
        mixed[pl.ds(1, NARROW // 2, stride=2), :] = pltpu.roll(parts[8], 64, 1)
        packed[4 * NARROW : ROWS, :] = jnp.where(
            lane < 64, mixed[: NARROW // 2, :], pltpu.roll(mixed[NARROW // 2 :, :], 64, 1)
        )

    last = jnp.zeros((23, 128), F32)
    after_wide = (index >= 5) & (index < 13)

    @pl.when(after_wide)
    def _():
        packed[ROWS:, :] = jnp.concatenate(head + [last], 0)

    @pl.when(jnp.logical_not(after_wide))
    def _():
        rows = head[:4] + [halves_turned(head[4 + j], head[5 + j]) for j in range(4)]
        rows.append(jnp.where(lane < 64, 0.0, pltpu.roll(head[4], 64, 1)))
        rows.append(jnp.where(lane < 64, 0.0, head[8]))
        packed[ROWS:, :] = jnp.concatenate(rows + [last[:22]], 0)

    out[...] = packed[pl.ds(pl.multiple_of(core * HALF, 16), HALF), :].astype(BF16)


def unpack_kernel(idx, own, twin, out, packed, window, mixed):
    index, core, down, left = idx[0], idx[1], idx[2], idx[3]
    lane = lax.broadcasted_iota(jnp.int32, (1, 128), 1)
    packed[pl.ds(pl.multiple_of(core * HALF, 16), HALF), :] = own[...]
    packed[pl.ds(pl.multiple_of((1 - core) * HALF, 16), HALF), :] = twin[...]
    head = [packed[ROWS + k : ROWS + k + 1, :] for k in range(10)]
    window[1737:, :] = jnp.zeros((15, 128), F32)
    wide = (index >= 4) & (index < 12)

    @pl.when(wide)
    def _():
        for j in range(12):
            window[pl.ds(9 + j, WIDE, stride=12), :] = packed[WIDE * j : WIDE * (j + 1), :]

    @pl.when(jnp.logical_not(wide))
    def _():
        half = packed[4 * NARROW : ROWS, :]
        mixed[: NARROW // 2, :] = half
        mixed[NARROW // 2 :, :] = pltpu.roll(half, 64, 1)
        odd = []
        for j in range(4):
            window[pl.ds(9 + j, NARROW // 2, stride=9), :] = packed[
                pl.ds(NARROW * j, NARROW // 2, stride=2), :
            ]
            odd.append(pltpu.roll(packed[pl.ds(NARROW * j + 1, NARROW // 2, stride=2), :], 64, 1))
        odd.append(mixed[pl.ds(1, NARROW // 2, stride=2), :])
        before = mixed[pl.ds(0, NARROW // 2, stride=2), :]
        for j in range(4):
            window[pl.ds(13 + j, NARROW // 2, stride=9), :] = jnp.where(lane < 64, before, odd[j])
            before = odd[j]
        window[pl.ds(17, NARROW // 2, stride=9), :] = jnp.where(
            lane < 64, before, pltpu.roll(odd[4], 64, 1)
        )

    after_wide = (index >= 5) & (index < 13)

    @pl.when(after_wide)
    def _():
        window[0:9, :] = jnp.concatenate(head[:9], 0)

    @pl.when(jnp.logical_not(after_wide))
    def _():
        odd = [pltpu.roll(row, 64, 1) for row in head[4:8]]
        before, rows = pltpu.roll(head[8], 64, 1), head[:4]
        for j in range(4):
            rows.append(jnp.where(lane < 64, before, odd[j]))
            before = odd[j]
        rows.append(jnp.where(lane < 64, before, head[9]))
        window[0:9, :] = jnp.concatenate(rows, 0)

    lanes = pltpu.roll(window[...], jnp.bitwise_and(128 - left, 127), 1)
    window[...] = lanes
    out[...] = jnp.where(
        lane < 128 - left, window[pl.ds(down, 1736), :], window[pl.ds(down + 1, 1736), :]
    )


def chunk_index(index, core, lay):
    start = index * lay.step
    return jnp.stack([index, core, start // 128, start % 128]).astype(jnp.int32)


def pack_own(params, index, core, lay):
    if lay.count != CANON:
        window = jnp.zeros((lay.gains + lay.chunk,), params.dtype)
        window = lax.dynamic_update_slice(window, params, (index * lay.step,))
        payload = pack_payload(window, index, lay)
        return lax.dynamic_slice_in_dim(payload, core * lay.half, lay.half, 0)
    flat = jnp.pad(params, (0, 1736 * 128 - lay.shard)).reshape(1736, 128)
    vmem = pl.BlockSpec(memory_space=pltpu.VMEM)
    return pl.pallas_call(
        pack_kernel,
        name="pack_own_chunk",
        in_specs=[pl.BlockSpec(memory_space=pltpu.SMEM), vmem],
        out_specs=vmem,
        out_shape=jax.ShapeDtypeStruct((HALF, 128), BF16),
        scratch_shapes=[
            pltpu.VMEM((1760, 128), F32),
            pltpu.VMEM((1744, 128), F32),
            pltpu.VMEM((2 * HALF, 128), F32),
            pltpu.VMEM((NARROW, 128), F32),
        ],
        compiler_params=pltpu.CompilerParams(vmem_limit_bytes=VMEM_LIMIT),
    )(chunk_index(index, core, lay), flat)


def unpack_own(own, twin, index, core, lay):
    if lay.count != CANON:
        rows = jnp.where(core == 0, jnp.stack([own, twin], 0), jnp.stack([twin, own], 0))
        window = unpack_payload(rows.reshape(2 * lay.half, 128), index, lay)
        return lax.dynamic_slice(window, (index * lay.step,), (lay.shard,))
    vmem = pl.BlockSpec(memory_space=pltpu.VMEM)
    rows = pl.pallas_call(
        unpack_kernel,
        name="unpack_own_chunk",
        in_specs=[pl.BlockSpec(memory_space=pltpu.SMEM), vmem, vmem],
        out_specs=vmem,
        out_shape=jax.ShapeDtypeStruct((1736, 128), F32),
        scratch_shapes=[
            pltpu.VMEM((2 * HALF, 128), F32),
            pltpu.VMEM((1752, 128), F32),
            pltpu.VMEM((NARROW, 128), F32),
        ],
        compiler_params=pltpu.CompilerParams(vmem_limit_bytes=VMEM_LIMIT),
    )(chunk_index(index, core, lay), own, twin)
    return rows.reshape(-1)[: lay.shard]


def tables(positions):
    cosine, sine = rope_tables(positions)
    return jnp.concatenate([cosine, cosine], 1), jnp.concatenate([-sine, sine], 1)


def layer_kernels(length, width):
    groups = length // SEQ_LEN * KV_HEADS
    kv_width = KV_HEADS * HEAD
    smem = pl.BlockSpec(memory_space=pltpu.SMEM)
    vmem = pl.BlockSpec(memory_space=pltpu.VMEM)
    hbm = pl.BlockSpec(memory_space=pltpu.HBM)
    anywhere = pl.BlockSpec(memory_space=pl.ANY)
    params = pltpu.CompilerParams(vmem_limit_bytes=VMEM_LIMIT)

    def sds(shape, dtype):
        return jax.ShapeDtypeStruct(shape, dtype)

    def cost(flops):
        return pl.CostEstimate(flops=flops, bytes_accessed=8_000_000, transcendentals=600_000)

    piece, block = sds((4, HALF, 128), BF16), sds((2, HALF, 128), BF16)
    weights = [sds((width, width), BF16), sds((width, kv_width), BF16)]
    weights = weights + [weights[1], weights[0]]
    saved = [
        sds((groups, 3 * SEQ_LEN, SEQ_LEN), F32),
        sds((groups, 3 * SEQ_LEN, HEAD), BF16),
        sds((groups, SEQ_LEN, HEAD), BF16),
        sds((groups, SEQ_LEN, HEAD), BF16),
    ]
    rows = sds((length, width), F32)
    low_rows = sds((length, width), BF16)
    gain = sds((1, width), F32)
    outs = [rows, rows, gain, low_rows] + saved + weights + [gain]
    forward = pl.pallas_call(
        first_kernel,
        name="forward_and_ff_backward",
        in_specs=[smem] + [anywhere] * 14 + [hbm, vmem, vmem, hbm],
        out_specs=[hbm] * len(outs) + [anywhere] * 10,
        out_shape=outs + [block] * 8 + [piece] * 2,
        scratch_shapes=[pltpu.VMEM(out.shape, out.dtype) for out in outs]
        + [
            pltpu.VMEM((CANON, 2 * HALF, 128), BF16),
            pltpu.VMEM((12, 2 * HALF, 128), BF16),
            pltpu.VMEM((width, length), BF16),
            pltpu.VMEM((width, length), BF16),
            pltpu.VMEM((length, width), BF16),
            pltpu.VMEM((length, width), F32),
            pltpu.VMEM((length, width), BF16),
            pltpu.VMEM((width, length), BF16),
            pltpu.VMEM((length, width), F32),
            pltpu.VMEM((width, 128), F32),
            pltpu.VMEM((width, 128), F32),
            pltpu.SemaphoreType.DMA((2,)),
            pltpu.SemaphoreType.DMA((4,)),
            pltpu.SemaphoreType.DMA((3,)),
            pltpu.SemaphoreType.DMA((len(outs),)),
        ],
        compiler_params=params,
        cost_estimate=cost(20 * length * width * FF),
    )
    attention_back = pl.pallas_call(
        second_kernel,
        name="attention_backward",
        in_specs=[smem] + [vmem] * 16 + [anywhere] * 2,
        out_specs=[hbm] * 2 + [anywhere] * 6,
        out_shape=[sds((width, length), BF16), sds((width, length), F32)] + [block] * 4 + [piece] * 2,
        scratch_shapes=[
            pltpu.VMEM((4, 2 * HALF, 128), BF16),
            pltpu.VMEM((2, 4, HALF, 128), BF16),
            pltpu.VMEM((width, length), BF16),
            pltpu.VMEM((width, length), F32),
            pltpu.VMEM((length, width), F32),
            pltpu.VMEM((length, kv_width), F32),
            pltpu.VMEM((length, kv_width), F32),
            pltpu.VMEM((width, 128), F32),
            pltpu.VMEM((width, 128), F32),
            pltpu.SemaphoreType.DMA((2,)),
            pltpu.SemaphoreType.DMA((1,)),
            pltpu.SemaphoreType.DMA((3,)),
        ],
        compiler_params=params,
        cost_estimate=cost(10 * length * width * width),
    )
    return forward, attention_back


def flat_of(payloads, lay):
    n = lay.count
    heads = payloads[:, lay.rows : lay.rows + 10]
    flats = [unhead_narrow(heads[0])]
    for i in range(n):
        wide = n // 4 <= i < 3 * n // 4
        body = payloads[i, : lay.rows]
        flat = unpack_wide(body, FF) if wide else unpack_narrow(body)
        if i + 1 < n:
            tail = unhead_wide(heads[i + 1]) if wide else unhead_narrow(heads[i + 1])
            flat = jnp.concatenate([flat[: -lay.gains], flat[-lay.gains :] + tail])
        flats.append(flat)
    return jnp.concatenate(flats)


def payloads_of(flat, lay):
    windows = [
        flat[i * lay.chunk : (i + 1) * lay.chunk + lay.gains] for i in range(lay.count)
    ]
    return jnp.stack([pack_payload(window, i, lay) for i, window in enumerate(windows)], 0)


def canonical(blocks, twins, lay, canon, index, core):
    sides = []
    for side in (blocks, twins):
        side = jnp.stack([jnp.concatenate(value, 0) for value in side], 0)
        sides.append(side.reshape(lay.count, lay.half, 128))
    both = jnp.where(core == 0, jnp.stack(sides, 1), jnp.stack(sides[::-1], 1))
    both = both.reshape(lay.count, 2 * lay.half, 128)
    both = jnp.take(both, jnp.arange(lay.count, dtype=jnp.int32) ^ index, axis=0)
    flat = flat_of(both, lay)
    zeros = jnp.zeros((canon.gains,), flat.dtype)
    rows = []
    for i in range(CANON):
        window = flat[i * canon.chunk : (i + 1) * canon.chunk + canon.gains]
        if i:
            window = jnp.concatenate([zeros, window[canon.gains :]])
        rows.append(pack_payload(window, i, canon))
    rows = jnp.stack(rows, 0).reshape(PLANES, 4, 2, canon.half, 128)
    pieces = []
    for c in range(2):
        side = rows[:, :, c]
        pieces = pieces + [side[0]] + [side[p, :2] for p in range(1, PLANES)]
        pieces = pieces + [side[p, 2:] for p in range(1, PLANES)]
    return pieces


def from_canonical(slots, lay, canon, place, core):
    sides = []
    for which in range(2):
        sides.append(jnp.stack([slot[which] for slot in slots], 0))
    rows = jnp.stack(sides, 2).reshape(CANON, 2 * canon.half, 128)
    flats = [unhead_narrow(rows[0, canon.rows : canon.rows + 10])]
    for i in range(CANON):
        body = rows[i, : canon.rows]
        flats.append(unpack_wide(body, FF) if 4 <= i < 12 else unpack_narrow(body))
    rows = payloads_of(jnp.concatenate(flats), lay)
    rows = rows.reshape(PLANES, lay.in_plane, 2, lay.half, 128)
    rows = jnp.take(rows, jnp.arange(lay.in_plane, dtype=jnp.int32) ^ place, axis=1)
    rows = rows.reshape(PLANES, 1 << lay.y_bits, 1 << lay.x_bits, 2, lay.half, 128)
    sides = [jnp.take(rows, side, axis=3) for side in (core, 1 - core)]
    return [[list(side[p]) for p in range(PLANES)] for side in sides]


def add(left, right):
    return left.astype(F32) + right.astype(F32)


def on_device(lay, canon, tokens_in, positions, params, cotangent):
    index = lax.axis_index("dp")
    core = lax.axis_index("rep")
    n, half, in_plane = lay.count, lay.half, lay.in_plane
    plane, place = index // in_plane, index % in_plane
    same = n == CANON
    firsts, seconds = hops(lay)
    forward, attention_back = layer_kernels(*tokens_in.shape)
    mine = pack_own(params, index, core, lay)
    angles = tables(positions)
    if same:
        idx = jnp.stack([plane, place, core, 1]).astype(jnp.int32)
        pieces, angles = balanced_gather(mine, lay, angles)
    else:
        idx = jnp.zeros((4,), jnp.int32)
        blocks = gather(mine, lay)
        twins = [[swap_rep(block) for block in value] for value in blocks]
        pieces = canonical(blocks, twins, lay, canon, index, core)
    results = forward(idx, *pieces, tokens_in.T, *angles, cotangent.T)
    d_gain = results[2]
    saved, slots, held = results[:13], (results[13:17], results[17:21]), results[21:23]
    if same:
        (first,), (second,) = firsts, seconds
        moved = [hop(add(far, swap_rep(send)).astype(BF16), second, n) for _, far, _, send in slots]
        near = [add(keep, swap_rep(send)) for keep, _, send, _ in slots]
    output, d_input, *results = attention_back(idx, tokens_in.T, *angles, *saved, *held)
    output, d_input = output.T, d_input.T
    keep_near, keep_far, send_near, send_far, keep, send = results
    if same:
        moved, send_far, send_near, send = lax.optimization_barrier((moved, send_far, send_near, send))
        third = hop(add(keep_far, swap_rep(send_far)).astype(BF16), second, n)
        early = [(near[j] + moved[j].astype(F32)).astype(BF16) for j in range(2)]
        early = [add(value[0], hop(value[1], first, n)).astype(BF16) for value in early]
        third = (add(keep_near, swap_rep(send_near)) + third.astype(F32)).astype(BF16)
        third = add(third[0], hop(third[1], first, n)).astype(BF16)
        mine = add(keep, swap_rep(send)).astype(BF16)

        def pick(values, s):
            table = ((0, 1, 2), (2, 1, 0), (1, 2, 0), (1, 0, 2))
            result = values[table[3][s - 1]]
            for z in range(3):
                result = jnp.where(plane == z, values[table[z][s - 1]], result)
            return result

        mine, third = lax.optimization_barrier((mine, third))
        planes = early + [third]
        parts = [swap(pick(planes, s), s << (lay.bits - 2), n) for s in range(1, PLANES)]
        both = tuple(a ^ b for a, b in zip(first, second))
        inner = [hop(mine[d], masks, n) for d, masks in ((1, first), (2, second), (3, both))]
        parts, inner = lax.optimization_barrier((parts, inner))
        total = (add(mine[0], inner[0]) + add(inner[1], inner[2])) + (
            parts[0].astype(F32) + add(parts[1], parts[2])
        )
    else:
        slots = [(near, far, other, last) for near, far, other, last in slots]
        slots.append((keep_near, keep_far, send_near, send_far))
        planes = [(keep, send)]
        for near, far, other, last in slots:
            planes.append((jnp.concatenate([near, far], 0), jnp.concatenate([other, last], 0)))
        keeps, sends = from_canonical(planes, lay, canon, place, core)
        moved = []
        for keep, send in zip(keeps, sends):
            pair = pair_sum(keep, send)
            moved.append(add_blocks(pair[0], send_blocks(pair, seconds, n)))
        blocks = split_first(moved, lay)
        planes = add_blocks(blocks[0], send_blocks(blocks, firsts, n))
        total = reduce_planes(planes, plane, lay)
    other = swap_rep(total)
    if same:
        at = ROWS + 26 - HALF
        d_gain = jnp.where(core == 1, total[at : at + 5], other[at : at + 5]).reshape(-1)[: lay.width]
    else:
        d_gain = sum_everywhere(d_gain[0], lay)
    return output, d_input, unpack_own(total, other, index, core, lay), d_gain


def solution(mesh):
    def run(tokens_in, positions, params, cotangent):
        total, width = params.shape[0], tokens_in.shape[1]
        lay = Layout(mesh.shape["dp"], total, width)
        canon = Layout(CANON, total, width)
        rows = P(("dp", "rep"), None)
        return jax.shard_map(
            lambda *args: on_device(lay, canon, *args),
            mesh=mesh,
            in_specs=(rows, P(("dp", "rep")), P("dp"), rows),
            out_specs=(rows, rows, P("dp"), P()),
            check_vma=False,
        )(tokens_in, positions, params, cotangent)

    return run
```

```python
import jax
import jax.numpy as jnp
from jax import lax
from jax.experimental import pallas as pl
from jax.experimental.pallas import tpu as pltpu
from jax.sharding import PartitionSpec as P

HEADS = 9
KV_HEADS = 3
HEAD = 64
FF = 1536
SEQ_LEN = 128
PLANES = 4
CANON = 16

EPS = 1e-05
ROPE_BASE = 100000.0

F32, BF16 = jnp.float32, jnp.bfloat16
ROWS, HALF = 1728, 880
MAIN, REST = 768, 112
NARROW, WIDE = 384, 144
VMEM_LIMIT = 52 * 1024 * 1024


class Layout:
    def __init__(self, count, total, width):
        self.count = count
        self.width = width
        self.gains = 2 * width
        self.shard = total // count
        self.chunk = (total - self.gains) // count
        self.step = self.gains // count
        self.rows = self.chunk // 128
        half = -(-(self.rows + 10) // 2)
        self.half = -(-half // 16) * 16
        self.first = -(-(self.half // 2) // 16) * 16
        self.extra = 2 * self.half - self.rows
        self.bits = count.bit_length() - 1
        rest = self.bits - 2
        self.x_bits = -(-rest // 2)
        self.y_bits = rest - self.x_bits
        self.in_plane = 1 << rest
        self.flip = self.x_bits == self.y_bits


def pack_wide(flat, width):
    panels = width // 128
    return flat.reshape(-1, panels, 128).transpose(1, 0, 2).reshape(-1, 128)


def unpack_wide(rows, width):
    panels = width // 128
    return rows.reshape(panels, -1, 128).transpose(1, 0, 2).reshape(-1)


def pack_narrow(flat):
    rows = flat.reshape(-1, 576)
    count = rows.shape[0]
    panels = rows[:, :512].reshape(count, 4, 128).transpose(1, 0, 2).reshape(-1, 128)
    tail = rows[:, 512:]
    return jnp.concatenate([panels, jnp.concatenate([tail[: count // 2], tail[count // 2 :]], 1)], 0)


def unpack_narrow(packed):
    count = packed.shape[0] * 2 // 9
    panels = packed[: 4 * count].reshape(4, count, 128).transpose(1, 0, 2).reshape(count, 512)
    half = packed[4 * count :]
    tail = jnp.concatenate([half[:, :64], half[:, 64:]], 0)
    return jnp.concatenate([panels, tail], 1).reshape(-1)


def head_narrow(flat):
    rows = flat.reshape(2, 576)
    tail = jnp.pad(rows[:, 512:], ((0, 0), (64, 0)))
    return jnp.concatenate([rows[:, :512].reshape(8, 128), tail], 0)


def unhead_narrow(rows):
    return jnp.concatenate([rows[:8].reshape(2, 512), rows[8:10, 64:]], 1).reshape(-1)


def head_wide(flat):
    return jnp.pad(flat.reshape(9, 128), ((0, 1), (0, 0)))


def unhead_wide(rows):
    return rows[:9].reshape(-1)


def is_wide(index, count):
    return (index >= count // 4) & (index < 3 * count // 4)


def pack_payload(window, index, lay):
    head, chunk = window[: lay.gains], window[lay.gains :]
    body = jnp.where(is_wide(index, lay.count), pack_wide(chunk, FF), pack_narrow(chunk))
    top = jnp.where(is_wide(index - 1, lay.count), head_wide(head), head_narrow(head))
    return jnp.concatenate([body, jnp.pad(top, ((0, lay.extra - 10), (0, 0)))], 0)


def unpack_payload(rows, index, lay):
    body, top = rows[: lay.rows], rows[lay.rows : lay.rows + 10]
    chunk = jnp.where(is_wide(index, lay.count), unpack_wide(body, FF), unpack_narrow(body))
    head = jnp.where(is_wide(index - 1, lay.count), unhead_wide(top), unhead_narrow(top))
    return jnp.concatenate([head, chunk])


def swap(value, mask, count):
    return lax.ppermute(value, "dp", [(i, i ^ mask) for i in range(count)])


def swap_rep(value):
    return lax.ppermute(value, "rep", [(0, 1), (1, 0)])


def hop(value, masks, count):
    pairs = [(2 * i + c, 2 * (i ^ masks[c]) + c) for i in range(count) for c in range(2)]
    return lax.ppermute(value, ("dp", "rep"), pairs)


def hops(lay):
    xs = [d for d in range(1, 1 << lay.x_bits)]
    ys = [e << lay.x_bits for e in range(1, 1 << lay.y_bits)]
    if lay.flip:
        return list(zip(xs, ys)), list(zip(ys, xs))
    return list(zip(xs, xs)), list(zip(ys, ys))


def gather_hops(value, masks, count):
    return jnp.stack([value] + [hop(value, pair, count) for pair in masks], 0)


def gather(half, lay):
    n = lay.count
    first, second = hops(lay)
    planes = [half] + [swap(half, s << (lay.bits - 2), n) for s in range(1, PLANES)]
    blocks = []
    for plane in planes:
        block = gather_hops(plane, first, n)
        blocks.append([block] + [hop(block, masks, n) for masks in second])
    return blocks


def balanced_gather(half, lay, beside):
    n = lay.count
    (first,), (second,) = hops(lay)
    both = tuple(a ^ b for a, b in zip(first, second))
    across = [swap(half, s << (lay.bits - 2), n) for s in range(1, PLANES)]
    plane = [hop(half, masks, n) for masks in (first, second, both)]
    across, plane, beside = lax.optimization_barrier((across, plane, beside))
    own = jnp.stack([half] + plane, 0)
    near = [jnp.stack([value, hop(value, first, n)], 0) for value in across]
    far = [hop(value, second, n) for value in near]
    early = [own] + near
    far[0], twins = lax.optimization_barrier(
        (far[0], [swap_rep(value) for value in early + far[1:]])
    )
    return early + far + twins[:4] + [swap_rep(far[0])] + twins[4:], beside


def pair_sum(keep, send):
    return [
        (mine.astype(F32) + swap_rep(other).astype(F32)).astype(BF16)
        for mine, other in zip(keep, send)
    ]


def send_blocks(blocks, masks, count):
    return [hop(block, pair, count) for block, pair in zip(blocks[1:], masks)]


def add_blocks(block, arrived):
    total = block.astype(F32)
    for value in arrived:
        total = total + value.astype(F32)
    return total.astype(BF16)


def split_first(planes, lay):
    return [jnp.stack([value[j] for value in planes], 0) for j in range(len(hops(lay)[0]) + 1)]


def reduce_planes(planes, plane, lay):
    parts = [jnp.take(planes, plane, axis=0).astype(F32)]
    for s in range(1, PLANES):
        part = swap(jnp.take(planes, plane ^ s, axis=0), s << (lay.bits - 2), lay.count)
        parts.append(part.astype(F32))
    return (parts[0] + parts[1]) + (parts[2] + parts[3])


def sum_everywhere(value, lay):
    value = value + swap_rep(value)
    for bit in range(lay.bits):
        value = value + swap(value, 1 << bit, lay.count)
    return value


def rope_tables(places):
    expon = jnp.arange(HEAD // 2).astype(jnp.float32) * (2.0 / HEAD)
    inverse = jnp.power(ROPE_BASE, -expon)
    angle = places.astype(jnp.float32)[..., None] * inverse
    return (jnp.cos(angle), jnp.sin(angle))


def dot(left, right):
    return jnp.dot(left, right, preferred_element_type=F32)


def dot_nt(left, right):
    return lax.dot_general(left, right, (((1,), (1,)), ((), ())), preferred_element_type=F32)


def dot_tn(left, right):
    return lax.dot_general(left, right, (((0,), (0,)), ((), ())), preferred_element_type=F32)


def row_of_head(head, which):
    parts = [head[4 * which + j : 4 * which + j + 1] for j in range(4)]
    return jnp.concatenate(parts + [head[8 + which : 9 + which, 64:]], 1)


def head_of_rows(rows):
    parts = [row[:, 128 * j : 128 * j + 128] for row in rows for j in range(4)]
    zeros = jnp.zeros((1, 64), F32)
    parts = parts + [jnp.concatenate([zeros, row[:, 512:]], 1) for row in rows]
    return jnp.concatenate(parts + [jnp.zeros((6, 128), F32)], 0)


def gain_rows(gain, low):
    parts = [gain[:, 128 * j : 128 * j + 128] for j in range(4)]
    parts = parts + [jnp.concatenate([gain[:, 512:], gain[:, 512:]], 1)]
    return jnp.concatenate([low[:10]] + parts + [jnp.zeros((1, 128), F32)], 0)


def load_narrow(ref, index):
    parts = [ref[index, NARROW * j : NARROW * (j + 1), :] for j in range(4)]
    half = ref[index, 4 * NARROW : ROWS, :]
    tail = jnp.concatenate([half[:, :64], half[:, 64:]], 0)
    return jnp.concatenate(parts + [tail], 1)


def store_narrow(ref, index, value):
    for j in range(4):
        ref[index, NARROW * j : NARROW * (j + 1), :] = value[:, 128 * j : 128 * (j + 1)].astype(BF16)
    tail = value[:, 512:]
    tail = jnp.concatenate([tail[: NARROW // 2], tail[NARROW // 2 :]], 1)
    ref[index, 4 * NARROW : ROWS, :] = tail.astype(BF16)


def narrow_tiles():
    tiles = [(NARROW * (j + 1) - 16, j, 4 + j) for j in range(4)]
    return tiles + [(ROWS - 16, 8, 9)]


def add_tail(ref, index, wide):
    head = ref[index + 1, ROWS : ROWS + 16, :].astype(F32)
    row = lax.broadcasted_iota(jnp.int32, (16, 128), 0)
    if wide:
        for k in range(9):
            at = WIDE * (4 + k) - 16
            tile = ref[index, at : at + 16, :].astype(F32)
            tile = tile + jnp.where(row == 15, head[k : k + 1], 0.0)
            ref[index, at : at + 16, :] = tile.astype(BF16)
    else:
        for at, upper, lower in narrow_tiles():
            tile = ref[index, at : at + 16, :].astype(F32)
            tile = tile + jnp.where(row == 14, head[upper : upper + 1], 0.0)
            tile = tile + jnp.where(row == 15, head[lower : lower + 1], 0.0)
            ref[index, at : at + 16, :] = tile.astype(BF16)


def tail_of(ref, index, wide):
    if wide:
        parts = []
        for k in range(9):
            at = WIDE * (4 + k) - 16
            parts.append(ref[index, at : at + 16, :].astype(F32)[15:16])
        return jnp.concatenate(parts + [jnp.zeros((7, 128), F32)], 0)
    tiles = [ref[index, at : at + 16, :].astype(F32) for at, _, _ in narrow_tiles()]
    parts = [tile[14:15] for tile in tiles[:4]] + [tile[15:16] for tile in tiles[:4]]
    parts = parts + [tiles[4][14:15], tiles[4][15:16]]
    return jnp.concatenate(parts + [jnp.zeros((6, 128), F32)], 0)


def spread(value, first, second, out):
    for m in range(3):
        part = value[:, 192 * m : 192 * (m + 1)].astype(F32)
        first[pl.ds(m, 192, stride=3), :] = part[:, :128]
        second[pl.ds(m, 192, stride=3), :] = jnp.concatenate([part[:, 128:], part[:, 128:]], 1)
    out[:, :128] = first[...].astype(BF16)
    out[:, 128:] = second[:, :64].astype(BF16)


def unspread(value, first, second):
    first[...] = value[:, :128]
    second[...] = jnp.concatenate([value[:, 128:], value[:, 128:]], 1)
    parts = []
    for m in range(3):
        parts.append(first[pl.ds(m, 192, stride=3), :])
        parts.append(second[pl.ds(m, 192, stride=3), :][:, :64])
    return jnp.concatenate(parts, 1)


def turn(vector, cosine, sine):
    swapped = jnp.concatenate([vector[:, 32:], vector[:, :32]], 1)
    return vector * cosine + swapped * sine


def piece_copies(idx, at_plane, sides, dst, sem, outward):
    place, core, flip = idx[1], idx[2], idx[3]
    copies = []
    for which, refs in enumerate(sides):
        side = jnp.bitwise_xor(core, which)
        for d in range(4):
            turned = ((d & 1) << 1) | (d >> 1)
            chunk = 4 * at_plane + jnp.bitwise_xor(place, jnp.where(side * flip == 1, turned, d))
            ref = refs[0].at[d] if len(refs) == 1 else refs[d // 2].at[d % 2]
            for start, rows in ((0, MAIN), (MAIN, REST)) if outward else ((0, HALF),):
                outer = ref.at[pl.ds(start, rows), :]
                at = pl.multiple_of(side * HALF + start, 16)
                inner = dst.at[chunk, pl.ds(at, rows), :]
                pair = (inner, outer) if outward else (outer, inner)
                copies.append((start > 0, pltpu.make_async_copy(pair[0], pair[1], sem)))
    return copies


def wait_plane(ref, base, sem):
    whole = ref.at[pl.ds(base, 4)]
    pltpu.make_async_copy(whole, whole, sem).wait()


def slot_plane(plane, slot):
    own = jnp.where(plane == 0, 3, plane)
    low = jnp.where(own == 1, 2, 1)
    return [low, 6 - own - low, own][slot]


def first_kernel(idx, *refs):
    pieces = list(zip(refs[:7], refs[7:14]))
    tok_hbm, cos, sin, cot_hbm = refs[14:18]
    refs = refs[18:]
    results, outs = refs[:13], refs[13:23]
    refs = refs[23:]
    y_acc, dr_out, dg_out, att_out, p_out, q_out, k_out, v_out, wq, wk, wv, wo, gain_out = refs[:13]
    w, g, tok, cot_t, cot, att, n2_ref, n2t_ref, dn_acc, first, second = refs[13:24]
    in_sem, sems, out_sems, result_sems = refs[24:]
    saves = [
        pltpu.make_async_copy(src, dst, result_sems.at[i])
        for i, (src, dst) in enumerate(zip(refs[:13], results))
    ]
    load = pltpu.make_async_copy(tok_hbm, tok, in_sem.at[0])
    load.start()
    load_cot = pltpu.make_async_copy(cot_hbm, cot_t, in_sem.at[1])
    load_cot.start()
    planes = []
    for s in range(PLANES):
        sides = [[ref] for ref in pieces[0]]
        if s:
            sides = list(zip(pieces[s], pieces[s + 3]))
        at_plane = jnp.bitwise_xor(idx[0], s)
        copies = piece_copies(idx, at_plane, sides, w, sems.at[at_plane], False)
        planes.append([copy for _, copy in copies])
    for p in range(PLANES):
        for s in range(PLANES):

            @pl.when(jnp.bitwise_xor(idx[0], s) == p)
            def _(copies=planes[s]):
                for copy in copies:
                    copy.start()

    tokens = tok.shape[1]
    load.wait()
    x = tok[...].astype(F32).T
    normed = x * lax.rsqrt(jnp.mean(x * x, -1, keepdims=True) + EPS)
    load_cot.wait()
    cot[...] = cot_t[...].astype(F32).T.astype(BF16)
    wait_plane(w, 0, sems.at[0])
    for c in range(3):
        add_tail(w, c, False)
    gains = w[0, ROWS : ROWS + 16, :].astype(F32)
    gain_in, gain_mid = row_of_head(gains, 0), row_of_head(gains, 1)
    gain_out[...] = gain_in
    n1 = (normed * gain_in).astype(BF16)
    wq[:NARROW, :] = load_narrow(w, 0)
    mixed_chunk = load_narrow(w, 1)
    wq[NARROW:, :] = mixed_chunk[:192]
    spread(mixed_chunk[192:], first, second, wk)
    mixed_chunk = load_narrow(w, 2)
    spread(mixed_chunk[:192], first, second, wv)
    wo[:192, :] = mixed_chunk[192:]

    query, keys, values = dot(n1, wq[...]), dot(n1, wk[...]), dot(n1, wv[...])
    row = lax.broadcasted_iota(jnp.int32, (3 * SEQ_LEN, SEQ_LEN), 0)
    causal = jnp.bitwise_and(row, SEQ_LEN - 1) >= lax.broadcasted_iota(
        jnp.int32, (3 * SEQ_LEN, SEQ_LEN), 1
    )
    for b in range(tokens // SEQ_LEN):
        part = slice(SEQ_LEN * b, SEQ_LEN * (b + 1))
        cosine, sine = cos[part, :], sin[part, :]
        for kv in range(KV_HEADS):
            at = KV_HEADS * b + kv
            heads = [
                turn(query[part, HEAD * h : HEAD * (h + 1)], cosine, sine)
                for h in range(3 * kv, 3 * kv + 3)
            ]
            q3 = jnp.concatenate(heads, 0).astype(BF16)
            k1 = turn(keys[part, HEAD * kv : HEAD * (kv + 1)], cosine, sine).astype(BF16)
            v1 = values[part, HEAD * kv : HEAD * (kv + 1)].astype(BF16)
            q_out[at], k_out[at], v_out[at] = q3, k1, v1
            score = jnp.where(causal, dot_nt(q3, k1) * HEAD**-0.5, -1e30)
            expon = jnp.exp(score - jnp.max(score, -1, keepdims=True))
            probs = expon / jnp.sum(expon, -1, keepdims=True)
            p_out[at] = probs
            mix = dot(probs.astype(BF16), v1)
            for r in range(3):
                h = 3 * kv + r
                att[part, HEAD * h : HEAD * (h + 1)] = mix[SEQ_LEN * r : SEQ_LEN * (r + 1)]
    attended = att[...].astype(BF16)
    att_out[...] = attended
    wait_plane(w, 4, sems.at[1])
    add_tail(w, 3, False)
    wo[192:, :] = load_narrow(w, 3)
    for copy in saves[3:]:
        copy.start()
    mixed = x + dot(attended, wo[...])
    inverse = lax.rsqrt(jnp.mean(mixed * mixed, -1, keepdims=True) + EPS)
    normed_mid = mixed * inverse
    n2 = normed_mid * gain_mid
    n2_ref[...] = n2.astype(BF16)
    n2t_ref[...] = n2.astype(BF16).astype(F32).T.astype(BF16)
    y_acc[...] = mixed
    dn_acc[...] = jnp.zeros_like(dn_acc)
    wait_plane(w, 8, sems.at[2])
    wait_plane(w, 12, sems.at[3])

    def fix(i, carry):
        add_tail(w, i + 4, True)
        return carry

    lax.fori_loop(0, 8, fix, 0)
    for c in (12, 13, 14):
        add_tail(w, c, False)

    def block(k, carry):
        def wide(base, p):
            at = pl.multiple_of((6 * k + p) * WIDE, 16)
            return jnp.concatenate([w[base + d, pl.ds(at, WIDE), :] for d in range(4)], 0)

        w_gate = jnp.concatenate([wide(4, p) for p in range(6)], 1)
        w_up = jnp.concatenate([wide(8, p) for p in range(6)], 1)
        w_down = jnp.concatenate([load_narrow(w, 12 + 2 * k), load_narrow(w, 13 + 2 * k)], 0)
        c = cot[...]
        gate, up = dot(n2_ref[...], w_gate), dot(n2_ref[...], w_up)
        sigma = 1.0 / (1.0 + jnp.exp(-gate))
        silu = gate * sigma
        hidden = (silu * up).astype(BF16)
        y_acc[...] += dot(hidden, w_down)
        d_down = dot_tn(hidden, c)
        store_narrow(g, 8 + 2 * k, d_down[:NARROW])
        store_narrow(g, 9 + 2 * k, d_down[NARROW:])
        d_hidden = dot_nt(c, w_down)
        d_gate = (d_hidden * up * sigma * (1.0 + gate * (1.0 - sigma))).astype(BF16)
        d_up = (d_hidden * silu).astype(BF16)
        dn_acc[...] += dot_nt(d_gate, w_gate) + dot_nt(d_up, w_up)
        for base, d_out in ((0, d_gate), (4, d_up)):
            grad = dot(n2t_ref[...], d_out).astype(BF16)
            for p in range(6):
                at = pl.multiple_of((6 * k + p) * WIDE, 16)
                for d in range(4):
                    g[base + d, pl.ds(at, WIDE), :] = grad[
                        WIDE * d : WIDE * (d + 1), 128 * p : 128 * (p + 1)
                    ]
        return carry

    lax.fori_loop(0, 2, block, 0)
    stores = []
    for slot in range(3):
        sides = [outs[4 * slot : 4 * slot + 2], outs[4 * slot + 2 : 4 * slot + 4]]
        if slot == 2:
            sides = [outs[8:9], outs[9:10]]
        at_plane = slot_plane(idx[0], slot) - 1
        stores = stores + piece_copies(idx, at_plane, sides, g, out_sems.at[slot], True)
    for last, copy in stores:
        if not last:
            copy.start()
    d_norm = dn_acc[...]
    d_gain = jnp.sum(d_norm * normed_mid, 0, keepdims=True)
    dg_out[...] = d_gain
    scaled = d_norm * gain_mid
    d_mixed = cot[...].astype(F32) + inverse * (
        scaled - normed_mid * jnp.mean(scaled * normed_mid, -1, keepdims=True)
    )
    last_rows = dot_tn(att_out[:, 512:], d_mixed.astype(BF16))
    for c in range(12):
        if c:
            top = tail_of(g, c - 1, c - 1 < 8)
        else:
            top = head_of_rows([last_rows[62:63], last_rows[63:64]])
        g[c, ROWS : ROWS + 16, :] = top.astype(BF16)
        g[c, ROWS + 16 :, :] = gain_rows(d_gain, jnp.zeros((16, 128), F32)).astype(BF16)
    for last, copy in stores:
        if last:
            copy.start()
    dr_out[...] = d_mixed
    for copy in saves[:3]:
        copy.start()
    for copy in saves:
        copy.wait()
    for slot in range(3):
        wait_plane(g, 4 * slot, out_sems.at[slot])


def second_kernel(idx, *refs):
    tok, cos, sin, y_in, dr, dg, att, p_in, q_in, k_in, v_in, wq, wk, wv, wo, gain = refs[:16]
    held, (y_out, dx_out), third, mine = refs[16:18], refs[18:20], refs[20:24], refs[24:26]
    g, bounce, y_t, dx_t, dq_ref, dk_ref, dv_ref, first, second, in_sem, out_sems, held_sem = refs[26:]
    tokens = tok.shape[1]
    ground = idx[0] == 0
    fetch = [
        pltpu.make_async_copy(held[side], bounce.at[side], held_sem.at[side]) for side in range(2)
    ]

    @pl.when(ground)
    def _():
        for copy in fetch:
            copy.start()

    d_mixed = dr[...]
    branch = d_mixed.astype(BF16)
    dw_out = dot_tn(att[...], branch)
    d_att = dot_nt(branch, wo[...])
    @pl.when(ground)
    def _():
        for copy in fetch:
            copy.wait()
        for side in range(2):
            for j in range(2):
                source = bounce.at[side, pl.ds(2 * j, 2)]
                pltpu.make_async_copy(source, third[2 * side + j], held_sem.at[2]).start()

    for b in range(tokens // SEQ_LEN):
        part = slice(SEQ_LEN * b, SEQ_LEN * (b + 1))
        cosine, sine = cos[part, :], -sin[part, :]
        for kv in range(KV_HEADS):
            at = KV_HEADS * b + kv
            heads = [d_att[part, HEAD * h : HEAD * (h + 1)] for h in range(3 * kv, 3 * kv + 3)]
            d3 = jnp.concatenate(heads, 0).astype(BF16)
            probs, q3, k1, v1 = p_in[at], q_in[at], k_in[at], v_in[at]
            d_probs = dot_nt(d3, v1)
            dv_ref[part, HEAD * kv : HEAD * (kv + 1)] = dot_tn(probs.astype(BF16), d3)
            inner = jnp.sum(d_probs * probs, -1, keepdims=True)
            d_score = (probs * (d_probs - inner)).astype(BF16)
            dq3 = dot(d_score, k1) * HEAD**-0.5
            for r in range(3):
                h = 3 * kv + r
                dq_ref[part, HEAD * h : HEAD * (h + 1)] = turn(
                    dq3[SEQ_LEN * r : SEQ_LEN * (r + 1)], cosine, sine
                )
            dk_ref[part, HEAD * kv : HEAD * (kv + 1)] = turn(
                dot_tn(d_score, q3) * HEAD**-0.5, cosine, sine
            )
    dq, dk, dv = dq_ref[...].astype(BF16), dk_ref[...].astype(BF16), dv_ref[...].astype(BF16)
    x = tok[...].astype(F32)
    inverse = lax.rsqrt(jnp.mean(x * x, 0, keepdims=True) + EPS)
    normed = x * inverse
    gain_column = jnp.broadcast_to(gain[...], (8, gain.shape[1])).T[:, :1]
    n1t = (normed * gain_column).astype(BF16)
    dw_query = dot(n1t, dq)
    store_narrow(g, 0, dw_query[:NARROW])
    dw = unspread(dot(n1t, dk), first, second)
    store_narrow(g, 1, jnp.concatenate([dw_query[NARROW:], dw], 0))
    dw = unspread(dot(n1t, dv), first, second)
    store_narrow(g, 2, jnp.concatenate([dw, dw_out[:192]], 0))
    store_narrow(g, 3, dw_out[192:])
    d_norm = dot_nt(wq[...], dq) + dot_nt(wk[...], dk) + dot_nt(wv[...], dv)
    d_gain = jnp.sum(d_norm * normed, 1, keepdims=True)
    d_gain = jnp.broadcast_to(d_gain, (d_gain.shape[0], 128)).T[:1]
    for c in range(4):
        top = tail_of(g, c - 1, False) if c else head_of_rows([d_gain, dg[...]])
        g[c, ROWS : ROWS + 16, :] = top.astype(BF16)
        g[c, ROWS + 16 :, :] = gain_rows(dg[...], jnp.zeros((16, 128), F32)).astype(BF16)

    @pl.when(ground)
    def _():
        for _, copy in piece_copies(idx, 0, [mine[:1], mine[1:]], g, out_sems.at[0], True):
            copy.start()

    @pl.when(jnp.logical_not(ground))
    def _():
        for _, copy in piece_copies(idx, 0, [third[:2], third[2:]], g, out_sems.at[0], True):
            copy.start()

    scaled = d_norm * gain_column
    dx_t[...] = d_mixed.T + inverse * (
        scaled - normed * jnp.mean(scaled * normed, 0, keepdims=True)
    )
    y_t[...] = y_in[...].T.astype(BF16)
    stores = [
        pltpu.make_async_copy(src, dst, in_sem.at[i])
        for i, (src, dst) in enumerate(((dx_t, dx_out), (y_t, y_out)))
    ]
    for copy in stores:
        copy.start()
    for copy in stores:
        copy.wait()
    wait_plane(g, 0, out_sems.at[0])

    @pl.when(ground)
    def _():
        wait_plane(g, 0, held_sem.at[2])


def halves_turned(low, high):
    lane = lax.broadcasted_iota(jnp.int32, low.shape, 1)
    return jnp.where(lane < 64, pltpu.roll(low, 64, 1), pltpu.roll(high, 64, 1))


def pack_kernel(idx, flat, out, rolled, window, packed, mixed):
    index, core, down, right = idx[0], idx[1], idx[2], idx[3]
    lane = lax.broadcasted_iota(jnp.int32, (1, 128), 1)
    rolled[0:16, :] = jnp.zeros((16, 128), F32)
    rolled[16:1752, :] = pltpu.roll(flat[...].astype(F32), right, 1)
    rolled[1752:1760, :] = jnp.zeros((8, 128), F32)
    window[...] = jnp.where(
        lane >= right, rolled[pl.ds(16 - down, 1744), :], rolled[pl.ds(15 - down, 1744), :]
    )
    head = [window[k : k + 1, :] for k in range(9)]
    wide = (index >= 4) & (index < 12)

    @pl.when(wide)
    def _():
        for j in range(12):
            packed[WIDE * j : WIDE * (j + 1), :] = window[pl.ds(9 + j, WIDE, stride=12), :]

    @pl.when(jnp.logical_not(wide))
    def _():
        parts = [window[pl.ds(9 + k, NARROW // 2, stride=9), :] for k in range(9)]
        for j in range(4):
            packed[pl.ds(NARROW * j, NARROW // 2, stride=2), :] = parts[j]
            packed[pl.ds(NARROW * j + 1, NARROW // 2, stride=2), :] = halves_turned(
                parts[4 + j], parts[5 + j]
            )
        mixed[pl.ds(0, NARROW // 2, stride=2), :] = parts[4]
        mixed[pl.ds(1, NARROW // 2, stride=2), :] = pltpu.roll(parts[8], 64, 1)
        packed[4 * NARROW : ROWS, :] = jnp.where(
            lane < 64, mixed[: NARROW // 2, :], pltpu.roll(mixed[NARROW // 2 :, :], 64, 1)
        )

    last = jnp.zeros((23, 128), F32)
    after_wide = (index >= 5) & (index < 13)

    @pl.when(after_wide)
    def _():
        packed[ROWS:, :] = jnp.concatenate(head + [last], 0)

    @pl.when(jnp.logical_not(after_wide))
    def _():
        rows = head[:4] + [halves_turned(head[4 + j], head[5 + j]) for j in range(4)]
        rows.append(jnp.where(lane < 64, 0.0, pltpu.roll(head[4], 64, 1)))
        rows.append(jnp.where(lane < 64, 0.0, head[8]))
        packed[ROWS:, :] = jnp.concatenate(rows + [last[:22]], 0)

    out[...] = packed[pl.ds(pl.multiple_of(core * HALF, 16), HALF), :].astype(BF16)


def unpack_kernel(idx, own, twin, out, packed, window, mixed):
    index, core, down, left = idx[0], idx[1], idx[2], idx[3]
    lane = lax.broadcasted_iota(jnp.int32, (1, 128), 1)
    packed[pl.ds(pl.multiple_of(core * HALF, 16), HALF), :] = own[...]
    packed[pl.ds(pl.multiple_of((1 - core) * HALF, 16), HALF), :] = twin[...]
    head = [packed[ROWS + k : ROWS + k + 1, :] for k in range(10)]
    window[1737:, :] = jnp.zeros((15, 128), F32)
    wide = (index >= 4) & (index < 12)

    @pl.when(wide)
    def _():
        for j in range(12):
            window[pl.ds(9 + j, WIDE, stride=12), :] = packed[WIDE * j : WIDE * (j + 1), :]

    @pl.when(jnp.logical_not(wide))
    def _():
        half = packed[4 * NARROW : ROWS, :]
        mixed[: NARROW // 2, :] = half
        mixed[NARROW // 2 :, :] = pltpu.roll(half, 64, 1)
        odd = []
        for j in range(4):
            window[pl.ds(9 + j, NARROW // 2, stride=9), :] = packed[
                pl.ds(NARROW * j, NARROW // 2, stride=2), :
            ]
            odd.append(pltpu.roll(packed[pl.ds(NARROW * j + 1, NARROW // 2, stride=2), :], 64, 1))
        odd.append(mixed[pl.ds(1, NARROW // 2, stride=2), :])
        before = mixed[pl.ds(0, NARROW // 2, stride=2), :]
        for j in range(4):
            window[pl.ds(13 + j, NARROW // 2, stride=9), :] = jnp.where(lane < 64, before, odd[j])
            before = odd[j]
        window[pl.ds(17, NARROW // 2, stride=9), :] = jnp.where(
            lane < 64, before, pltpu.roll(odd[4], 64, 1)
        )

    after_wide = (index >= 5) & (index < 13)

    @pl.when(after_wide)
    def _():
        window[0:9, :] = jnp.concatenate(head[:9], 0)

    @pl.when(jnp.logical_not(after_wide))
    def _():
        odd = [pltpu.roll(row, 64, 1) for row in head[4:8]]
        before, rows = pltpu.roll(head[8], 64, 1), head[:4]
        for j in range(4):
            rows.append(jnp.where(lane < 64, before, odd[j]))
            before = odd[j]
        rows.append(jnp.where(lane < 64, before, head[9]))
        window[0:9, :] = jnp.concatenate(rows, 0)

    lanes = pltpu.roll(window[...], jnp.bitwise_and(128 - left, 127), 1)
    window[...] = lanes
    out[...] = jnp.where(
        lane < 128 - left, window[pl.ds(down, 1736), :], window[pl.ds(down + 1, 1736), :]
    )


def chunk_index(index, core, lay):
    start = index * lay.step
    return jnp.stack([index, core, start // 128, start % 128]).astype(jnp.int32)


def pack_own(params, index, core, lay):
    if lay.count != CANON:
        window = jnp.zeros((lay.gains + lay.chunk,), params.dtype)
        window = lax.dynamic_update_slice(window, params, (index * lay.step,))
        payload = pack_payload(window, index, lay)
        return lax.dynamic_slice_in_dim(payload, core * lay.half, lay.half, 0)
    flat = jnp.pad(params, (0, 1736 * 128 - lay.shard)).reshape(1736, 128)
    vmem = pl.BlockSpec(memory_space=pltpu.VMEM)
    return pl.pallas_call(
        pack_kernel,
        name="pack_own_chunk",
        in_specs=[pl.BlockSpec(memory_space=pltpu.SMEM), vmem],
        out_specs=vmem,
        out_shape=jax.ShapeDtypeStruct((HALF, 128), BF16),
        scratch_shapes=[
            pltpu.VMEM((1760, 128), F32),
            pltpu.VMEM((1744, 128), F32),
            pltpu.VMEM((2 * HALF, 128), F32),
            pltpu.VMEM((NARROW, 128), F32),
        ],
        compiler_params=pltpu.CompilerParams(vmem_limit_bytes=VMEM_LIMIT),
    )(chunk_index(index, core, lay), flat)


def unpack_own(own, twin, index, core, lay):
    if lay.count != CANON:
        rows = jnp.where(core == 0, jnp.stack([own, twin], 0), jnp.stack([twin, own], 0))
        window = unpack_payload(rows.reshape(2 * lay.half, 128), index, lay)
        return lax.dynamic_slice(window, (index * lay.step,), (lay.shard,))
    vmem = pl.BlockSpec(memory_space=pltpu.VMEM)
    rows = pl.pallas_call(
        unpack_kernel,
        name="unpack_own_chunk",
        in_specs=[pl.BlockSpec(memory_space=pltpu.SMEM), vmem, vmem],
        out_specs=vmem,
        out_shape=jax.ShapeDtypeStruct((1736, 128), F32),
        scratch_shapes=[
            pltpu.VMEM((2 * HALF, 128), F32),
            pltpu.VMEM((1752, 128), F32),
            pltpu.VMEM((NARROW, 128), F32),
        ],
        compiler_params=pltpu.CompilerParams(vmem_limit_bytes=VMEM_LIMIT),
    )(chunk_index(index, core, lay), own, twin)
    return rows.reshape(-1)[: lay.shard]


def tables(positions):
    cosine, sine = rope_tables(positions)
    return jnp.concatenate([cosine, cosine], 1), jnp.concatenate([-sine, sine], 1)


def layer_kernels(length, width):
    groups = length // SEQ_LEN * KV_HEADS
    kv_width = KV_HEADS * HEAD
    smem = pl.BlockSpec(memory_space=pltpu.SMEM)
    vmem = pl.BlockSpec(memory_space=pltpu.VMEM)
    hbm = pl.BlockSpec(memory_space=pltpu.HBM)
    anywhere = pl.BlockSpec(memory_space=pl.ANY)
    params = pltpu.CompilerParams(vmem_limit_bytes=VMEM_LIMIT)

    def sds(shape, dtype):
        return jax.ShapeDtypeStruct(shape, dtype)

    def cost(flops):
        return pl.CostEstimate(flops=flops, bytes_accessed=8_000_000, transcendentals=600_000)

    piece, block = sds((4, HALF, 128), BF16), sds((2, HALF, 128), BF16)
    weights = [sds((width, width), BF16), sds((width, kv_width), BF16)]
    weights = weights + [weights[1], weights[0]]
    saved = [
        sds((groups, 3 * SEQ_LEN, SEQ_LEN), F32),
        sds((groups, 3 * SEQ_LEN, HEAD), BF16),
        sds((groups, SEQ_LEN, HEAD), BF16),
        sds((groups, SEQ_LEN, HEAD), BF16),
    ]
    rows = sds((length, width), F32)
    low_rows = sds((length, width), BF16)
    gain = sds((1, width), F32)
    outs = [rows, rows, gain, low_rows] + saved + weights + [gain]
    forward = pl.pallas_call(
        first_kernel,
        name="forward_and_ff_backward",
        in_specs=[smem] + [hbm] * 14 + [hbm, vmem, vmem, hbm],
        out_specs=[hbm] * len(outs) + [anywhere] * 10,
        out_shape=outs + [block] * 8 + [piece] * 2,
        scratch_shapes=[pltpu.VMEM(out.shape, out.dtype) for out in outs]
        + [
            pltpu.VMEM((CANON, 2 * HALF, 128), BF16),
            pltpu.VMEM((12, 2 * HALF, 128), BF16),
            pltpu.VMEM((width, length), BF16),
            pltpu.VMEM((width, length), BF16),
            pltpu.VMEM((length, width), BF16),
            pltpu.VMEM((length, width), F32),
            pltpu.VMEM((length, width), BF16),
            pltpu.VMEM((width, length), BF16),
            pltpu.VMEM((length, width), F32),
            pltpu.VMEM((width, 128), F32),
            pltpu.VMEM((width, 128), F32),
            pltpu.SemaphoreType.DMA((2,)),
            pltpu.SemaphoreType.DMA((4,)),
            pltpu.SemaphoreType.DMA((3,)),
            pltpu.SemaphoreType.DMA((len(outs),)),
        ],
        compiler_params=params,
        cost_estimate=cost(20 * length * width * FF),
    )
    attention_back = pl.pallas_call(
        second_kernel,
        name="attention_backward",
        in_specs=[smem] + [vmem] * 16 + [anywhere] * 2,
        out_specs=[hbm] * 2 + [anywhere] * 6,
        out_shape=[sds((width, length), BF16), sds((width, length), F32)] + [block] * 4 + [piece] * 2,
        scratch_shapes=[
            pltpu.VMEM((4, 2 * HALF, 128), BF16),
            pltpu.VMEM((2, 4, HALF, 128), BF16),
            pltpu.VMEM((width, length), BF16),
            pltpu.VMEM((width, length), F32),
            pltpu.VMEM((length, width), F32),
            pltpu.VMEM((length, kv_width), F32),
            pltpu.VMEM((length, kv_width), F32),
            pltpu.VMEM((width, 128), F32),
            pltpu.VMEM((width, 128), F32),
            pltpu.SemaphoreType.DMA((2,)),
            pltpu.SemaphoreType.DMA((1,)),
            pltpu.SemaphoreType.DMA((3,)),
        ],
        compiler_params=params,
        cost_estimate=cost(10 * length * width * width),
    )
    return forward, attention_back


def flat_of(payloads, lay):
    n = lay.count
    heads = payloads[:, lay.rows : lay.rows + 10]
    flats = [unhead_narrow(heads[0])]
    for i in range(n):
        wide = n // 4 <= i < 3 * n // 4
        body = payloads[i, : lay.rows]
        flat = unpack_wide(body, FF) if wide else unpack_narrow(body)
        if i + 1 < n:
            tail = unhead_wide(heads[i + 1]) if wide else unhead_narrow(heads[i + 1])
            flat = jnp.concatenate([flat[: -lay.gains], flat[-lay.gains :] + tail])
        flats.append(flat)
    return jnp.concatenate(flats)


def payloads_of(flat, lay):
    windows = [
        flat[i * lay.chunk : (i + 1) * lay.chunk + lay.gains] for i in range(lay.count)
    ]
    return jnp.stack([pack_payload(window, i, lay) for i, window in enumerate(windows)], 0)


def canonical(blocks, twins, lay, canon, index, core):
    sides = []
    for side in (blocks, twins):
        side = jnp.stack([jnp.concatenate(value, 0) for value in side], 0)
        sides.append(side.reshape(lay.count, lay.half, 128))
    both = jnp.where(core == 0, jnp.stack(sides, 1), jnp.stack(sides[::-1], 1))
    both = both.reshape(lay.count, 2 * lay.half, 128)
    both = jnp.take(both, jnp.arange(lay.count, dtype=jnp.int32) ^ index, axis=0)
    flat = flat_of(both, lay)
    zeros = jnp.zeros((canon.gains,), flat.dtype)
    rows = []
    for i in range(CANON):
        window = flat[i * canon.chunk : (i + 1) * canon.chunk + canon.gains]
        if i:
            window = jnp.concatenate([zeros, window[canon.gains :]])
        rows.append(pack_payload(window, i, canon))
    rows = jnp.stack(rows, 0).reshape(PLANES, 4, 2, canon.half, 128)
    pieces = []
    for c in range(2):
        side = rows[:, :, c]
        pieces = pieces + [side[0]] + [side[p, :2] for p in range(1, PLANES)]
        pieces = pieces + [side[p, 2:] for p in range(1, PLANES)]
    return pieces


def from_canonical(slots, lay, canon, place, core):
    sides = []
    for which in range(2):
        sides.append(jnp.stack([slot[which] for slot in slots], 0))
    rows = jnp.stack(sides, 2).reshape(CANON, 2 * canon.half, 128)
    flats = [unhead_narrow(rows[0, canon.rows : canon.rows + 10])]
    for i in range(CANON):
        body = rows[i, : canon.rows]
        flats.append(unpack_wide(body, FF) if 4 <= i < 12 else unpack_narrow(body))
    rows = payloads_of(jnp.concatenate(flats), lay)
    rows = rows.reshape(PLANES, lay.in_plane, 2, lay.half, 128)
    rows = jnp.take(rows, jnp.arange(lay.in_plane, dtype=jnp.int32) ^ place, axis=1)
    rows = rows.reshape(PLANES, 1 << lay.y_bits, 1 << lay.x_bits, 2, lay.half, 128)
    sides = [jnp.take(rows, side, axis=3) for side in (core, 1 - core)]
    return [[list(side[p]) for p in range(PLANES)] for side in sides]


def add(left, right):
    return left.astype(F32) + right.astype(F32)


def on_device(lay, canon, tokens_in, positions, params, cotangent):
    index = lax.axis_index("dp")
    core = lax.axis_index("rep")
    n, half, in_plane = lay.count, lay.half, lay.in_plane
    plane, place = index // in_plane, index % in_plane
    same = n == CANON
    firsts, seconds = hops(lay)
    forward, attention_back = layer_kernels(*tokens_in.shape)
    mine = pack_own(params, index, core, lay)
    angles = tables(positions)
    if same:
        idx = jnp.stack([plane, place, core, 1]).astype(jnp.int32)
        pieces, angles = balanced_gather(mine, lay, angles)
    else:
        idx = jnp.zeros((4,), jnp.int32)
        blocks = gather(mine, lay)
        twins = [[swap_rep(block) for block in value] for value in blocks]
        pieces = canonical(blocks, twins, lay, canon, index, core)
    results = forward(idx, *pieces, tokens_in.T, *angles, cotangent.T)
    d_gain = results[2]
    saved, slots, held = results[:13], (results[13:17], results[17:21]), results[21:23]
    if same:
        (first,), (second,) = firsts, seconds
        moved = [hop(add(far, swap_rep(send)).astype(BF16), second, n) for _, far, _, send in slots]
        near = [add(keep, swap_rep(send)) for keep, _, send, _ in slots]
    output, d_input, *results = attention_back(idx, tokens_in.T, *angles, *saved, *held)
    output, d_input = output.T, d_input.T
    keep_near, keep_far, send_near, send_far, keep, send = results
    if same:
        moved, send_far, send_near, send = lax.optimization_barrier((moved, send_far, send_near, send))
        third = hop(add(keep_far, swap_rep(send_far)).astype(BF16), second, n)
        early = [(near[j] + moved[j].astype(F32)).astype(BF16) for j in range(2)]
        early = [add(value[0], hop(value[1], first, n)).astype(BF16) for value in early]
        third = (add(keep_near, swap_rep(send_near)) + third.astype(F32)).astype(BF16)
        third = add(third[0], hop(third[1], first, n)).astype(BF16)
        keep, send = [jnp.where(plane == 0, a, b) for a, b in zip((keep, send), held)]
        mine = add(keep, swap_rep(send)).astype(BF16)

        def pick(values, s):
            table = ((0, 1, 2), (2, 1, 0), (1, 2, 0), (1, 0, 2))
            result = values[table[3][s - 1]]
            for z in range(3):
                result = jnp.where(plane == z, values[table[z][s - 1]], result)
            return result

        mine, third = lax.optimization_barrier((mine, third))
        planes = early + [third]
        parts = [swap(pick(planes, s), s << (lay.bits - 2), n) for s in range(1, PLANES)]
        both = tuple(a ^ b for a, b in zip(first, second))
        inner = [hop(mine[d], masks, n) for d, masks in ((1, first), (2, second), (3, both))]
        parts, inner = lax.optimization_barrier((parts, inner))
        total = (add(mine[0], inner[0]) + add(inner[1], inner[2])) + (
            parts[0].astype(F32) + add(parts[1], parts[2])
        )
    else:
        slots = [(near, far, other, last) for near, far, other, last in slots]
        slots.append((keep_near, keep_far, send_near, send_far))
        planes = [(keep, send)]
        for near, far, other, last in slots:
            planes.append((jnp.concatenate([near, far], 0), jnp.concatenate([other, last], 0)))
        keeps, sends = from_canonical(planes, lay, canon, place, core)
        moved = []
        for keep, send in zip(keeps, sends):
            pair = pair_sum(keep, send)
            moved.append(add_blocks(pair[0], send_blocks(pair, seconds, n)))
        blocks = split_first(moved, lay)
        planes = add_blocks(blocks[0], send_blocks(blocks, firsts, n))
        total = reduce_planes(planes, plane, lay)
    other = swap_rep(total)
    if same:
        at = ROWS + 26 - HALF
        d_gain = jnp.where(core == 1, total[at : at + 5], other[at : at + 5]).reshape(-1)[: lay.width]
    else:
        d_gain = sum_everywhere(d_gain[0], lay)
    return output, d_input, unpack_own(total, other, index, core, lay), d_gain


def solution(mesh):
    def run(tokens_in, positions, params, cotangent):
        total, width = params.shape[0], tokens_in.shape[1]
        lay = Layout(mesh.shape["dp"], total, width)
        canon = Layout(CANON, total, width)
        rows = P(("dp", "rep"), None)
        return jax.shard_map(
            lambda *args: on_device(lay, canon, *args),
            mesh=mesh,
            in_specs=(rows, P(("dp", "rep")), P("dp"), rows),
            out_specs=(rows, rows, P("dp"), P()),
            check_vma=False,
        )(tokens_in, positions, params, cotangent)

    return run
```

```python
import jax
import jax.numpy as jnp
from jax import lax
from jax.experimental import pallas as pl
from jax.experimental.pallas import tpu as pltpu
from jax.sharding import PartitionSpec as P

HEADS = 9
KV_HEADS = 3
HEAD = 64
FF = 1536
SEQ_LEN = 128
PLANES = 4
CANON = 16

EPS = 1e-05
ROPE_BASE = 100000.0

F32, BF16 = jnp.float32, jnp.bfloat16
ROWS, HALF = 1728, 880
MAIN, REST = 768, 112
NARROW, WIDE = 384, 144
VMEM_LIMIT = 52 * 1024 * 1024


class Layout:
    def __init__(self, count, total, width):
        self.count = count
        self.width = width
        self.gains = 2 * width
        self.shard = total // count
        self.chunk = (total - self.gains) // count
        self.step = self.gains // count
        self.rows = self.chunk // 128
        half = -(-(self.rows + 10) // 2)
        self.half = -(-half // 16) * 16
        self.first = -(-(self.half // 2) // 16) * 16
        self.extra = 2 * self.half - self.rows
        self.bits = count.bit_length() - 1
        rest = self.bits - 2
        self.x_bits = -(-rest // 2)
        self.y_bits = rest - self.x_bits
        self.in_plane = 1 << rest
        self.flip = self.x_bits == self.y_bits


def pack_wide(flat, width):
    panels = width // 128
    return flat.reshape(-1, panels, 128).transpose(1, 0, 2).reshape(-1, 128)


def unpack_wide(rows, width):
    panels = width // 128
    return rows.reshape(panels, -1, 128).transpose(1, 0, 2).reshape(-1)


def pack_narrow(flat):
    rows = flat.reshape(-1, 576)
    count = rows.shape[0]
    panels = rows[:, :512].reshape(count, 4, 128).transpose(1, 0, 2).reshape(-1, 128)
    tail = rows[:, 512:]
    return jnp.concatenate([panels, jnp.concatenate([tail[: count // 2], tail[count // 2 :]], 1)], 0)


def unpack_narrow(packed):
    count = packed.shape[0] * 2 // 9
    panels = packed[: 4 * count].reshape(4, count, 128).transpose(1, 0, 2).reshape(count, 512)
    half = packed[4 * count :]
    tail = jnp.concatenate([half[:, :64], half[:, 64:]], 0)
    return jnp.concatenate([panels, tail], 1).reshape(-1)


def head_narrow(flat):
    rows = flat.reshape(2, 576)
    tail = jnp.pad(rows[:, 512:], ((0, 0), (64, 0)))
    return jnp.concatenate([rows[:, :512].reshape(8, 128), tail], 0)


def unhead_narrow(rows):
    return jnp.concatenate([rows[:8].reshape(2, 512), rows[8:10, 64:]], 1).reshape(-1)


def head_wide(flat):
    return jnp.pad(flat.reshape(9, 128), ((0, 1), (0, 0)))


def unhead_wide(rows):
    return rows[:9].reshape(-1)


def is_wide(index, count):
    return (index >= count // 4) & (index < 3 * count // 4)


def pack_payload(window, index, lay):
    head, chunk = window[: lay.gains], window[lay.gains :]
    body = jnp.where(is_wide(index, lay.count), pack_wide(chunk, FF), pack_narrow(chunk))
    top = jnp.where(is_wide(index - 1, lay.count), head_wide(head), head_narrow(head))
    return jnp.concatenate([body, jnp.pad(top, ((0, lay.extra - 10), (0, 0)))], 0)


def unpack_payload(rows, index, lay):
    body, top = rows[: lay.rows], rows[lay.rows : lay.rows + 10]
    chunk = jnp.where(is_wide(index, lay.count), unpack_wide(body, FF), unpack_narrow(body))
    head = jnp.where(is_wide(index - 1, lay.count), unhead_wide(top), unhead_narrow(top))
    return jnp.concatenate([head, chunk])


def swap(value, mask, count):
    return lax.ppermute(value, "dp", [(i, i ^ mask) for i in range(count)])


def swap_rep(value):
    return lax.ppermute(value, "rep", [(0, 1), (1, 0)])


def hop(value, masks, count):
    pairs = [(2 * i + c, 2 * (i ^ masks[c]) + c) for i in range(count) for c in range(2)]
    return lax.ppermute(value, ("dp", "rep"), pairs)


def hops(lay):
    xs = [d for d in range(1, 1 << lay.x_bits)]
    ys = [e << lay.x_bits for e in range(1, 1 << lay.y_bits)]
    if lay.flip:
        return list(zip(xs, ys)), list(zip(ys, xs))
    return list(zip(xs, xs)), list(zip(ys, ys))


def gather_hops(value, masks, count):
    return jnp.stack([value] + [hop(value, pair, count) for pair in masks], 0)


def gather(half, lay):
    n = lay.count
    first, second = hops(lay)
    planes = [half] + [swap(half, s << (lay.bits - 2), n) for s in range(1, PLANES)]
    blocks = []
    for plane in planes:
        block = gather_hops(plane, first, n)
        blocks.append([block] + [hop(block, masks, n) for masks in second])
    return blocks


def balanced_gather(half, lay, beside):
    n = lay.count
    (first,), (second,) = hops(lay)
    both = tuple(a ^ b for a, b in zip(first, second))
    across = [swap(half, s << (lay.bits - 2), n) for s in range(1, PLANES)]
    plane = [hop(half, masks, n) for masks in (first, second, both)]
    across, plane, beside = lax.optimization_barrier((across, plane, beside))
    own = jnp.stack([half] + plane, 0)
    near = [jnp.stack([value, hop(value, first, n)], 0) for value in across]
    far = [hop(value, second, n) for value in near]
    early = [own] + near
    far[0], twins = lax.optimization_barrier(
        (far[0], [swap_rep(value) for value in early + far[1:]])
    )
    return early + far + twins[:4] + [swap_rep(far[0])] + twins[4:], beside


def pair_sum(keep, send):
    return [
        (mine.astype(F32) + swap_rep(other).astype(F32)).astype(BF16)
        for mine, other in zip(keep, send)
    ]


def send_blocks(blocks, masks, count):
    return [hop(block, pair, count) for block, pair in zip(blocks[1:], masks)]


def add_blocks(block, arrived):
    total = block.astype(F32)
    for value in arrived:
        total = total + value.astype(F32)
    return total.astype(BF16)


def split_first(planes, lay):
    return [jnp.stack([value[j] for value in planes], 0) for j in range(len(hops(lay)[0]) + 1)]


def reduce_planes(planes, plane, lay):
    parts = [jnp.take(planes, plane, axis=0).astype(F32)]
    for s in range(1, PLANES):
        part = swap(jnp.take(planes, plane ^ s, axis=0), s << (lay.bits - 2), lay.count)
        parts.append(part.astype(F32))
    return (parts[0] + parts[1]) + (parts[2] + parts[3])


def sum_everywhere(value, lay):
    value = value + swap_rep(value)
    for bit in range(lay.bits):
        value = value + swap(value, 1 << bit, lay.count)
    return value


def rope_tables(places):
    expon = jnp.arange(HEAD // 2).astype(jnp.float32) * (2.0 / HEAD)
    inverse = jnp.power(ROPE_BASE, -expon)
    angle = places.astype(jnp.float32)[..., None] * inverse
    return (jnp.cos(angle), jnp.sin(angle))


def dot(left, right):
    return jnp.dot(left, right, preferred_element_type=F32)


def dot_nt(left, right):
    return lax.dot_general(left, right, (((1,), (1,)), ((), ())), preferred_element_type=F32)


def dot_tn(left, right):
    return lax.dot_general(left, right, (((0,), (0,)), ((), ())), preferred_element_type=F32)


def row_of_head(head, which):
    parts = [head[4 * which + j : 4 * which + j + 1] for j in range(4)]
    return jnp.concatenate(parts + [head[8 + which : 9 + which, 64:]], 1)


def head_of_rows(rows):
    parts = [row[:, 128 * j : 128 * j + 128] for row in rows for j in range(4)]
    zeros = jnp.zeros((1, 64), F32)
    parts = parts + [jnp.concatenate([zeros, row[:, 512:]], 1) for row in rows]
    return jnp.concatenate(parts + [jnp.zeros((6, 128), F32)], 0)


def gain_rows(gain, low):
    parts = [gain[:, 128 * j : 128 * j + 128] for j in range(4)]
    parts = parts + [jnp.concatenate([gain[:, 512:], gain[:, 512:]], 1)]
    return jnp.concatenate([low[:10]] + parts + [jnp.zeros((1, 128), F32)], 0)


def load_narrow(ref, index):
    parts = [ref[index, NARROW * j : NARROW * (j + 1), :] for j in range(4)]
    half = ref[index, 4 * NARROW : ROWS, :]
    tail = jnp.concatenate([half[:, :64], half[:, 64:]], 0)
    return jnp.concatenate(parts + [tail], 1)


def store_narrow(ref, index, value):
    for j in range(4):
        ref[index, NARROW * j : NARROW * (j + 1), :] = value[:, 128 * j : 128 * (j + 1)].astype(BF16)
    tail = value[:, 512:]
    tail = jnp.concatenate([tail[: NARROW // 2], tail[NARROW // 2 :]], 1)
    ref[index, 4 * NARROW : ROWS, :] = tail.astype(BF16)


def narrow_tiles():
    tiles = [(NARROW * (j + 1) - 16, j, 4 + j) for j in range(4)]
    return tiles + [(ROWS - 16, 8, 9)]


def add_tail(ref, index, wide):
    head = ref[index + 1, ROWS : ROWS + 16, :].astype(F32)
    row = lax.broadcasted_iota(jnp.int32, (16, 128), 0)
    if wide:
        for k in range(9):
            at = WIDE * (4 + k) - 16
            tile = ref[index, at : at + 16, :].astype(F32)
            tile = tile + jnp.where(row == 15, head[k : k + 1], 0.0)
            ref[index, at : at + 16, :] = tile.astype(BF16)
    else:
        for at, upper, lower in narrow_tiles():
            tile = ref[index, at : at + 16, :].astype(F32)
            tile = tile + jnp.where(row == 14, head[upper : upper + 1], 0.0)
            tile = tile + jnp.where(row == 15, head[lower : lower + 1], 0.0)
            ref[index, at : at + 16, :] = tile.astype(BF16)


def tail_of(ref, index, wide):
    if wide:
        parts = []
        for k in range(9):
            at = WIDE * (4 + k) - 16
            parts.append(ref[index, at : at + 16, :].astype(F32)[15:16])
        return jnp.concatenate(parts + [jnp.zeros((7, 128), F32)], 0)
    tiles = [ref[index, at : at + 16, :].astype(F32) for at, _, _ in narrow_tiles()]
    parts = [tile[14:15] for tile in tiles[:4]] + [tile[15:16] for tile in tiles[:4]]
    parts = parts + [tiles[4][14:15], tiles[4][15:16]]
    return jnp.concatenate(parts + [jnp.zeros((6, 128), F32)], 0)


def spread(value, first, second, out):
    for m in range(3):
        part = value[:, 192 * m : 192 * (m + 1)].astype(F32)
        first[pl.ds(m, 192, stride=3), :] = part[:, :128]
        second[pl.ds(m, 192, stride=3), :] = jnp.concatenate([part[:, 128:], part[:, 128:]], 1)
    out[:, :128] = first[...].astype(BF16)
    out[:, 128:] = second[:, :64].astype(BF16)


def unspread(value, first, second):
    first[...] = value[:, :128]
    second[...] = jnp.concatenate([value[:, 128:], value[:, 128:]], 1)
    parts = []
    for m in range(3):
        parts.append(first[pl.ds(m, 192, stride=3), :])
        parts.append(second[pl.ds(m, 192, stride=3), :][:, :64])
    return jnp.concatenate(parts, 1)


def turn(vector, cosine, sine):
    swapped = jnp.concatenate([vector[:, 32:], vector[:, :32]], 1)
    return vector * cosine + swapped * sine


def piece_copies(idx, at_plane, sides, dst, sem, outward):
    place, core, flip = idx[1], idx[2], idx[3]
    copies = []
    for which, refs in enumerate(sides):
        side = jnp.bitwise_xor(core, which)
        for d in range(4):
            turned = ((d & 1) << 1) | (d >> 1)
            chunk = 4 * at_plane + jnp.bitwise_xor(place, jnp.where(side * flip == 1, turned, d))
            ref = refs[0].at[d] if len(refs) == 1 else refs[d // 2].at[d % 2]
            for start, rows in ((0, MAIN), (MAIN, REST)) if outward else ((0, HALF),):
                outer = ref.at[pl.ds(start, rows), :]
                at = pl.multiple_of(side * HALF + start, 16)
                inner = dst.at[chunk, pl.ds(at, rows), :]
                pair = (inner, outer) if outward else (outer, inner)
                copies.append((start > 0, pltpu.make_async_copy(pair[0], pair[1], sem)))
    return copies


def wait_plane(ref, base, sem):
    whole = ref.at[pl.ds(base, 4)]
    pltpu.make_async_copy(whole, whole, sem).wait()


def slot_plane(plane, slot):
    own = jnp.where(plane == 0, 3, plane)
    low = jnp.where(own == 1, 2, 1)
    return [low, 6 - own - low, own][slot]


def first_kernel(idx, *refs):
    pieces = list(zip(refs[:7], refs[7:14]))
    tok_hbm, cos, sin, cot_hbm = refs[14:18]
    refs = refs[18:]
    results, outs = refs[:13], refs[13:23]
    refs = refs[23:]
    y_acc, dr_out, dg_out, att_out, p_out, q_out, k_out, v_out, wq, wk, wv, wo, gain_out = refs[:13]
    w, g, tok, cot_t, cot, att, n2_ref, n2t_ref, dn_acc, first, second = refs[13:24]
    in_sem, sems, out_sems, result_sems = refs[24:]
    saves = [
        pltpu.make_async_copy(src, dst, result_sems.at[i])
        for i, (src, dst) in enumerate(zip(refs[:13], results))
    ]
    load = pltpu.make_async_copy(tok_hbm, tok, in_sem.at[0])
    load.start()
    load_cot = pltpu.make_async_copy(cot_hbm, cot_t, in_sem.at[1])
    load_cot.start()
    planes = []
    for s in range(PLANES):
        sides = [[ref] for ref in pieces[0]]
        if s:
            sides = list(zip(pieces[s], pieces[s + 3]))
        at_plane = jnp.bitwise_xor(idx[0], s)
        copies = piece_copies(idx, at_plane, sides, w, sems.at[at_plane], False)
        planes.append([copy for _, copy in copies])
    for p in range(PLANES):
        for s in range(PLANES):

            @pl.when(jnp.bitwise_xor(idx[0], s) == p)
            def _(copies=planes[s]):
                for copy in copies:
                    copy.start()

    tokens = tok.shape[1]
    load.wait()
    x = tok[...].astype(F32).T
    normed = x * lax.rsqrt(jnp.mean(x * x, -1, keepdims=True) + EPS)
    load_cot.wait()
    cot[...] = cot_t[...].astype(F32).T.astype(BF16)
    wait_plane(w, 0, sems.at[0])
    for c in range(3):
        add_tail(w, c, False)
    gains = w[0, ROWS : ROWS + 16, :].astype(F32)
    gain_in, gain_mid = row_of_head(gains, 0), row_of_head(gains, 1)
    gain_out[...] = gain_in
    n1 = (normed * gain_in).astype(BF16)
    wq[:NARROW, :] = load_narrow(w, 0)
    mixed_chunk = load_narrow(w, 1)
    wq[NARROW:, :] = mixed_chunk[:192]
    spread(mixed_chunk[192:], first, second, wk)
    mixed_chunk = load_narrow(w, 2)
    spread(mixed_chunk[:192], first, second, wv)
    wo[:192, :] = mixed_chunk[192:]

    query, keys, values = dot(n1, wq[...]), dot(n1, wk[...]), dot(n1, wv[...])
    row = lax.broadcasted_iota(jnp.int32, (3 * SEQ_LEN, SEQ_LEN), 0)
    causal = jnp.bitwise_and(row, SEQ_LEN - 1) >= lax.broadcasted_iota(
        jnp.int32, (3 * SEQ_LEN, SEQ_LEN), 1
    )
    for b in range(tokens // SEQ_LEN):
        part = slice(SEQ_LEN * b, SEQ_LEN * (b + 1))
        cosine, sine = cos[part, :], sin[part, :]
        for kv in range(KV_HEADS):
            at = KV_HEADS * b + kv
            heads = [
                turn(query[part, HEAD * h : HEAD * (h + 1)], cosine, sine)
                for h in range(3 * kv, 3 * kv + 3)
            ]
            q3 = jnp.concatenate(heads, 0).astype(BF16)
            k1 = turn(keys[part, HEAD * kv : HEAD * (kv + 1)], cosine, sine).astype(BF16)
            v1 = values[part, HEAD * kv : HEAD * (kv + 1)].astype(BF16)
            q_out[at], k_out[at], v_out[at] = q3, k1, v1
            score = jnp.where(causal, dot_nt(q3, k1) * HEAD**-0.5, -1e30)
            expon = jnp.exp(score - jnp.max(score, -1, keepdims=True))
            probs = expon / jnp.sum(expon, -1, keepdims=True)
            p_out[at] = probs
            mix = dot(probs.astype(BF16), v1)
            for r in range(3):
                h = 3 * kv + r
                att[part, HEAD * h : HEAD * (h + 1)] = mix[SEQ_LEN * r : SEQ_LEN * (r + 1)]
    attended = att[...].astype(BF16)
    att_out[...] = attended
    wait_plane(w, 4, sems.at[1])
    add_tail(w, 3, False)
    wo[192:, :] = load_narrow(w, 3)
    for copy in saves[3:]:
        copy.start()
    mixed = x + dot(attended, wo[...])
    inverse = lax.rsqrt(jnp.mean(mixed * mixed, -1, keepdims=True) + EPS)
    normed_mid = mixed * inverse
    n2 = normed_mid * gain_mid
    n2_ref[...] = n2.astype(BF16)
    n2t_ref[...] = n2.astype(BF16).astype(F32).T.astype(BF16)
    y_acc[...] = mixed
    dn_acc[...] = jnp.zeros_like(dn_acc)
    wait_plane(w, 8, sems.at[2])
    wait_plane(w, 12, sems.at[3])

    def fix(i, carry):
        add_tail(w, i + 4, True)
        return carry

    lax.fori_loop(0, 8, fix, 0)
    for c in (12, 13, 14):
        add_tail(w, c, False)

    def block(k, carry):
        def wide(base, p):
            at = pl.multiple_of((6 * k + p) * WIDE, 16)
            return jnp.concatenate([w[base + d, pl.ds(at, WIDE), :] for d in range(4)], 0)

        w_gate = jnp.concatenate([wide(4, p) for p in range(6)], 1)
        w_up = jnp.concatenate([wide(8, p) for p in range(6)], 1)
        w_down = jnp.concatenate([load_narrow(w, 12 + 2 * k), load_narrow(w, 13 + 2 * k)], 0)
        c = cot[...]
        gate, up = dot(n2_ref[...], w_gate), dot(n2_ref[...], w_up)
        sigma = 1.0 / (1.0 + jnp.exp(-gate))
        silu = gate * sigma
        hidden = (silu * up).astype(BF16)
        y_acc[...] += dot(hidden, w_down)
        d_down = dot_tn(hidden, c)
        store_narrow(g, 8 + 2 * k, d_down[:NARROW])
        store_narrow(g, 9 + 2 * k, d_down[NARROW:])
        d_hidden = dot_nt(c, w_down)
        d_gate = (d_hidden * up * sigma * (1.0 + gate * (1.0 - sigma))).astype(BF16)
        d_up = (d_hidden * silu).astype(BF16)
        dn_acc[...] += dot_nt(d_gate, w_gate) + dot_nt(d_up, w_up)
        for base, d_out in ((0, d_gate), (4, d_up)):
            grad = dot(n2t_ref[...], d_out).astype(BF16)
            for p in range(6):
                at = pl.multiple_of((6 * k + p) * WIDE, 16)
                for d in range(4):
                    g[base + d, pl.ds(at, WIDE), :] = grad[
                        WIDE * d : WIDE * (d + 1), 128 * p : 128 * (p + 1)
                    ]
        return carry

    lax.fori_loop(0, 2, block, 0)
    stores = []
    for slot in range(3):
        sides = [outs[4 * slot : 4 * slot + 2], outs[4 * slot + 2 : 4 * slot + 4]]
        if slot == 2:
            sides = [outs[8:9], outs[9:10]]
        at_plane = slot_plane(idx[0], slot) - 1
        stores = stores + piece_copies(idx, at_plane, sides, g, out_sems.at[slot], True)
    for last, copy in stores:
        if not last:
            copy.start()
    d_norm = dn_acc[...]
    d_gain = jnp.sum(d_norm * normed_mid, 0, keepdims=True)
    dg_out[...] = d_gain
    scaled = d_norm * gain_mid
    d_mixed = cot[...].astype(F32) + inverse * (
        scaled - normed_mid * jnp.mean(scaled * normed_mid, -1, keepdims=True)
    )
    last_rows = dot_tn(att_out[:, 512:], d_mixed.astype(BF16))
    for c in range(12):
        if c:
            top = tail_of(g, c - 1, c - 1 < 8)
        else:
            top = head_of_rows([last_rows[62:63], last_rows[63:64]])
        g[c, ROWS : ROWS + 16, :] = top.astype(BF16)
        g[c, ROWS + 16 :, :] = gain_rows(d_gain, jnp.zeros((16, 128), F32)).astype(BF16)
    for last, copy in stores:
        if last:
            copy.start()
    dr_out[...] = d_mixed
    for copy in saves[:3]:
        copy.start()
    for copy in saves:
        copy.wait()
    for slot in range(3):
        wait_plane(g, 4 * slot, out_sems.at[slot])


def second_kernel(idx, *refs):
    tok, cos, sin, y_in, dr, dg, att, p_in, q_in, k_in, v_in, wq, wk, wv, wo, gain = refs[:16]
    held, (y_out, dx_out), third, mine = refs[16:18], refs[18:20], refs[20:24], refs[24:26]
    g, bounce, y_t, dx_t, dq_ref, dk_ref, dv_ref, first, second, in_sem, out_sems, held_sem = refs[26:]
    tokens = tok.shape[1]
    ground = idx[0] == 0
    fetch = [
        pltpu.make_async_copy(held[side], bounce.at[side], held_sem.at[side]) for side in range(2)
    ]

    @pl.when(ground)
    def _():
        for copy in fetch:
            copy.start()

    d_mixed = dr[...]
    branch = d_mixed.astype(BF16)
    dw_out = dot_tn(att[...], branch)
    d_att = dot_nt(branch, wo[...])
    @pl.when(ground)
    def _():
        for copy in fetch:
            copy.wait()
        for side in range(2):
            for j in range(2):
                source = bounce.at[side, pl.ds(2 * j, 2)]
                pltpu.make_async_copy(source, third[2 * side + j], held_sem.at[2]).start()

    for b in range(tokens // SEQ_LEN):
        part = slice(SEQ_LEN * b, SEQ_LEN * (b + 1))
        cosine, sine = cos[part, :], -sin[part, :]
        for kv in range(KV_HEADS):
            at = KV_HEADS * b + kv
            heads = [d_att[part, HEAD * h : HEAD * (h + 1)] for h in range(3 * kv, 3 * kv + 3)]
            d3 = jnp.concatenate(heads, 0).astype(BF16)
            probs, q3, k1, v1 = p_in[at], q_in[at], k_in[at], v_in[at]
            d_probs = dot_nt(d3, v1)
            dv_ref[part, HEAD * kv : HEAD * (kv + 1)] = dot_tn(probs.astype(BF16), d3)
            inner = jnp.sum(d_probs * probs, -1, keepdims=True)
            d_score = (probs * (d_probs - inner)).astype(BF16)
            dq3 = dot(d_score, k1) * HEAD**-0.5
            for r in range(3):
                h = 3 * kv + r
                dq_ref[part, HEAD * h : HEAD * (h + 1)] = turn(
                    dq3[SEQ_LEN * r : SEQ_LEN * (r + 1)], cosine, sine
                )
            dk_ref[part, HEAD * kv : HEAD * (kv + 1)] = turn(
                dot_tn(d_score, q3) * HEAD**-0.5, cosine, sine
            )
    dq, dk, dv = dq_ref[...].astype(BF16), dk_ref[...].astype(BF16), dv_ref[...].astype(BF16)
    x = tok[...].astype(F32)
    inverse = lax.rsqrt(jnp.mean(x * x, 0, keepdims=True) + EPS)
    normed = x * inverse
    gain_column = jnp.broadcast_to(gain[...], (8, gain.shape[1])).T[:, :1]
    n1t = (normed * gain_column).astype(BF16)
    dw_query = dot(n1t, dq)
    store_narrow(g, 0, dw_query[:NARROW])
    dw = unspread(dot(n1t, dk), first, second)
    store_narrow(g, 1, jnp.concatenate([dw_query[NARROW:], dw], 0))
    dw = unspread(dot(n1t, dv), first, second)
    store_narrow(g, 2, jnp.concatenate([dw, dw_out[:192]], 0))
    store_narrow(g, 3, dw_out[192:])
    d_norm = dot_nt(wq[...], dq) + dot_nt(wk[...], dk) + dot_nt(wv[...], dv)
    d_gain = jnp.sum(d_norm * normed, 1, keepdims=True)
    d_gain = jnp.broadcast_to(d_gain, (d_gain.shape[0], 128)).T[:1]
    for c in range(4):
        top = tail_of(g, c - 1, False) if c else head_of_rows([d_gain, dg[...]])
        g[c, ROWS : ROWS + 16, :] = top.astype(BF16)
        g[c, ROWS + 16 :, :] = gain_rows(dg[...], jnp.zeros((16, 128), F32)).astype(BF16)

    @pl.when(ground)
    def _():
        for _, copy in piece_copies(idx, 0, [mine[:1], mine[1:]], g, out_sems.at[0], True):
            copy.start()

    @pl.when(jnp.logical_not(ground))
    def _():
        for _, copy in piece_copies(idx, 0, [third[:2], third[2:]], g, out_sems.at[0], True):
            copy.start()

    scaled = d_norm * gain_column
    dx_t[...] = d_mixed.T + inverse * (
        scaled - normed * jnp.mean(scaled * normed, 0, keepdims=True)
    )
    y_t[...] = y_in[...].T.astype(BF16)
    stores = [
        pltpu.make_async_copy(src, dst, in_sem.at[i])
        for i, (src, dst) in enumerate(((dx_t, dx_out), (y_t, y_out)))
    ]
    for copy in stores:
        copy.start()
    for copy in stores:
        copy.wait()
    wait_plane(g, 0, out_sems.at[0])

    @pl.when(ground)
    def _():
        wait_plane(g, 0, held_sem.at[2])


def halves_turned(low, high):
    lane = lax.broadcasted_iota(jnp.int32, low.shape, 1)
    return jnp.where(lane < 64, pltpu.roll(low, 64, 1), pltpu.roll(high, 64, 1))


def pack_kernel(idx, flat, out, rolled, window, packed, mixed):
    index, core, down, right = idx[0], idx[1], idx[2], idx[3]
    lane = lax.broadcasted_iota(jnp.int32, (1, 128), 1)
    rolled[0:16, :] = jnp.zeros((16, 128), F32)
    rolled[16:1752, :] = pltpu.roll(flat[...].astype(F32), right, 1)
    rolled[1752:1760, :] = jnp.zeros((8, 128), F32)
    window[...] = jnp.where(
        lane >= right, rolled[pl.ds(16 - down, 1744), :], rolled[pl.ds(15 - down, 1744), :]
    )
    head = [window[k : k + 1, :] for k in range(9)]
    wide = (index >= 4) & (index < 12)

    @pl.when(wide)
    def _():
        for j in range(12):
            packed[WIDE * j : WIDE * (j + 1), :] = window[pl.ds(9 + j, WIDE, stride=12), :]

    @pl.when(jnp.logical_not(wide))
    def _():
        parts = [window[pl.ds(9 + k, NARROW // 2, stride=9), :] for k in range(9)]
        for j in range(4):
            packed[pl.ds(NARROW * j, NARROW // 2, stride=2), :] = parts[j]
            packed[pl.ds(NARROW * j + 1, NARROW // 2, stride=2), :] = halves_turned(
                parts[4 + j], parts[5 + j]
            )
        mixed[pl.ds(0, NARROW // 2, stride=2), :] = parts[4]
        mixed[pl.ds(1, NARROW // 2, stride=2), :] = pltpu.roll(parts[8], 64, 1)
        packed[4 * NARROW : ROWS, :] = jnp.where(
            lane < 64, mixed[: NARROW // 2, :], pltpu.roll(mixed[NARROW // 2 :, :], 64, 1)
        )

    last = jnp.zeros((23, 128), F32)
    after_wide = (index >= 5) & (index < 13)

    @pl.when(after_wide)
    def _():
        packed[ROWS:, :] = jnp.concatenate(head + [last], 0)

    @pl.when(jnp.logical_not(after_wide))
    def _():
        rows = head[:4] + [halves_turned(head[4 + j], head[5 + j]) for j in range(4)]
        rows.append(jnp.where(lane < 64, 0.0, pltpu.roll(head[4], 64, 1)))
        rows.append(jnp.where(lane < 64, 0.0, head[8]))
        packed[ROWS:, :] = jnp.concatenate(rows + [last[:22]], 0)

    out[...] = packed[pl.ds(pl.multiple_of(core * HALF, 16), HALF), :].astype(BF16)


def unpack_kernel(idx, own, twin, out, packed, window, mixed):
    index, core, down, left = idx[0], idx[1], idx[2], idx[3]
    lane = lax.broadcasted_iota(jnp.int32, (1, 128), 1)
    packed[pl.ds(pl.multiple_of(core * HALF, 16), HALF), :] = own[...]
    packed[pl.ds(pl.multiple_of((1 - core) * HALF, 16), HALF), :] = twin[...]
    head = [packed[ROWS + k : ROWS + k + 1, :] for k in range(10)]
    window[1737:, :] = jnp.zeros((15, 128), F32)
    wide = (index >= 4) & (index < 12)

    @pl.when(wide)
    def _():
        for j in range(12):
            window[pl.ds(9 + j, WIDE, stride=12), :] = packed[WIDE * j : WIDE * (j + 1), :]

    @pl.when(jnp.logical_not(wide))
    def _():
        half = packed[4 * NARROW : ROWS, :]
        mixed[: NARROW // 2, :] = half
        mixed[NARROW // 2 :, :] = pltpu.roll(half, 64, 1)
        odd = []
        for j in range(4):
            window[pl.ds(9 + j, NARROW // 2, stride=9), :] = packed[
                pl.ds(NARROW * j, NARROW // 2, stride=2), :
            ]
            odd.append(pltpu.roll(packed[pl.ds(NARROW * j + 1, NARROW // 2, stride=2), :], 64, 1))
        odd.append(mixed[pl.ds(1, NARROW // 2, stride=2), :])
        before = mixed[pl.ds(0, NARROW // 2, stride=2), :]
        for j in range(4):
            window[pl.ds(13 + j, NARROW // 2, stride=9), :] = jnp.where(lane < 64, before, odd[j])
            before = odd[j]
        window[pl.ds(17, NARROW // 2, stride=9), :] = jnp.where(
            lane < 64, before, pltpu.roll(odd[4], 64, 1)
        )

    after_wide = (index >= 5) & (index < 13)

    @pl.when(after_wide)
    def _():
        window[0:9, :] = jnp.concatenate(head[:9], 0)

    @pl.when(jnp.logical_not(after_wide))
    def _():
        odd = [pltpu.roll(row, 64, 1) for row in head[4:8]]
        before, rows = pltpu.roll(head[8], 64, 1), head[:4]
        for j in range(4):
            rows.append(jnp.where(lane < 64, before, odd[j]))
            before = odd[j]
        rows.append(jnp.where(lane < 64, before, head[9]))
        window[0:9, :] = jnp.concatenate(rows, 0)

    lanes = pltpu.roll(window[...], jnp.bitwise_and(128 - left, 127), 1)
    window[...] = lanes
    out[...] = jnp.where(
        lane < 128 - left, window[pl.ds(down, 1736), :], window[pl.ds(down + 1, 1736), :]
    )


def chunk_index(index, core, lay):
    start = index * lay.step
    return jnp.stack([index, core, start // 128, start % 128]).astype(jnp.int32)


def pack_own(params, index, core, lay):
    if lay.count != CANON:
        window = jnp.zeros((lay.gains + lay.chunk,), params.dtype)
        window = lax.dynamic_update_slice(window, params, (index * lay.step,))
        payload = pack_payload(window, index, lay)
        return lax.dynamic_slice_in_dim(payload, core * lay.half, lay.half, 0)
    flat = jnp.pad(params, (0, 1736 * 128 - lay.shard)).reshape(1736, 128)
    vmem = pl.BlockSpec(memory_space=pltpu.VMEM)
    return pl.pallas_call(
        pack_kernel,
        name="pack_own_chunk",
        in_specs=[pl.BlockSpec(memory_space=pltpu.SMEM), vmem],
        out_specs=vmem,
        out_shape=jax.ShapeDtypeStruct((HALF, 128), BF16),
        scratch_shapes=[
            pltpu.VMEM((1760, 128), F32),
            pltpu.VMEM((1744, 128), F32),
            pltpu.VMEM((2 * HALF, 128), F32),
            pltpu.VMEM((NARROW, 128), F32),
        ],
        compiler_params=pltpu.CompilerParams(vmem_limit_bytes=VMEM_LIMIT),
    )(chunk_index(index, core, lay), flat)


def unpack_own(own, twin, index, core, lay):
    if lay.count != CANON:
        rows = jnp.where(core == 0, jnp.stack([own, twin], 0), jnp.stack([twin, own], 0))
        window = unpack_payload(rows.reshape(2 * lay.half, 128), index, lay)
        return lax.dynamic_slice(window, (index * lay.step,), (lay.shard,))
    vmem = pl.BlockSpec(memory_space=pltpu.VMEM)
    rows = pl.pallas_call(
        unpack_kernel,
        name="unpack_own_chunk",
        in_specs=[pl.BlockSpec(memory_space=pltpu.SMEM), vmem, vmem],
        out_specs=vmem,
        out_shape=jax.ShapeDtypeStruct((1736, 128), F32),
        scratch_shapes=[
            pltpu.VMEM((2 * HALF, 128), F32),
            pltpu.VMEM((1752, 128), F32),
            pltpu.VMEM((NARROW, 128), F32),
        ],
        compiler_params=pltpu.CompilerParams(vmem_limit_bytes=VMEM_LIMIT),
    )(chunk_index(index, core, lay), own, twin)
    return rows.reshape(-1)[: lay.shard]


def tables(positions):
    cosine, sine = rope_tables(positions)
    return jnp.concatenate([cosine, cosine], 1), jnp.concatenate([-sine, sine], 1)


def layer_kernels(length, width):
    groups = length // SEQ_LEN * KV_HEADS
    kv_width = KV_HEADS * HEAD
    smem = pl.BlockSpec(memory_space=pltpu.SMEM)
    vmem = pl.BlockSpec(memory_space=pltpu.VMEM)
    hbm = pl.BlockSpec(memory_space=pltpu.HBM)
    anywhere = pl.BlockSpec(memory_space=pl.ANY)
    params = pltpu.CompilerParams(vmem_limit_bytes=VMEM_LIMIT)

    def sds(shape, dtype):
        return jax.ShapeDtypeStruct(shape, dtype)

    def cost(flops):
        return pl.CostEstimate(flops=flops, bytes_accessed=8_000_000, transcendentals=600_000)

    piece, block = sds((4, HALF, 128), BF16), sds((2, HALF, 128), BF16)
    weights = [sds((width, width), BF16), sds((width, kv_width), BF16)]
    weights = weights + [weights[1], weights[0]]
    saved = [
        sds((groups, 3 * SEQ_LEN, SEQ_LEN), F32),
        sds((groups, 3 * SEQ_LEN, HEAD), BF16),
        sds((groups, SEQ_LEN, HEAD), BF16),
        sds((groups, SEQ_LEN, HEAD), BF16),
    ]
    rows = sds((length, width), F32)
    low_rows = sds((length, width), BF16)
    gain = sds((1, width), F32)
    outs = [rows, rows, gain, low_rows] + saved + weights + [gain]
    forward = pl.pallas_call(
        first_kernel,
        name="forward_and_ff_backward",
        in_specs=[smem] + [hbm] * 14 + [hbm, vmem, vmem, hbm],
        out_specs=[hbm] * len(outs) + [anywhere] * 10,
        out_shape=outs + [block] * 8 + [piece] * 2,
        scratch_shapes=[pltpu.VMEM(out.shape, out.dtype) for out in outs]
        + [
            pltpu.VMEM((CANON, 2 * HALF, 128), BF16),
            pltpu.VMEM((12, 2 * HALF, 128), BF16),
            pltpu.VMEM((width, length), BF16),
            pltpu.VMEM((width, length), BF16),
            pltpu.VMEM((length, width), BF16),
            pltpu.VMEM((length, width), F32),
            pltpu.VMEM((length, width), BF16),
            pltpu.VMEM((width, length), BF16),
            pltpu.VMEM((length, width), F32),
            pltpu.VMEM((width, 128), F32),
            pltpu.VMEM((width, 128), F32),
            pltpu.SemaphoreType.DMA((2,)),
            pltpu.SemaphoreType.DMA((4,)),
            pltpu.SemaphoreType.DMA((3,)),
            pltpu.SemaphoreType.DMA((len(outs),)),
        ],
        compiler_params=params,
        cost_estimate=cost(20 * length * width * FF),
    )
    attention_back = pl.pallas_call(
        second_kernel,
        name="attention_backward",
        in_specs=[smem] + [vmem] * 16 + [anywhere] * 2,
        out_specs=[hbm] * 2 + [anywhere] * 6,
        out_shape=[sds((width, length), BF16), sds((width, length), F32)] + [block] * 4 + [piece] * 2,
        scratch_shapes=[
            pltpu.VMEM((4, 2 * HALF, 128), BF16),
            pltpu.VMEM((2, 4, HALF, 128), BF16),
            pltpu.VMEM((width, length), BF16),
            pltpu.VMEM((width, length), F32),
            pltpu.VMEM((length, width), F32),
            pltpu.VMEM((length, kv_width), F32),
            pltpu.VMEM((length, kv_width), F32),
            pltpu.VMEM((width, 128), F32),
            pltpu.VMEM((width, 128), F32),
            pltpu.SemaphoreType.DMA((2,)),
            pltpu.SemaphoreType.DMA((1,)),
            pltpu.SemaphoreType.DMA((3,)),
        ],
        compiler_params=pltpu.CompilerParams(vmem_limit_bytes=60 * 1024 * 1024),
        cost_estimate=cost(10 * length * width * width),
    )
    return forward, attention_back


def flat_of(payloads, lay):
    n = lay.count
    heads = payloads[:, lay.rows : lay.rows + 10]
    flats = [unhead_narrow(heads[0])]
    for i in range(n):
        wide = n // 4 <= i < 3 * n // 4
        body = payloads[i, : lay.rows]
        flat = unpack_wide(body, FF) if wide else unpack_narrow(body)
        if i + 1 < n:
            tail = unhead_wide(heads[i + 1]) if wide else unhead_narrow(heads[i + 1])
            flat = jnp.concatenate([flat[: -lay.gains], flat[-lay.gains :] + tail])
        flats.append(flat)
    return jnp.concatenate(flats)


def payloads_of(flat, lay):
    windows = [
        flat[i * lay.chunk : (i + 1) * lay.chunk + lay.gains] for i in range(lay.count)
    ]
    return jnp.stack([pack_payload(window, i, lay) for i, window in enumerate(windows)], 0)


def canonical(blocks, twins, lay, canon, index, core):
    sides = []
    for side in (blocks, twins):
        side = jnp.stack([jnp.concatenate(value, 0) for value in side], 0)
        sides.append(side.reshape(lay.count, lay.half, 128))
    both = jnp.where(core == 0, jnp.stack(sides, 1), jnp.stack(sides[::-1], 1))
    both = both.reshape(lay.count, 2 * lay.half, 128)
    both = jnp.take(both, jnp.arange(lay.count, dtype=jnp.int32) ^ index, axis=0)
    flat = flat_of(both, lay)
    zeros = jnp.zeros((canon.gains,), flat.dtype)
    rows = []
    for i in range(CANON):
        window = flat[i * canon.chunk : (i + 1) * canon.chunk + canon.gains]
        if i:
            window = jnp.concatenate([zeros, window[canon.gains :]])
        rows.append(pack_payload(window, i, canon))
    rows = jnp.stack(rows, 0).reshape(PLANES, 4, 2, canon.half, 128)
    pieces = []
    for c in range(2):
        side = rows[:, :, c]
        pieces = pieces + [side[0]] + [side[p, :2] for p in range(1, PLANES)]
        pieces = pieces + [side[p, 2:] for p in range(1, PLANES)]
    return pieces


def from_canonical(slots, lay, canon, place, core):
    sides = []
    for which in range(2):
        sides.append(jnp.stack([slot[which] for slot in slots], 0))
    rows = jnp.stack(sides, 2).reshape(CANON, 2 * canon.half, 128)
    flats = [unhead_narrow(rows[0, canon.rows : canon.rows + 10])]
    for i in range(CANON):
        body = rows[i, : canon.rows]
        flats.append(unpack_wide(body, FF) if 4 <= i < 12 else unpack_narrow(body))
    rows = payloads_of(jnp.concatenate(flats), lay)
    rows = rows.reshape(PLANES, lay.in_plane, 2, lay.half, 128)
    rows = jnp.take(rows, jnp.arange(lay.in_plane, dtype=jnp.int32) ^ place, axis=1)
    rows = rows.reshape(PLANES, 1 << lay.y_bits, 1 << lay.x_bits, 2, lay.half, 128)
    sides = [jnp.take(rows, side, axis=3) for side in (core, 1 - core)]
    return [[list(side[p]) for p in range(PLANES)] for side in sides]


def add(left, right):
    return left.astype(F32) + right.astype(F32)


def on_device(lay, canon, tokens_in, positions, params, cotangent):
    index = lax.axis_index("dp")
    core = lax.axis_index("rep")
    n, half, in_plane = lay.count, lay.half, lay.in_plane
    plane, place = index // in_plane, index % in_plane
    same = n == CANON
    firsts, seconds = hops(lay)
    forward, attention_back = layer_kernels(*tokens_in.shape)
    mine = pack_own(params, index, core, lay)
    angles = tables(positions)
    if same:
        idx = jnp.stack([plane, place, core, 1]).astype(jnp.int32)
        pieces, angles = balanced_gather(mine, lay, angles)
    else:
        idx = jnp.zeros((4,), jnp.int32)
        blocks = gather(mine, lay)
        twins = [[swap_rep(block) for block in value] for value in blocks]
        pieces = canonical(blocks, twins, lay, canon, index, core)
    results = forward(idx, *pieces, tokens_in.T, *angles, cotangent.T)
    d_gain = results[2]
    saved, slots, held = results[:13], (results[13:17], results[17:21]), results[21:23]
    if same:
        (first,), (second,) = firsts, seconds
        moved = [hop(add(far, swap_rep(send)).astype(BF16), second, n) for _, far, _, send in slots]
        near = [add(keep, swap_rep(send)) for keep, _, send, _ in slots]
    output, d_input, *results = attention_back(idx, tokens_in.T, *angles, *saved, *held)
    output, d_input = output.T, d_input.T
    keep_near, keep_far, send_near, send_far, keep, send = results
    if same:
        moved, send_far, send_near, send = lax.optimization_barrier((moved, send_far, send_near, send))
        third = hop(add(keep_far, swap_rep(send_far)).astype(BF16), second, n)
        early = [(near[j] + moved[j].astype(F32)).astype(BF16) for j in range(2)]
        early = [add(value[0], hop(value[1], first, n)).astype(BF16) for value in early]
        third = (add(keep_near, swap_rep(send_near)) + third.astype(F32)).astype(BF16)
        third = add(third[0], hop(third[1], first, n)).astype(BF16)
        keep, send = [jnp.where(plane == 0, a, b) for a, b in zip((keep, send), held)]
        mine = add(keep, swap_rep(send)).astype(BF16)

        def pick(values, s):
            table = ((0, 1, 2), (2, 1, 0), (1, 2, 0), (1, 0, 2))
            result = values[table[3][s - 1]]
            for z in range(3):
                result = jnp.where(plane == z, values[table[z][s - 1]], result)
            return result

        mine, third = lax.optimization_barrier((mine, third))
        planes = early + [third]
        parts = [swap(pick(planes, s), s << (lay.bits - 2), n) for s in range(1, PLANES)]
        both = tuple(a ^ b for a, b in zip(first, second))
        inner = [hop(mine[d], masks, n) for d, masks in ((1, first), (2, second), (3, both))]
        parts, inner = lax.optimization_barrier((parts, inner))
        total = (add(mine[0], inner[0]) + add(inner[1], inner[2])) + (
            parts[0].astype(F32) + add(parts[1], parts[2])
        )
    else:
        slots = [(near, far, other, last) for near, far, other, last in slots]
        slots.append((keep_near, keep_far, send_near, send_far))
        planes = [(keep, send)]
        for near, far, other, last in slots:
            planes.append((jnp.concatenate([near, far], 0), jnp.concatenate([other, last], 0)))
        keeps, sends = from_canonical(planes, lay, canon, place, core)
        moved = []
        for keep, send in zip(keeps, sends):
            pair = pair_sum(keep, send)
            moved.append(add_blocks(pair[0], send_blocks(pair, seconds, n)))
        blocks = split_first(moved, lay)
        planes = add_blocks(blocks[0], send_blocks(blocks, firsts, n))
        total = reduce_planes(planes, plane, lay)
    other = swap_rep(total)
    if same:
        at = ROWS + 26 - HALF
        d_gain = jnp.where(core == 1, total[at : at + 5], other[at : at + 5]).reshape(-1)[: lay.width]
    else:
        d_gain = sum_everywhere(d_gain[0], lay)
    return output, d_input, unpack_own(total, other, index, core, lay), d_gain


def solution(mesh):
    def run(tokens_in, positions, params, cotangent):
        total, width = params.shape[0], tokens_in.shape[1]
        lay = Layout(mesh.shape["dp"], total, width)
        canon = Layout(CANON, total, width)
        rows = P(("dp", "rep"), None)
        return jax.shard_map(
            lambda *args: on_device(lay, canon, *args),
            mesh=mesh,
            in_specs=(rows, P(("dp", "rep")), P("dp"), rows),
            out_specs=(rows, rows, P("dp"), P()),
            check_vma=False,
        )(tokens_in, positions, params, cotangent)

    return run
```

```python
import jax
import jax.numpy as jnp
from jax import lax
from jax.experimental import pallas as pl
from jax.experimental.pallas import tpu as pltpu
from jax.sharding import PartitionSpec as P

HEADS = 9
KV_HEADS = 3
HEAD = 64
FF = 1536
SEQ_LEN = 128
PLANES = 4
CANON = 16

EPS = 1e-05
ROPE_BASE = 100000.0

F32, BF16 = jnp.float32, jnp.bfloat16
ROWS, HALF = 1728, 880
MAIN, REST = 768, 112
NARROW, WIDE = 384, 144
VMEM_LIMIT = 52 * 1024 * 1024


class Layout:
    def __init__(self, count, total, width):
        self.count = count
        self.width = width
        self.gains = 2 * width
        self.shard = total // count
        self.chunk = (total - self.gains) // count
        self.step = self.gains // count
        self.rows = self.chunk // 128
        half = -(-(self.rows + 10) // 2)
        self.half = -(-half // 16) * 16
        self.first = -(-(self.half // 2) // 16) * 16
        self.extra = 2 * self.half - self.rows
        self.bits = count.bit_length() - 1
        rest = self.bits - 2
        self.x_bits = -(-rest // 2)
        self.y_bits = rest - self.x_bits
        self.in_plane = 1 << rest
        self.flip = self.x_bits == self.y_bits


def pack_wide(flat, width):
    panels = width // 128
    return flat.reshape(-1, panels, 128).transpose(1, 0, 2).reshape(-1, 128)


def unpack_wide(rows, width):
    panels = width // 128
    return rows.reshape(panels, -1, 128).transpose(1, 0, 2).reshape(-1)


def pack_narrow(flat):
    rows = flat.reshape(-1, 576)
    count = rows.shape[0]
    panels = rows[:, :512].reshape(count, 4, 128).transpose(1, 0, 2).reshape(-1, 128)
    tail = rows[:, 512:]
    return jnp.concatenate([panels, jnp.concatenate([tail[: count // 2], tail[count // 2 :]], 1)], 0)


def unpack_narrow(packed):
    count = packed.shape[0] * 2 // 9
    panels = packed[: 4 * count].reshape(4, count, 128).transpose(1, 0, 2).reshape(count, 512)
    half = packed[4 * count :]
    tail = jnp.concatenate([half[:, :64], half[:, 64:]], 0)
    return jnp.concatenate([panels, tail], 1).reshape(-1)


def head_narrow(flat):
    rows = flat.reshape(2, 576)
    tail = jnp.pad(rows[:, 512:], ((0, 0), (64, 0)))
    return jnp.concatenate([rows[:, :512].reshape(8, 128), tail], 0)


def unhead_narrow(rows):
    return jnp.concatenate([rows[:8].reshape(2, 512), rows[8:10, 64:]], 1).reshape(-1)


def head_wide(flat):
    return jnp.pad(flat.reshape(9, 128), ((0, 1), (0, 0)))


def unhead_wide(rows):
    return rows[:9].reshape(-1)


def is_wide(index, count):
    return (index >= count // 4) & (index < 3 * count // 4)


def pack_payload(window, index, lay):
    head, chunk = window[: lay.gains], window[lay.gains :]
    body = jnp.where(is_wide(index, lay.count), pack_wide(chunk, FF), pack_narrow(chunk))
    top = jnp.where(is_wide(index - 1, lay.count), head_wide(head), head_narrow(head))
    return jnp.concatenate([body, jnp.pad(top, ((0, lay.extra - 10), (0, 0)))], 0)


def unpack_payload(rows, index, lay):
    body, top = rows[: lay.rows], rows[lay.rows : lay.rows + 10]
    chunk = jnp.where(is_wide(index, lay.count), unpack_wide(body, FF), unpack_narrow(body))
    head = jnp.where(is_wide(index - 1, lay.count), unhead_wide(top), unhead_narrow(top))
    return jnp.concatenate([head, chunk])


def swap(value, mask, count):
    return lax.ppermute(value, "dp", [(i, i ^ mask) for i in range(count)])


def swap_rep(value):
    return lax.ppermute(value, "rep", [(0, 1), (1, 0)])


def hop(value, masks, count):
    pairs = [(2 * i + c, 2 * (i ^ masks[c]) + c) for i in range(count) for c in range(2)]
    return lax.ppermute(value, ("dp", "rep"), pairs)


def hops(lay):
    xs = [d for d in range(1, 1 << lay.x_bits)]
    ys = [e << lay.x_bits for e in range(1, 1 << lay.y_bits)]
    if lay.flip:
        return list(zip(xs, ys)), list(zip(ys, xs))
    return list(zip(xs, xs)), list(zip(ys, ys))


def gather_hops(value, masks, count):
    return jnp.stack([value] + [hop(value, pair, count) for pair in masks], 0)


def gather(half, lay):
    n = lay.count
    first, second = hops(lay)
    planes = [half] + [swap(half, s << (lay.bits - 2), n) for s in range(1, PLANES)]
    blocks = []
    for plane in planes:
        block = gather_hops(plane, first, n)
        blocks.append([block] + [hop(block, masks, n) for masks in second])
    return blocks


def balanced_gather(half, lay, beside):
    n = lay.count
    (first,), (second,) = hops(lay)
    both = tuple(a ^ b for a, b in zip(first, second))
    across = [swap(half, s << (lay.bits - 2), n) for s in range(1, PLANES)]
    plane = [hop(half, masks, n) for masks in (first, second, both)]
    across, plane, beside = lax.optimization_barrier((across, plane, beside))
    own = jnp.stack([half] + plane, 0)
    near = [jnp.stack([value, hop(value, first, n)], 0) for value in across]
    far = [hop(value, second, n) for value in near]
    early = [own] + near
    far[0], twins = lax.optimization_barrier(
        (far[0], [swap_rep(value) for value in early + far[1:]])
    )
    return early + far + twins[:4] + [swap_rep(far[0])] + twins[4:], beside


def pair_sum(keep, send):
    return [
        (mine.astype(F32) + swap_rep(other).astype(F32)).astype(BF16)
        for mine, other in zip(keep, send)
    ]


def send_blocks(blocks, masks, count):
    return [hop(block, pair, count) for block, pair in zip(blocks[1:], masks)]


def add_blocks(block, arrived):
    total = block.astype(F32)
    for value in arrived:
        total = total + value.astype(F32)
    return total.astype(BF16)


def split_first(planes, lay):
    return [jnp.stack([value[j] for value in planes], 0) for j in range(len(hops(lay)[0]) + 1)]


def reduce_planes(planes, plane, lay):
    parts = [jnp.take(planes, plane, axis=0).astype(F32)]
    for s in range(1, PLANES):
        part = swap(jnp.take(planes, plane ^ s, axis=0), s << (lay.bits - 2), lay.count)
        parts.append(part.astype(F32))
    return (parts[0] + parts[1]) + (parts[2] + parts[3])


def sum_everywhere(value, lay):
    value = value + swap_rep(value)
    for bit in range(lay.bits):
        value = value + swap(value, 1 << bit, lay.count)
    return value


def rope_tables(places):
    expon = jnp.arange(HEAD // 2).astype(jnp.float32) * (2.0 / HEAD)
    inverse = jnp.power(ROPE_BASE, -expon)
    angle = places.astype(jnp.float32)[..., None] * inverse
    return (jnp.cos(angle), jnp.sin(angle))


def dot(left, right):
    return jnp.dot(left, right, preferred_element_type=F32)


def dot_nt(left, right):
    return lax.dot_general(left, right, (((1,), (1,)), ((), ())), preferred_element_type=F32)


def dot_tn(left, right):
    return lax.dot_general(left, right, (((0,), (0,)), ((), ())), preferred_element_type=F32)


def row_of_head(head, which):
    parts = [head[4 * which + j : 4 * which + j + 1] for j in range(4)]
    return jnp.concatenate(parts + [head[8 + which : 9 + which, 64:]], 1)


def head_of_rows(rows):
    parts = [row[:, 128 * j : 128 * j + 128] for row in rows for j in range(4)]
    zeros = jnp.zeros((1, 64), F32)
    parts = parts + [jnp.concatenate([zeros, row[:, 512:]], 1) for row in rows]
    return jnp.concatenate(parts + [jnp.zeros((6, 128), F32)], 0)


def gain_rows(gain, low):
    parts = [gain[:, 128 * j : 128 * j + 128] for j in range(4)]
    parts = parts + [jnp.concatenate([gain[:, 512:], gain[:, 512:]], 1)]
    return jnp.concatenate([low[:10]] + parts + [jnp.zeros((1, 128), F32)], 0)


def load_narrow(ref, index):
    parts = [ref[index, NARROW * j : NARROW * (j + 1), :] for j in range(4)]
    half = ref[index, 4 * NARROW : ROWS, :]
    tail = jnp.concatenate([half[:, :64], half[:, 64:]], 0)
    return jnp.concatenate(parts + [tail], 1)


def store_narrow(ref, index, value):
    for j in range(4):
        ref[index, NARROW * j : NARROW * (j + 1), :] = value[:, 128 * j : 128 * (j + 1)].astype(BF16)
    tail = value[:, 512:]
    tail = jnp.concatenate([tail[: NARROW // 2], tail[NARROW // 2 :]], 1)
    ref[index, 4 * NARROW : ROWS, :] = tail.astype(BF16)


def narrow_tiles():
    tiles = [(NARROW * (j + 1) - 16, j, 4 + j) for j in range(4)]
    return tiles + [(ROWS - 16, 8, 9)]


def add_tail(ref, index, wide):
    head = ref[index + 1, ROWS : ROWS + 16, :].astype(F32)
    row = lax.broadcasted_iota(jnp.int32, (16, 128), 0)
    if wide:
        for k in range(9):
            at = WIDE * (4 + k) - 16
            tile = ref[index, at : at + 16, :].astype(F32)
            tile = tile + jnp.where(row == 15, head[k : k + 1], 0.0)
            ref[index, at : at + 16, :] = tile.astype(BF16)
    else:
        for at, upper, lower in narrow_tiles():
            tile = ref[index, at : at + 16, :].astype(F32)
            tile = tile + jnp.where(row == 14, head[upper : upper + 1], 0.0)
            tile = tile + jnp.where(row == 15, head[lower : lower + 1], 0.0)
            ref[index, at : at + 16, :] = tile.astype(BF16)


def tail_of(ref, index, wide):
    if wide:
        parts = []
        for k in range(9):
            at = WIDE * (4 + k) - 16
            parts.append(ref[index, at : at + 16, :].astype(F32)[15:16])
        return jnp.concatenate(parts + [jnp.zeros((7, 128), F32)], 0)
    tiles = [ref[index, at : at + 16, :].astype(F32) for at, _, _ in narrow_tiles()]
    parts = [tile[14:15] for tile in tiles[:4]] + [tile[15:16] for tile in tiles[:4]]
    parts = parts + [tiles[4][14:15], tiles[4][15:16]]
    return jnp.concatenate(parts + [jnp.zeros((6, 128), F32)], 0)


def spread(value, first, second, out):
    for m in range(3):
        part = value[:, 192 * m : 192 * (m + 1)].astype(F32)
        first[pl.ds(m, 192, stride=3), :] = part[:, :128]
        second[pl.ds(m, 192, stride=3), :] = jnp.concatenate([part[:, 128:], part[:, 128:]], 1)
    out[:, :128] = first[:576, :].astype(BF16)
    out[:, 128:] = second[:576, :64].astype(BF16)


def unspread(value, first, second):
    first[:576, :] = value[:, :128]
    second[:576, :] = jnp.concatenate([value[:, 128:], value[:, 128:]], 1)
    parts = []
    for m in range(3):
        parts.append(first[pl.ds(m, 192, stride=3), :])
        parts.append(second[pl.ds(m, 192, stride=3), :][:, :64])
    return jnp.concatenate(parts, 1)


def turn(vector, cosine, sine):
    swapped = jnp.concatenate([vector[:, 32:], vector[:, :32]], 1)
    return vector * cosine + swapped * sine


def piece_copies(idx, at_plane, sides, dst, sem, outward):
    place, core, flip = idx[1], idx[2], idx[3]
    copies = []
    for which, refs in enumerate(sides):
        side = jnp.bitwise_xor(core, which)
        for d in range(4):
            turned = ((d & 1) << 1) | (d >> 1)
            chunk = 4 * at_plane + jnp.bitwise_xor(place, jnp.where(side * flip == 1, turned, d))
            ref = refs[0].at[d] if len(refs) == 1 else refs[d // 2].at[d % 2]
            for start, rows in ((0, MAIN), (MAIN, REST)) if outward else ((0, HALF),):
                outer = ref.at[pl.ds(start, rows), :]
                at = pl.multiple_of(side * HALF + start, 16)
                inner = dst.at[chunk, pl.ds(at, rows), :]
                pair = (inner, outer) if outward else (outer, inner)
                copies.append((start > 0, pltpu.make_async_copy(pair[0], pair[1], sem)))
    return copies


def wait_plane(ref, base, sem):
    whole = ref.at[pl.ds(base, 4)]
    pltpu.make_async_copy(whole, whole, sem).wait()


def slot_plane(plane, slot):
    own = jnp.where(plane == 0, 3, plane)
    low = jnp.where(own == 1, 2, 1)
    return [low, 6 - own - low, own][slot]


def first_kernel(idx, *refs):
    pieces = list(zip(refs[:7], refs[7:14]))
    tok_hbm, cos, sin, cot_hbm = refs[14:18]
    refs = refs[18:]
    results, outs = refs[:13], refs[13:23]
    refs = refs[23:]
    y_acc, dr_out, dg_out, att_out, p_out, q_out, k_out, v_out, wq, wk, wv, wo, gain_out = refs[:13]
    w, g, tok, cot_t, cot, att, n2_ref, n2t_ref, dn_acc, first, second = refs[13:24]
    in_sem, sems, out_sems, result_sems = refs[24:]
    saves = [
        pltpu.make_async_copy(src, dst, result_sems.at[i])
        for i, (src, dst) in enumerate(zip(refs[:13], results))
    ]
    load = pltpu.make_async_copy(tok_hbm, tok, in_sem.at[0])
    load.start()
    load_cot = pltpu.make_async_copy(cot_hbm, cot_t, in_sem.at[1])
    load_cot.start()
    planes = []
    for s in range(PLANES):
        sides = [[ref] for ref in pieces[0]]
        if s:
            sides = list(zip(pieces[s], pieces[s + 3]))
        at_plane = jnp.bitwise_xor(idx[0], s)
        copies = piece_copies(idx, at_plane, sides, w, sems.at[at_plane], False)
        planes.append([copy for _, copy in copies])
    for p in range(PLANES):
        for s in range(PLANES):

            @pl.when(jnp.bitwise_xor(idx[0], s) == p)
            def _(copies=planes[s]):
                for copy in copies:
                    copy.start()

    tokens = tok.shape[1]
    load.wait()
    x = tok[...].astype(F32).T
    normed = x * lax.rsqrt(jnp.mean(x * x, -1, keepdims=True) + EPS)
    load_cot.wait()
    cot[...] = cot_t[...].astype(F32).T.astype(BF16)
    wait_plane(w, 0, sems.at[0])
    for c in range(3):
        add_tail(w, c, False)
    gains = w[0, ROWS : ROWS + 16, :].astype(F32)
    gain_in, gain_mid = row_of_head(gains, 0), row_of_head(gains, 1)
    gain_out[...] = gain_in
    n1 = (normed * gain_in).astype(BF16)
    wq[:NARROW, :] = load_narrow(w, 0)
    mixed_chunk = load_narrow(w, 1)
    wq[NARROW:, :] = mixed_chunk[:192]
    spread(mixed_chunk[192:], first, second, wk)
    mixed_chunk = load_narrow(w, 2)
    spread(mixed_chunk[:192], first, second, wv)
    wo[:192, :] = mixed_chunk[192:]

    query, keys, values = dot(n1, wq[...]), dot(n1, wk[...]), dot(n1, wv[...])
    row = lax.broadcasted_iota(jnp.int32, (3 * SEQ_LEN, SEQ_LEN), 0)
    causal = jnp.bitwise_and(row, SEQ_LEN - 1) >= lax.broadcasted_iota(
        jnp.int32, (3 * SEQ_LEN, SEQ_LEN), 1
    )
    for b in range(tokens // SEQ_LEN):
        part = slice(SEQ_LEN * b, SEQ_LEN * (b + 1))
        cosine, sine = cos[part, :], sin[part, :]
        for kv in range(KV_HEADS):
            at = KV_HEADS * b + kv
            heads = [
                turn(query[part, HEAD * h : HEAD * (h + 1)], cosine, sine)
                for h in range(3 * kv, 3 * kv + 3)
            ]
            q3 = jnp.concatenate(heads, 0).astype(BF16)
            k1 = turn(keys[part, HEAD * kv : HEAD * (kv + 1)], cosine, sine).astype(BF16)
            v1 = values[part, HEAD * kv : HEAD * (kv + 1)].astype(BF16)
            q_out[at], k_out[at], v_out[at] = q3, k1, v1
            score = jnp.where(causal, dot_nt(q3, k1) * HEAD**-0.5, -1e30)
            expon = jnp.exp(score - jnp.max(score, -1, keepdims=True))
            probs = expon / jnp.sum(expon, -1, keepdims=True)
            p_out[at] = probs
            mix = dot(probs.astype(BF16), v1)
            for r in range(3):
                h = 3 * kv + r
                att[part, HEAD * h : HEAD * (h + 1)] = mix[SEQ_LEN * r : SEQ_LEN * (r + 1)]
    attended = att[...].astype(BF16)
    att_out[...] = attended
    wait_plane(w, 4, sems.at[1])
    add_tail(w, 3, False)
    wo[192:, :] = load_narrow(w, 3)
    for copy in saves[3:]:
        copy.start()
    mixed = x + dot(attended, wo[...])
    inverse = lax.rsqrt(jnp.mean(mixed * mixed, -1, keepdims=True) + EPS)
    normed_mid = mixed * inverse
    n2 = normed_mid * gain_mid
    n2_ref[...] = n2.astype(BF16)
    n2t_ref[...] = n2.astype(BF16).astype(F32).T.astype(BF16)
    y_acc[...] = mixed
    dn_acc[...] = jnp.zeros_like(dn_acc)
    wait_plane(w, 8, sems.at[2])
    wait_plane(w, 12, sems.at[3])

    def fix(i, carry):
        add_tail(w, i + 4, True)
        return carry

    lax.fori_loop(0, 8, fix, 0)
    for c in (12, 13, 14):
        add_tail(w, c, False)

    def block(k, carry):
        def wide(base, p):
            at = pl.multiple_of((6 * k + p) * WIDE, 16)
            return jnp.concatenate([w[base + d, pl.ds(at, WIDE), :] for d in range(4)], 0)

        w_gate = jnp.concatenate([wide(4, p) for p in range(6)], 1)
        w_up = jnp.concatenate([wide(8, p) for p in range(6)], 1)
        w_down = jnp.concatenate([load_narrow(w, 12 + 2 * k), load_narrow(w, 13 + 2 * k)], 0)
        c = cot[...]
        gate, up = dot(n2_ref[...], w_gate), dot(n2_ref[...], w_up)
        sigma = 1.0 / (1.0 + jnp.exp(-gate))
        silu = gate * sigma
        hidden = (silu * up).astype(BF16)
        y_acc[...] += dot(hidden, w_down)
        d_down = dot_tn(hidden, c)
        store_narrow(g, 8 + 2 * k, d_down[:NARROW])
        store_narrow(g, 9 + 2 * k, d_down[NARROW:])
        d_hidden = dot_nt(c, w_down)
        d_gate = (d_hidden * up * sigma * (1.0 + gate * (1.0 - sigma))).astype(BF16)
        d_up = (d_hidden * silu).astype(BF16)
        dn_acc[...] += dot_nt(d_gate, w_gate) + dot_nt(d_up, w_up)
        for base, d_out in ((0, d_gate), (4, d_up)):
            grad = dot(n2t_ref[...], d_out).astype(BF16)
            for p in range(6):
                at = pl.multiple_of((6 * k + p) * WIDE, 16)
                for d in range(4):
                    g[base + d, pl.ds(at, WIDE), :] = grad[
                        WIDE * d : WIDE * (d + 1), 128 * p : 128 * (p + 1)
                    ]
        return carry

    lax.fori_loop(0, 2, block, 0)
    stores = []
    for slot in range(3):
        sides = [outs[4 * slot : 4 * slot + 2], outs[4 * slot + 2 : 4 * slot + 4]]
        if slot == 2:
            sides = [outs[8:9], outs[9:10]]
        at_plane = slot_plane(idx[0], slot) - 1
        stores = stores + piece_copies(idx, at_plane, sides, g, out_sems.at[slot], True)
    for last, copy in stores:
        if not last:
            copy.start()
    d_norm = dn_acc[...]
    d_gain = jnp.sum(d_norm * normed_mid, 0, keepdims=True)
    dg_out[...] = d_gain
    scaled = d_norm * gain_mid
    d_mixed = cot[...].astype(F32) + inverse * (
        scaled - normed_mid * jnp.mean(scaled * normed_mid, -1, keepdims=True)
    )
    last_rows = dot_tn(att_out[:, 512:], d_mixed.astype(BF16))
    for c in range(12):
        if c:
            top = tail_of(g, c - 1, c - 1 < 8)
        else:
            top = head_of_rows([last_rows[62:63], last_rows[63:64]])
        g[c, ROWS : ROWS + 16, :] = top.astype(BF16)
        g[c, ROWS + 16 :, :] = gain_rows(d_gain, jnp.zeros((16, 128), F32)).astype(BF16)
    for last, copy in stores:
        if last:
            copy.start()
    dr_out[...] = d_mixed
    for copy in saves[:3]:
        copy.start()
    for copy in saves:
        copy.wait()
    for slot in range(3):
        wait_plane(g, 4 * slot, out_sems.at[slot])


def second_kernel(idx, *refs):
    tok, cos, sin, y_in, dr, dg, att, p_in, q_in, k_in, v_in, wq, wk, wv, wo, gain = refs[:16]
    held, (y_out, dx_out), third, mine = refs[16:18], refs[18:20], refs[20:24], refs[24:26]
    g, bounce, y_t, dx_t, dq_ref, dk_ref, dv_ref, first, second, in_sem, out_sems, held_sem = refs[26:]
    tokens = tok.shape[1]
    ground = idx[0] == 0
    fetch = [
        pltpu.make_async_copy(held[side], bounce.at[side], held_sem.at[side]) for side in range(2)
    ]

    @pl.when(ground)
    def _():
        for copy in fetch:
            copy.start()

    d_mixed = dr[...]
    branch = d_mixed.astype(BF16)
    dw_out = dot_tn(att[...], branch)
    d_att = dot_nt(branch, wo[...])
    @pl.when(ground)
    def _():
        for copy in fetch:
            copy.wait()
        for side in range(2):
            for j in range(2):
                source = bounce.at[side, pl.ds(2 * j, 2)]
                pltpu.make_async_copy(source, third[2 * side + j], held_sem.at[2]).start()

    for b in range(tokens // SEQ_LEN):
        part = slice(SEQ_LEN * b, SEQ_LEN * (b + 1))
        cosine, sine = cos[part, :], -sin[part, :]
        for kv in range(KV_HEADS):
            at = KV_HEADS * b + kv
            heads = [d_att[part, HEAD * h : HEAD * (h + 1)] for h in range(3 * kv, 3 * kv + 3)]
            d3 = jnp.concatenate(heads, 0).astype(BF16)
            probs, q3, k1, v1 = p_in[at], q_in[at], k_in[at], v_in[at]
            d_probs = dot_nt(d3, v1)
            dv_ref[part, HEAD * kv : HEAD * (kv + 1)] = dot_tn(probs.astype(BF16), d3)
            inner = jnp.sum(d_probs * probs, -1, keepdims=True)
            d_score = (probs * (d_probs - inner)).astype(BF16)
            dq3 = dot(d_score, k1) * HEAD**-0.5
            for r in range(3):
                h = 3 * kv + r
                dq_ref[part, HEAD * h : HEAD * (h + 1)] = turn(
                    dq3[SEQ_LEN * r : SEQ_LEN * (r + 1)], cosine, sine
                )
            dk_ref[part, HEAD * kv : HEAD * (kv + 1)] = turn(
                dot_tn(d_score, q3) * HEAD**-0.5, cosine, sine
            )
    dq, dk, dv = dq_ref[...].astype(BF16), dk_ref[...].astype(BF16), dv_ref[...].astype(BF16)
    x = tok[...].astype(F32)
    inverse = lax.rsqrt(jnp.mean(x * x, 0, keepdims=True) + EPS)
    normed = x * inverse
    gain_column = jnp.broadcast_to(gain[...], (8, gain.shape[1])).T[:, :1]
    n1t = (normed * gain_column).astype(BF16)
    dw_query = dot(n1t, dq)
    store_narrow(g, 0, dw_query[:NARROW])
    dw = unspread(dot(n1t, dk), first, second)
    store_narrow(g, 1, jnp.concatenate([dw_query[NARROW:], dw], 0))
    dw = unspread(dot(n1t, dv), first, second)
    store_narrow(g, 2, jnp.concatenate([dw, dw_out[:192]], 0))
    store_narrow(g, 3, dw_out[192:])
    d_norm = dot_nt(wq[...], dq) + dot_nt(wk[...], dk) + dot_nt(wv[...], dv)
    d_gain = jnp.sum(d_norm * normed, 1, keepdims=True)
    d_gain = jnp.broadcast_to(d_gain, (d_gain.shape[0], 128)).T[:1]
    for c in range(4):
        top = tail_of(g, c - 1, False) if c else head_of_rows([d_gain, dg[...]])
        g[c, ROWS : ROWS + 16, :] = top.astype(BF16)
        g[c, ROWS + 16 :, :] = gain_rows(dg[...], jnp.zeros((16, 128), F32)).astype(BF16)

    @pl.when(ground)
    def _():
        for _, copy in piece_copies(idx, 0, [mine[:1], mine[1:]], g, out_sems.at[0], True):
            copy.start()

    @pl.when(jnp.logical_not(ground))
    def _():
        for _, copy in piece_copies(idx, 0, [third[:2], third[2:]], g, out_sems.at[0], True):
            copy.start()

    scaled = d_norm * gain_column
    dx_t[...] = d_mixed.T + inverse * (
        scaled - normed * jnp.mean(scaled * normed, 0, keepdims=True)
    )
    y_t[...] = y_in[...].T.astype(BF16)
    stores = [
        pltpu.make_async_copy(src, dst, in_sem.at[i])
        for i, (src, dst) in enumerate(((dx_t, dx_out), (y_t, y_out)))
    ]
    for copy in stores:
        copy.start()
    for copy in stores:
        copy.wait()
    wait_plane(g, 0, out_sems.at[0])

    @pl.when(ground)
    def _():
        wait_plane(g, 0, held_sem.at[2])


def halves_turned(low, high):
    lane = lax.broadcasted_iota(jnp.int32, low.shape, 1)
    return jnp.where(lane < 64, pltpu.roll(low, 64, 1), pltpu.roll(high, 64, 1))


def pack_kernel(idx, flat, out, rolled, window, packed, mixed):
    index, core, down, right = idx[0], idx[1], idx[2], idx[3]
    lane = lax.broadcasted_iota(jnp.int32, (1, 128), 1)
    rolled[0:16, :] = jnp.zeros((16, 128), F32)
    rolled[16:1752, :] = pltpu.roll(flat[...].astype(F32), right, 1)
    rolled[1752:1760, :] = jnp.zeros((8, 128), F32)
    window[:1744, :] = jnp.where(
        lane >= right, rolled[pl.ds(16 - down, 1744), :], rolled[pl.ds(15 - down, 1744), :]
    )
    head = [window[k : k + 1, :] for k in range(9)]
    wide = (index >= 4) & (index < 12)

    @pl.when(wide)
    def _():
        for j in range(12):
            packed[WIDE * j : WIDE * (j + 1), :] = window[pl.ds(9 + j, WIDE, stride=12), :]

    @pl.when(jnp.logical_not(wide))
    def _():
        parts = [window[pl.ds(9 + k, NARROW // 2, stride=9), :] for k in range(9)]
        for j in range(4):
            packed[pl.ds(NARROW * j, NARROW // 2, stride=2), :] = parts[j]
            packed[pl.ds(NARROW * j + 1, NARROW // 2, stride=2), :] = halves_turned(
                parts[4 + j], parts[5 + j]
            )
        mixed[pl.ds(0, NARROW // 2, stride=2), :] = parts[4]
        mixed[pl.ds(1, NARROW // 2, stride=2), :] = pltpu.roll(parts[8], 64, 1)
        packed[4 * NARROW : ROWS, :] = jnp.where(
            lane < 64, mixed[: NARROW // 2, :], pltpu.roll(mixed[NARROW // 2 : NARROW, :], 64, 1)
        )

    last = jnp.zeros((23, 128), F32)
    after_wide = (index >= 5) & (index < 13)

    @pl.when(after_wide)
    def _():
        packed[ROWS:, :] = jnp.concatenate(head + [last], 0)

    @pl.when(jnp.logical_not(after_wide))
    def _():
        rows = head[:4] + [halves_turned(head[4 + j], head[5 + j]) for j in range(4)]
        rows.append(jnp.where(lane < 64, 0.0, pltpu.roll(head[4], 64, 1)))
        rows.append(jnp.where(lane < 64, 0.0, head[8]))
        packed[ROWS:, :] = jnp.concatenate(rows + [last[:22]], 0)

    out[...] = packed[pl.ds(pl.multiple_of(core * HALF, 16), HALF), :].astype(BF16)


def unpack_kernel(idx, own, twin, out, packed, window, mixed):
    index, core, down, left = idx[0], idx[1], idx[2], idx[3]
    lane = lax.broadcasted_iota(jnp.int32, (1, 128), 1)
    packed[pl.ds(pl.multiple_of(core * HALF, 16), HALF), :] = own[...]
    packed[pl.ds(pl.multiple_of((1 - core) * HALF, 16), HALF), :] = twin[...]
    head = [packed[ROWS + k : ROWS + k + 1, :] for k in range(10)]
    window[1737:, :] = jnp.zeros((15, 128), F32)
    wide = (index >= 4) & (index < 12)

    @pl.when(wide)
    def _():
        for j in range(12):
            window[pl.ds(9 + j, WIDE, stride=12), :] = packed[WIDE * j : WIDE * (j + 1), :]

    @pl.when(jnp.logical_not(wide))
    def _():
        half = packed[4 * NARROW : ROWS, :]
        mixed[: NARROW // 2, :] = half
        mixed[NARROW // 2 : NARROW, :] = pltpu.roll(half, 64, 1)
        odd = []
        for j in range(4):
            window[pl.ds(9 + j, NARROW // 2, stride=9), :] = packed[
                pl.ds(NARROW * j, NARROW // 2, stride=2), :
            ]
            odd.append(pltpu.roll(packed[pl.ds(NARROW * j + 1, NARROW // 2, stride=2), :], 64, 1))
        odd.append(mixed[pl.ds(1, NARROW // 2, stride=2), :])
        before = mixed[pl.ds(0, NARROW // 2, stride=2), :]
        for j in range(4):
            window[pl.ds(13 + j, NARROW // 2, stride=9), :] = jnp.where(lane < 64, before, odd[j])
            before = odd[j]
        window[pl.ds(17, NARROW // 2, stride=9), :] = jnp.where(
            lane < 64, before, pltpu.roll(odd[4], 64, 1)
        )

    after_wide = (index >= 5) & (index < 13)

    @pl.when(after_wide)
    def _():
        window[0:9, :] = jnp.concatenate(head[:9], 0)

    @pl.when(jnp.logical_not(after_wide))
    def _():
        odd = [pltpu.roll(row, 64, 1) for row in head[4:8]]
        before, rows = pltpu.roll(head[8], 64, 1), head[:4]
        for j in range(4):
            rows.append(jnp.where(lane < 64, before, odd[j]))
            before = odd[j]
        rows.append(jnp.where(lane < 64, before, head[9]))
        window[0:9, :] = jnp.concatenate(rows, 0)

    lanes = pltpu.roll(window[...], jnp.bitwise_and(128 - left, 127), 1)
    window[...] = lanes
    out[...] = jnp.where(
        lane < 128 - left, window[pl.ds(down, 1736), :], window[pl.ds(down + 1, 1736), :]
    )


def chunk_index(index, core, lay):
    start = index * lay.step
    return jnp.stack([index, core, start // 128, start % 128]).astype(jnp.int32)


def pack_own(params, index, core, lay):
    if lay.count != CANON:
        window = jnp.zeros((lay.gains + lay.chunk,), params.dtype)
        window = lax.dynamic_update_slice(window, params, (index * lay.step,))
        payload = pack_payload(window, index, lay)
        return lax.dynamic_slice_in_dim(payload, core * lay.half, lay.half, 0)
    flat = jnp.pad(params, (0, 1736 * 128 - lay.shard)).reshape(1736, 128)
    vmem = pl.BlockSpec(memory_space=pltpu.VMEM)
    return pl.pallas_call(
        pack_kernel,
        name="pack_own_chunk",
        in_specs=[pl.BlockSpec(memory_space=pltpu.SMEM), vmem],
        out_specs=vmem,
        out_shape=jax.ShapeDtypeStruct((HALF, 128), BF16),
        scratch_shapes=[
            pltpu.VMEM((1760, 128), F32),
            pltpu.VMEM((1752, 128), F32),
            pltpu.VMEM((2 * HALF, 128), F32),
            pltpu.VMEM((NARROW + 8, 128), F32),
        ],
        compiler_params=pltpu.CompilerParams(vmem_limit_bytes=VMEM_LIMIT),
    )(chunk_index(index, core, lay), flat)


def unpack_own(own, twin, index, core, lay):
    if lay.count != CANON:
        rows = jnp.where(core == 0, jnp.stack([own, twin], 0), jnp.stack([twin, own], 0))
        window = unpack_payload(rows.reshape(2 * lay.half, 128), index, lay)
        return lax.dynamic_slice(window, (index * lay.step,), (lay.shard,))
    vmem = pl.BlockSpec(memory_space=pltpu.VMEM)
    rows = pl.pallas_call(
        unpack_kernel,
        name="unpack_own_chunk",
        in_specs=[pl.BlockSpec(memory_space=pltpu.SMEM), vmem, vmem],
        out_specs=vmem,
        out_shape=jax.ShapeDtypeStruct((1736, 128), F32),
        scratch_shapes=[
            pltpu.VMEM((2 * HALF, 128), F32),
            pltpu.VMEM((1752, 128), F32),
            pltpu.VMEM((NARROW + 8, 128), F32),
        ],
        compiler_params=pltpu.CompilerParams(vmem_limit_bytes=VMEM_LIMIT),
    )(chunk_index(index, core, lay), own, twin)
    return rows.reshape(-1)[: lay.shard]


def tables(positions):
    cosine, sine = rope_tables(positions)
    return jnp.concatenate([cosine, cosine], 1), jnp.concatenate([-sine, sine], 1)


def layer_kernels(length, width):
    groups = length // SEQ_LEN * KV_HEADS
    kv_width = KV_HEADS * HEAD
    smem = pl.BlockSpec(memory_space=pltpu.SMEM)
    vmem = pl.BlockSpec(memory_space=pltpu.VMEM)
    hbm = pl.BlockSpec(memory_space=pltpu.HBM)
    anywhere = pl.BlockSpec(memory_space=pl.ANY)
    params = pltpu.CompilerParams(vmem_limit_bytes=VMEM_LIMIT)

    def sds(shape, dtype):
        return jax.ShapeDtypeStruct(shape, dtype)

    def cost(flops):
        return pl.CostEstimate(flops=flops, bytes_accessed=8_000_000, transcendentals=600_000)

    piece, block = sds((4, HALF, 128), BF16), sds((2, HALF, 128), BF16)
    weights = [sds((width, width), BF16), sds((width, kv_width), BF16)]
    weights = weights + [weights[1], weights[0]]
    saved = [
        sds((groups, 3 * SEQ_LEN, SEQ_LEN), F32),
        sds((groups, 3 * SEQ_LEN, HEAD), BF16),
        sds((groups, SEQ_LEN, HEAD), BF16),
        sds((groups, SEQ_LEN, HEAD), BF16),
    ]
    rows = sds((length, width), F32)
    low_rows = sds((length, width), BF16)
    gain = sds((1, width), F32)
    outs = [rows, rows, gain, low_rows] + saved + weights + [gain]
    forward = pl.pallas_call(
        first_kernel,
        name="forward_and_ff_backward",
        in_specs=[smem] + [hbm] * 14 + [hbm, vmem, vmem, hbm],
        out_specs=[hbm] * len(outs) + [anywhere] * 10,
        out_shape=outs + [block] * 8 + [piece] * 2,
        scratch_shapes=[pltpu.VMEM(out.shape, out.dtype) for out in outs]
        + [
            pltpu.VMEM((CANON, 2 * HALF, 128), BF16),
            pltpu.VMEM((12, 2 * HALF, 128), BF16),
            pltpu.VMEM((width, length), BF16),
            pltpu.VMEM((width, length), BF16),
            pltpu.VMEM((length, width), BF16),
            pltpu.VMEM((length, width), F32),
            pltpu.VMEM((length, width), BF16),
            pltpu.VMEM((width, length), BF16),
            pltpu.VMEM((length, width), F32),
            pltpu.VMEM((width + 8, 128), F32),
            pltpu.VMEM((width + 8, 128), F32),
            pltpu.SemaphoreType.DMA((2,)),
            pltpu.SemaphoreType.DMA((4,)),
            pltpu.SemaphoreType.DMA((3,)),
            pltpu.SemaphoreType.DMA((len(outs),)),
        ],
        compiler_params=params,
        cost_estimate=cost(20 * length * width * FF),
    )
    attention_back = pl.pallas_call(
        second_kernel,
        name="attention_backward",
        in_specs=[smem] + [vmem] * 16 + [anywhere] * 2,
        out_specs=[hbm] * 2 + [anywhere] * 6,
        out_shape=[sds((width, length), BF16), sds((width, length), F32)] + [block] * 4 + [piece] * 2,
        scratch_shapes=[
            pltpu.VMEM((4, 2 * HALF, 128), BF16),
            pltpu.VMEM((2, 4, HALF, 128), BF16),
            pltpu.VMEM((width, length), BF16),
            pltpu.VMEM((width, length), F32),
            pltpu.VMEM((length, width), F32),
            pltpu.VMEM((length, kv_width), F32),
            pltpu.VMEM((length, kv_width), F32),
            pltpu.VMEM((width + 8, 128), F32),
            pltpu.VMEM((width + 8, 128), F32),
            pltpu.SemaphoreType.DMA((2,)),
            pltpu.SemaphoreType.DMA((1,)),
            pltpu.SemaphoreType.DMA((3,)),
        ],
        compiler_params=pltpu.CompilerParams(vmem_limit_bytes=60 * 1024 * 1024),
        cost_estimate=cost(10 * length * width * width),
    )
    return forward, attention_back


def flat_of(payloads, lay):
    n = lay.count
    heads = payloads[:, lay.rows : lay.rows + 10]
    flats = [unhead_narrow(heads[0])]
    for i in range(n):
        wide = n // 4 <= i < 3 * n // 4
        body = payloads[i, : lay.rows]
        flat = unpack_wide(body, FF) if wide else unpack_narrow(body)
        if i + 1 < n:
            tail = unhead_wide(heads[i + 1]) if wide else unhead_narrow(heads[i + 1])
            flat = jnp.concatenate([flat[: -lay.gains], flat[-lay.gains :] + tail])
        flats.append(flat)
    return jnp.concatenate(flats)


def payloads_of(flat, lay):
    windows = [
        flat[i * lay.chunk : (i + 1) * lay.chunk + lay.gains] for i in range(lay.count)
    ]
    return jnp.stack([pack_payload(window, i, lay) for i, window in enumerate(windows)], 0)


def canonical(blocks, twins, lay, canon, index, core):
    sides = []
    for side in (blocks, twins):
        side = jnp.stack([jnp.concatenate(value, 0) for value in side], 0)
        sides.append(side.reshape(lay.count, lay.half, 128))
    both = jnp.where(core == 0, jnp.stack(sides, 1), jnp.stack(sides[::-1], 1))
    both = both.reshape(lay.count, 2 * lay.half, 128)
    both = jnp.take(both, jnp.arange(lay.count, dtype=jnp.int32) ^ index, axis=0)
    flat = flat_of(both, lay)
    zeros = jnp.zeros((canon.gains,), flat.dtype)
    rows = []
    for i in range(CANON):
        window = flat[i * canon.chunk : (i + 1) * canon.chunk + canon.gains]
        if i:
            window = jnp.concatenate([zeros, window[canon.gains :]])
        rows.append(pack_payload(window, i, canon))
    rows = jnp.stack(rows, 0).reshape(PLANES, 4, 2, canon.half, 128)
    pieces = []
    for c in range(2):
        side = rows[:, :, c]
        pieces = pieces + [side[0]] + [side[p, :2] for p in range(1, PLANES)]
        pieces = pieces + [side[p, 2:] for p in range(1, PLANES)]
    return pieces


def from_canonical(slots, lay, canon, place, core):
    sides = []
    for which in range(2):
        sides.append(jnp.stack([slot[which] for slot in slots], 0))
    rows = jnp.stack(sides, 2).reshape(CANON, 2 * canon.half, 128)
    flats = [unhead_narrow(rows[0, canon.rows : canon.rows + 10])]
    for i in range(CANON):
        body = rows[i, : canon.rows]
        flats.append(unpack_wide(body, FF) if 4 <= i < 12 else unpack_narrow(body))
    rows = payloads_of(jnp.concatenate(flats), lay)
    rows = rows.reshape(PLANES, lay.in_plane, 2, lay.half, 128)
    rows = jnp.take(rows, jnp.arange(lay.in_plane, dtype=jnp.int32) ^ place, axis=1)
    rows = rows.reshape(PLANES, 1 << lay.y_bits, 1 << lay.x_bits, 2, lay.half, 128)
    sides = [jnp.take(rows, side, axis=3) for side in (core, 1 - core)]
    return [[list(side[p]) for p in range(PLANES)] for side in sides]


def add(left, right):
    return left.astype(F32) + right.astype(F32)


def on_device(lay, canon, tokens_in, positions, params, cotangent):
    index = lax.axis_index("dp")
    core = lax.axis_index("rep")
    n, half, in_plane = lay.count, lay.half, lay.in_plane
    plane, place = index // in_plane, index % in_plane
    same = n == CANON
    firsts, seconds = hops(lay)
    forward, attention_back = layer_kernels(*tokens_in.shape)
    mine = pack_own(params, index, core, lay)
    angles = tables(positions)
    if same:
        idx = jnp.stack([plane, place, core, 1]).astype(jnp.int32)
        pieces, angles = balanced_gather(mine, lay, angles)
    else:
        idx = jnp.zeros((4,), jnp.int32)
        blocks = gather(mine, lay)
        twins = [[swap_rep(block) for block in value] for value in blocks]
        pieces = canonical(blocks, twins, lay, canon, index, core)
    results = forward(idx, *pieces, tokens_in.T, *angles, cotangent.T)
    d_gain = results[2]
    saved, slots, held = results[:13], (results[13:17], results[17:21]), results[21:23]
    if same:
        (first,), (second,) = firsts, seconds
        moved = [hop(add(far, swap_rep(send)).astype(BF16), second, n) for _, far, _, send in slots]
        near = [add(keep, swap_rep(send)) for keep, _, send, _ in slots]
    output, d_input, *results = attention_back(idx, tokens_in.T, *angles, *saved, *held)
    output, d_input = output.T, d_input.T
    keep_near, keep_far, send_near, send_far, keep, send = results
    if same:
        moved, send_far, send_near, send = lax.optimization_barrier((moved, send_far, send_near, send))
        third = hop(add(keep_far, swap_rep(send_far)).astype(BF16), second, n)
        early = [(near[j] + moved[j].astype(F32)).astype(BF16) for j in range(2)]
        early = [add(value[0], hop(value[1], first, n)).astype(BF16) for value in early]
        third = (add(keep_near, swap_rep(send_near)) + third.astype(F32)).astype(BF16)
        third = add(third[0], hop(third[1], first, n)).astype(BF16)
        keep, send = [jnp.where(plane == 0, a, b) for a, b in zip((keep, send), held)]
        mine = add(keep, swap_rep(send)).astype(BF16)

        def pick(values, s):
            table = ((0, 1, 2), (2, 1, 0), (1, 2, 0), (1, 0, 2))
            result = values[table[3][s - 1]]
            for z in range(3):
                result = jnp.where(plane == z, values[table[z][s - 1]], result)
            return result

        mine, third = lax.optimization_barrier((mine, third))
        planes = early + [third]
        parts = [swap(pick(planes, s), s << (lay.bits - 2), n) for s in range(1, PLANES)]
        both = tuple(a ^ b for a, b in zip(first, second))
        inner = [hop(mine[d], masks, n) for d, masks in ((1, first), (2, second), (3, both))]
        parts, inner = lax.optimization_barrier((parts, inner))
        total = (add(mine[0], inner[0]) + add(inner[1], inner[2])) + (
            parts[0].astype(F32) + add(parts[1], parts[2])
        )
    else:
        slots = [(near, far, other, last) for near, far, other, last in slots]
        slots.append((keep_near, keep_far, send_near, send_far))
        planes = [(keep, send)]
        for near, far, other, last in slots:
            planes.append((jnp.concatenate([near, far], 0), jnp.concatenate([other, last], 0)))
        keeps, sends = from_canonical(planes, lay, canon, place, core)
        moved = []
        for keep, send in zip(keeps, sends):
            pair = pair_sum(keep, send)
            moved.append(add_blocks(pair[0], send_blocks(pair, seconds, n)))
        blocks = split_first(moved, lay)
        planes = add_blocks(blocks[0], send_blocks(blocks, firsts, n))
        total = reduce_planes(planes, plane, lay)
    other = swap_rep(total)
    if same:
        at = ROWS + 26 - HALF
        d_gain = jnp.where(core == 1, total[at : at + 5], other[at : at + 5]).reshape(-1)[: lay.width]
    else:
        d_gain = sum_everywhere(d_gain[0], lay)
    return output, d_input, unpack_own(total, other, index, core, lay), d_gain


def solution(mesh):
    def run(tokens_in, positions, params, cotangent):
        total, width = params.shape[0], tokens_in.shape[1]
        lay = Layout(mesh.shape["dp"], total, width)
        canon = Layout(CANON, total, width)
        rows = P(("dp", "rep"), None)
        return jax.shard_map(
            lambda *args: on_device(lay, canon, *args),
            mesh=mesh,
            in_specs=(rows, P(("dp", "rep")), P("dp"), rows),
            out_specs=(rows, rows, P("dp"), P()),
            check_vma=False,
        )(tokens_in, positions, params, cotangent)

    return run
```
